32 devices in a mesh: seq: 8 (over z, y), head: 4 (over x, core).
Axes of the slice: x: 2, y: 2, z: 4, core: 2. Of those that a mesh axis runs over, the one named last changes fastest.
Arguments:
- queries: bfloat16 [1024, 2048], P('seq', 'head'), may hold values from -1.25 to 1.25
- key_vectors: bfloat16 [1024, 2048], P('seq', 'head'), may hold values from -1.25 to 1.25
- value_vectors: bfloat16 [1024, 2048], P('seq', 'head'), may hold values from -4 to 4
- feature_proj: bfloat16 [16, 128, 256], P('head'), may hold values from -2.5 to 2.5
- out_weight: bfloat16 [2048, 2048], P('head'), may hold values from -0.1875 to 0.1875
- grad_output: bfloat16 [1024, 2048], P('seq', 'head'), may hold values from -4 to 4
Outputs:
- layer_out: bfloat16 [1024, 2048], P('seq', 'head')
- grad_queries: bfloat16 [1024, 2048], P('seq', 'head')
- grad_keys: bfloat16 [1024, 2048], P('seq', 'head')
- grad_values: bfloat16 [1024, 2048], P('seq', 'head')
The draws below stay inside these ranges and needn't reach their ends.
All inputs are finite; a program needn't handle non-finite values.
Results may differ from the reference program's by a relative error of at most 0.025.
Values may be sent and summed in bfloat16 or wider, within the bound.
No kernel may reach another device: no remote copies, remote signals or barrier semaphores. Data moves between devices by JAX's collectives and lax.ppermute only.
A program may use at most 128 MiB of HBM per device.

```python
import jax
import jax.numpy as jnp
from jax import lax

HEADS = 16
HEAD_DIM = 128
FEATURES = 256
DW = 2048
BLOCK = 128
HD = 2048
TOKENS = 1024


def raised(drawn, stream_key, source, target, blocks, factor):
    owner, partner = [(jnp.arange(drawn.shape[axis_at]) // (drawn.shape[axis_at] // blocks)).reshape([-1 if axis == axis_at else 1 for axis in range(drawn.ndim)]) for axis_at in (source, target)]
    chosen = jax.random.permutation(stream_key, blocks)[partner]
    strong = (owner == chosen) | (owner == (partner + blocks // 2) % blocks)
    return jnp.where(strong, factor * drawn, drawn)


def steps_of(key, dims, split, smallest, top_value):
    gain = 1.0
    for position, parts in split:
        heights = jax.random.uniform(jax.random.fold_in(jax.random.fold_in(key, 6), position), (parts,), jnp.float32, smallest / len(split), top_value / len(split))
        gain = gain * jnp.repeat(jnp.exp(heights), dims[position] // parts).reshape((-1,) + (1,) * (len(dims) - 1 - position))
    return gain


def gaussian(own_key, shape, deviation, limit, shards=(), kind=jnp.bfloat16):
    drawn = deviation * jax.random.normal(own_key, shape, jnp.float32)
    if shards:
        drawn = drawn * steps_of(own_key, shape, shards, -0.22, 0.18)
    return jnp.clip(drawn, -limit, limit).astype(kind)


def bell_draw_with(own_key, shape, spread, limit, pieces, heavy, held_as=jnp.bfloat16):
    array = spread * jax.random.normal(own_key, shape, jnp.float32)
    if pieces:
        array = array * steps_of(own_key, shape, pieces, -0.22, 0.18)
    return jnp.clip(raised(array, jax.random.fold_in(own_key, 3), *heavy), -limit, limit).astype(held_as)


def setup_inputs(seed: int = 0) -> dict:
    streams_of = jax.random.split(jax.random.key(seed), 7)
    queries = gaussian(streams_of[0], (TOKENS, HD), 0.5, 1.25, ((0, 8), (1, 4)))
    key_vectors = gaussian(streams_of[1], (TOKENS, HD), 0.5, 1.25, ((0, 8), (1, 4)))
    value_vectors = gaussian(streams_of[2], (TOKENS, HD), 1.0, 4.0, ((0, 8), (1, 4)))
    feature_proj = gaussian(streams_of[3], (HEADS, HEAD_DIM, FEATURES), 1.0, 2.5, ((0, 4),))
    out_weight = bell_draw_with(streams_of[4], (HD, DW), HD ** -0.5, 0.1875, ((0, 4),), (0, 1, 4, 2.0))
    grad_output = gaussian(streams_of[5], (TOKENS, DW), 1.0, 4.0, ((0, 8), (1, 4)))
    return dict(queries=queries, key_vectors=key_vectors, value_vectors=value_vectors, feature_proj=feature_proj, out_weight=out_weight, grad_output=grad_output)


epsilon = 1e-05

def lower_mask(width):
    row_ids = lax.broadcasted_iota(jnp.int32, (width, width), 0)
    col_ids = lax.broadcasted_iota(jnp.int32, (width, width), 1)
    return col_ids <= row_ids

def rounded(values):
    return lax.optimization_barrier(values.astype(jnp.bfloat16)).astype(jnp.float32)

def reference(queries, key_vectors, value_vectors, feature_proj, out_weight, grad_output):
    feat_scale = HEAD_DIM ** (-0.25)
    n_blocks = TOKENS // BLOCK
    causal = lower_mask(BLOCK)

    def one_head(packed):
        q_head, k_head, v_head, omega, w_rows = packed
        q_feat32 = jnp.exp(jnp.dot(q_head, omega, preferred_element_type=jnp.float32) * feat_scale)
        k_wide = k_head.astype(jnp.float32)
        half_sq = lax.optimization_barrier(jnp.sum(k_wide * k_wide, axis=1, keepdims=True)) * (feat_scale * feat_scale * 0.5)
        k_feat32 = jnp.exp(jnp.dot(k_head, omega, preferred_element_type=jnp.float32) * feat_scale - half_sq)
        q_blocks = rounded(q_feat32).reshape(n_blocks, BLOCK, FEATURES)
        k_blocks = rounded(k_feat32).reshape(n_blocks, BLOCK, FEATURES)
        v_blocks = v_head.astype(jnp.float32).reshape(n_blocks, BLOCK, HEAD_DIM)
        states = jnp.einsum('ncm,ncd->nmd', k_blocks, v_blocks)
        running = jnp.cumsum(states, axis=0)
        zero_state = jnp.zeros((1, FEATURES, HEAD_DIM), jnp.float32)
        carried = jnp.concatenate([zero_state, running[:-1]], axis=0)
        carried_b = rounded(carried)
        scores = jnp.where(causal, jnp.einsum('nim,njm->nij', q_blocks, k_blocks), 0.0)
        scores_b = rounded(scores)
        numerator = jnp.einsum('nij,njd->nid', scores_b, v_blocks) + jnp.einsum('nim,nmd->nid', q_blocks, carried_b)
        row_root = jnp.sqrt(lax.optimization_barrier(jnp.mean(numerator * numerator, axis=2, keepdims=True)) + epsilon)
        normed = numerator / row_root
        mixed_head = normed.astype(jnp.bfloat16).reshape(TOKENS, HEAD_DIM)
        grad_mixed = lax.dot_general(grad_output, w_rows, (((1,), (1,)), ((), ())), preferred_element_type=jnp.float32)
        grad_mixed = grad_mixed.reshape(n_blocks, BLOCK, HEAD_DIM)
        grad_numer = (grad_mixed - normed * lax.optimization_barrier(jnp.mean(grad_mixed * normed, axis=2, keepdims=True))) / row_root
        grad_numer_b = rounded(grad_numer)
        later_terms = jnp.einsum('nim,nid->nmd', q_blocks, grad_numer_b)
        backward_sum = jnp.cumsum(later_terms[::-1], axis=0)[::-1]
        after_sum = jnp.concatenate([backward_sum[1:], zero_state], axis=0)
        after_b = rounded(after_sum)
        grad_scores = rounded(jnp.where(causal, jnp.einsum('nid,njd->nij', grad_numer_b, v_blocks), 0.0))
        grad_v = jnp.einsum('nij,nid->njd', scores_b, grad_numer_b) + jnp.einsum('njm,nmd->njd', k_blocks, after_b)
        grad_qf = jnp.einsum('nij,njm->nim', grad_scores, k_blocks) + jnp.einsum('nid,nmd->nim', grad_numer_b, carried_b)
        grad_kf = jnp.einsum('nij,nim->njm', grad_scores, q_blocks) + jnp.einsum('njd,nmd->njm', v_blocks, after_b)
        query_terms = (grad_qf.reshape(TOKENS, FEATURES) * q_feat32).astype(jnp.bfloat16)
        key_terms = (grad_kf.reshape(TOKENS, FEATURES) * k_feat32).astype(jnp.bfloat16)
        grad_q = lax.dot_general(query_terms, omega, (((1,), (1,)), ((), ())), preferred_element_type=jnp.float32) * feat_scale
        key_total = lax.optimization_barrier(jnp.sum(key_terms.astype(jnp.float32), axis=1, keepdims=True))
        grad_k = lax.dot_general(key_terms, omega, (((1,), (1,)), ((), ())), preferred_element_type=jnp.float32) * feat_scale
        grad_k = grad_k - key_total * k_wide * (feat_scale * feat_scale)
        return (mixed_head, grad_q.astype(jnp.bfloat16), grad_k.astype(jnp.bfloat16), grad_v.reshape(TOKENS, HEAD_DIM).astype(jnp.bfloat16))

    def by_head(matrix):
        return jnp.transpose(matrix.reshape(TOKENS, HEADS, HEAD_DIM), (1, 0, 2))

    def from_heads(stacked):
        return jnp.transpose(stacked, (1, 0, 2)).reshape(TOKENS, HEADS * HEAD_DIM)
    weight_rows = out_weight.reshape(HEADS, HEAD_DIM, DW)
    mixed_all, grad_q_all, grad_k_all, grad_v_all = lax.map(one_head, (by_head(queries), by_head(key_vectors), by_head(value_vectors), feature_proj, weight_rows))
    mixed_flat = from_heads(mixed_all)
    layer_out = jnp.dot(mixed_flat, out_weight, preferred_element_type=jnp.float32).astype(jnp.bfloat16)
    return (layer_out, from_heads(grad_q_all), from_heads(grad_k_all), from_heads(grad_v_all))
```

```python
import functools

import jax
import jax.numpy as jnp
from jax import lax
from jax.experimental import pallas as pl
from jax.experimental.pallas import tpu as pltpu
from jax.sharding import PartitionSpec as P

EPSILON = 1e-05
VMEM = pl.BlockSpec(memory_space=pltpu.VMEM)
SMEM = pl.BlockSpec(memory_space=pltpu.SMEM)
NN = (((1,), (0,)), ((), ()))
NT = (((1,), (1,)), ((), ()))
TN = (((0,), (0,)), ((), ()))


def mm(a, b, dims=NN):
    return lax.dot_general(a, b, dims, preferred_element_type=jnp.float32)


def bf(x):
    return x.astype(jnp.bfloat16)


def call(body, outs, *args, flops=0, specs=None):
    size = sum(a.size * a.dtype.itemsize for a in args)
    size += sum(o.size * o.dtype.itemsize for o in outs)
    return pl.pallas_call(
        body,
        out_shape=outs,
        in_specs=specs or [VMEM] * len(args),
        out_specs=[VMEM] * len(outs),
        cost_estimate=pl.CostEstimate(flops=flops, bytes_accessed=size, transcendentals=0),
        compiler_params=pltpu.CompilerParams(vmem_limit_bytes=32 * 1024 * 1024),
    )(*args)


def struct(shape, dtype=jnp.bfloat16):
    return jax.ShapeDtypeStruct(shape, dtype)


def causal_mask(rows):
    row = lax.broadcasted_iota(jnp.int32, (rows, rows), 0)
    col = lax.broadcasted_iota(jnp.int32, (rows, rows), 1)
    return col <= row


def key_kernel(heads, k_ref, v_ref, om_ref, kf_ref, state_ref):
    dim, feats = om_ref.shape[1:]
    scale = dim ** (-0.25)
    for h in range(heads):
        cols, fcols = pl.ds(h * dim, dim), pl.ds(h * feats, feats)
        k = k_ref[:, cols]
        wide = k.astype(jnp.float32)
        half_sq = jnp.sum(wide * wide, axis=1, keepdims=True) * (scale * scale * 0.5)
        kf = bf(jnp.exp(mm(k, om_ref[h]) * scale - half_sq))
        kf_ref[:, fcols] = kf
        state_ref[cols, :] = bf(mm(v_ref[:, cols], kf, TN))


def local_kernel(heads, offsets, me_ref, q_ref, v_ref, om_ref, kf_ref, go_ref, w_ref,
                 qf_ref, scores_ref, num_ref, gm_ref):
    rows = q_ref.shape[0]
    dim, feats = om_ref.shape[1:]
    width = go_ref.shape[2]
    scale = dim ** (-0.25)
    causal = causal_mask(rows)
    for h in range(heads):
        cols, fcols = pl.ds(h * dim, dim), pl.ds(h * feats, feats)
        qf = bf(jnp.exp(mm(q_ref[:, cols], om_ref[h]) * scale))
        qf_ref[:, fcols] = qf
        scores = bf(jnp.where(causal, mm(qf, kf_ref[:, fcols], NT), 0.0))
        scores_ref[h] = scores
        num_ref[:, cols] = mm(scores, v_ref[:, cols])
    total = None
    for at, offset in enumerate(offsets):
        block = me_ref[0] ^ offset
        part = mm(go_ref[at], w_ref[:, pl.ds(pl.multiple_of(block * width, 128), width)], NT)
        total = part if total is None else total + part
    gm_ref[...] = total


def middle_kernel(heads, qf_ref, num_ref, gm_ref, carried_ref, mixed_ref, gn_ref, later_ref):
    dim = carried_ref.shape[0] // heads
    feats = carried_ref.shape[1]
    for h in range(heads):
        cols, fcols = pl.ds(h * dim, dim), pl.ds(h * feats, feats)
        qf = qf_ref[:, fcols]
        num = num_ref[:, cols] + mm(qf, carried_ref[cols, :], NT)
        inv = lax.rsqrt(jnp.mean(num * num, axis=1, keepdims=True) + EPSILON)
        normed = num * inv
        mixed_ref[:, cols] = bf(normed)
        gm = gm_ref[:, cols]
        gn = bf((gm - normed * jnp.mean(gm * normed, axis=1, keepdims=True)) * inv)
        gn_ref[:, cols] = gn
        later_ref[cols, :] = bf(mm(gn, qf, TN))


def project_kernel(offsets, me_ref, mixed_ref, w_ref, own_ref, sent_ref):
    width = own_ref.shape[2]
    half = len(offsets) // 2
    mixed = mixed_ref[...]
    for at, offset in enumerate(offsets):
        block = me_ref[0] ^ offset
        part = bf(mm(mixed, w_ref[:, pl.ds(pl.multiple_of(block * width, 128), width)]))
        if at < half:
            own_ref[at] = part
        else:
            sent_ref[at - half] = part


def query_kernel(heads, qf_ref, kf_ref, v_ref, om_ref, scores_ref, gn_ref, carried_ref,
                 gq_ref, gv_ref, gkf_ref):
    rows = qf_ref.shape[0]
    dim, feats = om_ref.shape[1:]
    scale = dim ** (-0.25)
    causal = causal_mask(rows)
    for h in range(heads):
        cols, fcols = pl.ds(h * dim, dim), pl.ds(h * feats, feats)
        qf, kf, gn = qf_ref[:, fcols], kf_ref[:, fcols], gn_ref[:, cols]
        gs = bf(jnp.where(causal, mm(gn, v_ref[:, cols], NT), 0.0))
        gqf = mm(gs, kf) + mm(gn, carried_ref[cols, :])
        terms = bf(gqf * qf.astype(jnp.float32))
        gq_ref[:, cols] = bf(mm(terms, om_ref[h], NT) * scale)
        gv_ref[:, cols] = mm(scores_ref[h], gn, TN)
        gkf_ref[:, fcols] = mm(gs, qf, TN)


def last_kernel(heads, k_ref, v_ref, om_ref, kf_ref, gv_in_ref, gkf_ref, after_ref,
                gk_ref, gv_ref):
    dim, feats = om_ref.shape[1:]
    scale = dim ** (-0.25)
    for h in range(heads):
        cols, fcols = pl.ds(h * dim, dim), pl.ds(h * feats, feats)
        kf, after = kf_ref[:, fcols], after_ref[cols, :]
        gv_ref[:, cols] = bf(gv_in_ref[:, cols] + mm(kf, after, NT))
        gkf = gkf_ref[:, fcols] + mm(v_ref[:, cols], after)
        terms = bf(gkf * kf.astype(jnp.float32))
        total = jnp.sum(terms.astype(jnp.float32), axis=1, keepdims=True)
        wide = k_ref[:, cols].astype(jnp.float32)
        gk_ref[:, cols] = bf(
            mm(terms, om_ref[h], NT) * scale - total * wide * (scale * scale)
        )


def prefix_kernel(in_ref, out_ref):
    total = jnp.zeros(in_ref.shape[1:], jnp.float32)
    for at in range(in_ref.shape[0]):
        out_ref[at] = bf(total)
        total = total + in_ref[at].astype(jnp.float32)


def swap(array, axis, bit):
    size = lax.axis_size(axis)
    return lax.ppermute(array, axis, [(i, i ^ bit) for i in range(size)])


def bits_of(size):
    return [1 << b for b in range(size.bit_length() - 1)]


def before(state, axis):
    size = lax.axis_size(axis)
    parts = state.reshape((size, state.shape[0] // size) + state.shape[1:])
    mine = lax.all_to_all(parts, axis, 0, 0)
    (sums,) = call(prefix_kernel, [struct(mine.shape)], mine)
    return lax.all_to_all(sums, axis, 0, 0).reshape(state.shape)


def after(state, axis):
    size = lax.axis_size(axis)
    step, inclusive, exclusive = 1, state.astype(jnp.float32), None
    while step < size:
        got = lax.ppermute(
            bf(inclusive), axis, [(i, i - step) for i in range(step, size)]
        ).astype(jnp.float32)
        exclusive = got if exclusive is None else exclusive + got
        inclusive = inclusive + got
        step *= 2
    return bf(exclusive)


def local(queries, key_vectors, value_vectors, feature_proj, out_weight, grad_output):
    heads, dim, feats = feature_proj.shape
    rows, width = grad_output.shape
    split = lax.axis_size("head")
    bits = bits_of(split)
    me = lax.axis_index("head").astype(jnp.int32).reshape(1)
    macs = rows * dim * feats * heads * 2

    kf, state = call(
        functools.partial(key_kernel, heads),
        [struct((rows, heads * feats)), struct((heads * dim, feats))],
        key_vectors, value_vectors, feature_proj, flops=2 * macs,
    )
    carried = before(state, "seq")

    offsets, gathered = [0], grad_output[None]
    for bit in reversed(bits):
        gathered = jnp.concatenate([gathered, swap(gathered, "head", bit)], axis=0)
        offsets = offsets + [o ^ bit for o in offsets]
    qf, scores, num, gm = call(
        functools.partial(local_kernel, heads, offsets),
        [
            struct((rows, heads * feats)),
            struct((heads, rows, rows)),
            struct((rows, heads * dim), jnp.float32),
            struct((rows, heads * dim), jnp.float32),
        ],
        me, queries, value_vectors, feature_proj, kf, gathered, out_weight,
        flops=3 * macs + 2 * rows * out_weight.size, specs=[SMEM] + [VMEM] * 6,
    )
    mixed, gn, later = call(
        functools.partial(middle_kernel, heads),
        [
            struct((rows, heads * dim)),
            struct((rows, heads * dim)),
            struct((heads * dim, feats)),
        ],
        qf, num, gm, carried, flops=2 * macs,
    )
    after_b = after(later, "seq")

    order = [o for o in range(split) if not o & 1] + [o for o in range(split) if o & 1]
    own, sent = call(
        functools.partial(project_kernel, order),
        [struct((split // 2, rows, width))] * 2,
        me, mixed, out_weight, flops=2 * rows * out_weight.size, specs=[SMEM, VMEM, VMEM],
    )
    total = own.astype(jnp.float32) + swap(sent, "head", 1).astype(jnp.float32)
    for bit in bits[1:]:
        pairs = total.reshape((total.shape[0] // 2, 2) + total.shape[1:])
        total = pairs[:, 0] + swap(bf(pairs[:, 1]), "head", bit).astype(jnp.float32)
    layer_out = bf(total[0])

    gq, gv_part, gkf_part = call(
        functools.partial(query_kernel, heads),
        [
            struct((rows, heads * dim)),
            struct((rows, heads * dim), jnp.float32),
            struct((rows, heads * feats), jnp.float32),
        ],
        qf, kf, value_vectors, feature_proj, scores, gn, carried, flops=5 * macs,
    )
    gk, gv = call(
        functools.partial(last_kernel, heads),
        [struct((rows, heads * dim))] * 2,
        key_vectors, value_vectors, feature_proj, kf, gv_part, gkf_part, after_b,
        flops=3 * macs,
    )
    return layer_out, gq, gk, gv


def solution(mesh):
    placed = (
        P("seq", "head"),
        P("seq", "head"),
        P("seq", "head"),
        P("head", None, None),
        P("head", None),
        P("seq", "head"),
    )
    return jax.shard_map(
        local,
        mesh=mesh,
        in_specs=placed,
        out_specs=(P("seq", "head"),) * 4,
        check_vma=False,
    )
```

```python
import functools

import jax
import jax.numpy as jnp
from jax import lax
from jax.experimental import pallas as pl
from jax.experimental.pallas import tpu as pltpu
from jax.sharding import PartitionSpec as P

EPSILON = 1e-05
VMEM = pl.BlockSpec(memory_space=pltpu.VMEM)
SMEM = pl.BlockSpec(memory_space=pltpu.SMEM)
HBM = pl.BlockSpec(memory_space=pltpu.HBM)
NN = (((1,), (0,)), ((), ()))
NT = (((1,), (1,)), ((), ()))
TN = (((0,), (0,)), ((), ()))


def mm(a, b, dims=NN):
    return lax.dot_general(a, b, dims, preferred_element_type=jnp.float32)


def bf(x):
    return x.astype(jnp.bfloat16)


def call(body, outs, *args, flops=0, specs=None, scratch=()):
    size = sum(a.size * a.dtype.itemsize for a in args)
    size += sum(o.size * o.dtype.itemsize for o in outs)
    return pl.pallas_call(
        body,
        out_shape=outs,
        in_specs=specs or [VMEM] * len(args),
        out_specs=[VMEM] * len(outs),
        scratch_shapes=list(scratch),
        cost_estimate=pl.CostEstimate(flops=flops, bytes_accessed=size, transcendentals=0),
        compiler_params=pltpu.CompilerParams(vmem_limit_bytes=32 * 1024 * 1024),
    )(*args)


def struct(shape, dtype=jnp.bfloat16):
    return jax.ShapeDtypeStruct(shape, dtype)


def causal_mask(rows):
    row = lax.broadcasted_iota(jnp.int32, (rows, rows), 0)
    col = lax.broadcasted_iota(jnp.int32, (rows, rows), 1)
    return col <= row


def key_kernel(heads, k_ref, v_ref, om_ref, kf_ref, state_ref):
    dim, feats = om_ref.shape[1:]
    scale = dim ** (-0.25)
    for h in range(heads):
        cols, fcols = pl.ds(h * dim, dim), pl.ds(h * feats, feats)
        k = k_ref[:, cols]
        wide = k.astype(jnp.float32)
        half_sq = jnp.sum(wide * wide, axis=1, keepdims=True) * (scale * scale * 0.5)
        kf = bf(jnp.exp(mm(k, om_ref[h]) * scale - half_sq))
        kf_ref[:, fcols] = kf
        state_ref[cols, :] = bf(mm(v_ref[:, cols], kf, TN))


def local_kernel(heads, offsets, me_ref, q_ref, v_ref, om_ref, kf_ref, go_ref, w_ref,
                 qf_ref, scores_ref, num_ref, gm_ref):
    rows = q_ref.shape[0]
    dim, feats = om_ref.shape[1:]
    width = go_ref.shape[2]
    scale = dim ** (-0.25)
    causal = causal_mask(rows)
    for h in range(heads):
        cols, fcols = pl.ds(h * dim, dim), pl.ds(h * feats, feats)
        qf = bf(jnp.exp(mm(q_ref[:, cols], om_ref[h]) * scale))
        qf_ref[:, fcols] = qf
        scores = bf(jnp.where(causal, mm(qf, kf_ref[:, fcols], NT), 0.0))
        scores_ref[h] = scores
        num_ref[:, cols] = mm(scores, v_ref[:, cols])
    total = None
    for at, offset in enumerate(offsets):
        block = me_ref[0] ^ offset
        part = mm(go_ref[at], w_ref[:, pl.ds(pl.multiple_of(block * width, 128), width)], NT)
        total = part if total is None else total + part
    gm_ref[...] = total


def middle_kernel(heads, qf_ref, num_ref, gm_ref, carried_ref, mixed_ref, gn_ref, later_ref):
    dim = carried_ref.shape[0] // heads
    feats = carried_ref.shape[1]
    for h in range(heads):
        cols, fcols = pl.ds(h * dim, dim), pl.ds(h * feats, feats)
        qf = qf_ref[:, fcols]
        num = num_ref[:, cols] + mm(qf, carried_ref[cols, :], NT)
        inv = lax.rsqrt(jnp.mean(num * num, axis=1, keepdims=True) + EPSILON)
        normed = num * inv
        mixed_ref[:, cols] = bf(normed)
        gm = gm_ref[:, cols]
        gn = bf((gm - normed * jnp.mean(gm * normed, axis=1, keepdims=True)) * inv)
        gn_ref[:, cols] = gn
        later_ref[cols, :] = bf(mm(gn, qf, TN))


def project_kernel(offsets, me_ref, mixed_ref, w_ref, own_ref, sent_ref):
    width = own_ref.shape[2]
    half = len(offsets) // 2
    mixed = mixed_ref[...]
    for at, offset in enumerate(offsets):
        block = me_ref[0] ^ offset
        part = bf(mm(mixed, w_ref[:, pl.ds(pl.multiple_of(block * width, 128), width)]))
        if at < half:
            own_ref[at] = part
        else:
            sent_ref[at - half] = part


def query_kernel(heads, qf_ref, kf_ref, v_ref, om_ref, scores_ref, gn_ref, carried_ref,
                 gq_ref, gv_ref, gkf_ref):
    rows = qf_ref.shape[0]
    dim, feats = om_ref.shape[1:]
    scale = dim ** (-0.25)
    causal = causal_mask(rows)
    for h in range(heads):
        cols, fcols = pl.ds(h * dim, dim), pl.ds(h * feats, feats)
        qf, kf, gn = qf_ref[:, fcols], kf_ref[:, fcols], gn_ref[:, cols]
        gs = bf(jnp.where(causal, mm(gn, v_ref[:, cols], NT), 0.0))
        gqf = mm(gs, kf) + mm(gn, carried_ref[cols, :])
        terms = bf(gqf * qf.astype(jnp.float32))
        gq_ref[:, cols] = bf(mm(terms, om_ref[h], NT) * scale)
        gv_ref[:, cols] = mm(scores_ref[h], gn, TN)
        gkf_ref[:, fcols] = mm(gs, qf, TN)


def last_kernel(heads, k_ref, v_ref, om_ref, kf_ref, gv_in_ref, gkf_ref, after_ref,
                gk_ref, gv_ref):
    dim, feats = om_ref.shape[1:]
    scale = dim ** (-0.25)
    for h in range(heads):
        cols, fcols = pl.ds(h * dim, dim), pl.ds(h * feats, feats)
        kf, after = kf_ref[:, fcols], after_ref[cols, :]
        gv_ref[:, cols] = bf(gv_in_ref[:, cols] + mm(kf, after, NT))
        gkf = gkf_ref[:, fcols] + mm(v_ref[:, cols], after)
        terms = bf(gkf * kf.astype(jnp.float32))
        total = jnp.sum(terms.astype(jnp.float32), axis=1, keepdims=True)
        wide = k_ref[:, cols].astype(jnp.float32)
        gk_ref[:, cols] = bf(
            mm(terms, om_ref[h], NT) * scale - total * wide * (scale * scale)
        )


def prefix_kernel(in_ref, out_ref):
    total = jnp.zeros(in_ref.shape[1:], jnp.float32)
    for at in range(in_ref.shape[0]):
        out_ref[at] = bf(total)
        total = total + in_ref[at].astype(jnp.float32)


def swap(array, axis, bit):
    size = lax.axis_size(axis)
    return lax.ppermute(array, axis, [(i, i ^ bit) for i in range(size)])


def bits_of(size):
    return [1 << b for b in range(size.bit_length() - 1)]


def before(state, axis):
    size = lax.axis_size(axis)
    parts = state.reshape((size, state.shape[0] // size) + state.shape[1:])
    mine = lax.all_to_all(parts, axis, 0, 0)
    (sums,) = call(prefix_kernel, [struct(mine.shape)], mine)
    return lax.all_to_all(sums, axis, 0, 0).reshape(state.shape)


def after(state, axis):
    size = lax.axis_size(axis)
    step, inclusive, exclusive = 1, state.astype(jnp.float32), None
    while step < size:
        got = lax.ppermute(
            bf(inclusive), axis, [(i, i - step) for i in range(step, size)]
        ).astype(jnp.float32)
        exclusive = got if exclusive is None else exclusive + got
        inclusive = inclusive + got
        step *= 2
    return bf(exclusive)


def reduce_blocks(own, sent, bits):
    total = own.astype(jnp.float32) + swap(sent, "head", 1).astype(jnp.float32)
    for bit in bits[1:]:
        pairs = total.reshape((total.shape[0] // 2, 2) + total.shape[1:])
        total = pairs[:, 0] + swap(bf(pairs[:, 1]), "head", bit).astype(jnp.float32)
    return bf(total[0])


def scanned(queries, key_vectors, value_vectors, feature_proj, out_weight, grad_output):
    heads, dim, feats = feature_proj.shape
    rows, width = grad_output.shape
    split = lax.axis_size("head")
    bits = bits_of(split)
    me = lax.axis_index("head").astype(jnp.int32).reshape(1)
    macs = rows * dim * feats * heads * 2

    kf, state = call(
        functools.partial(key_kernel, heads),
        [struct((rows, heads * feats)), struct((heads * dim, feats))],
        key_vectors, value_vectors, feature_proj, flops=2 * macs,
    )
    carried = before(state, "seq")

    offsets, gathered = [0], grad_output[None]
    for bit in reversed(bits):
        gathered = jnp.concatenate([gathered, swap(gathered, "head", bit)], axis=0)
        offsets = offsets + [o ^ bit for o in offsets]
    qf, scores, num, gm = call(
        functools.partial(local_kernel, heads, offsets),
        [
            struct((rows, heads * feats)),
            struct((heads, rows, rows)),
            struct((rows, heads * dim), jnp.float32),
            struct((rows, heads * dim), jnp.float32),
        ],
        me, queries, value_vectors, feature_proj, kf, gathered, out_weight,
        flops=3 * macs + 2 * rows * out_weight.size, specs=[SMEM] + [VMEM] * 6,
    )
    mixed, gn, later = call(
        functools.partial(middle_kernel, heads),
        [
            struct((rows, heads * dim)),
            struct((rows, heads * dim)),
            struct((heads * dim, feats)),
        ],
        qf, num, gm, carried, flops=2 * macs,
    )
    after_b = after(later, "seq")

    order = [o for o in range(split) if not o & 1] + [o for o in range(split) if o & 1]
    own, sent = call(
        functools.partial(project_kernel, order),
        [struct((split // 2, rows, width))] * 2,
        me, mixed, out_weight, flops=2 * rows * out_weight.size, specs=[SMEM, VMEM, VMEM],
    )
    layer_out = reduce_blocks(own, sent, bits)

    gq, gv_part, gkf_part = call(
        functools.partial(query_kernel, heads),
        [
            struct((rows, heads * dim)),
            struct((rows, heads * dim), jnp.float32),
            struct((rows, heads * feats), jnp.float32),
        ],
        qf, kf, value_vectors, feature_proj, scores, gn, carried, flops=5 * macs,
    )
    gk, gv = call(
        functools.partial(last_kernel, heads),
        [struct((rows, heads * dim))] * 2,
        key_vectors, value_vectors, feature_proj, kf, gv_part, gkf_part, after_b,
        flops=3 * macs,
    )
    return layer_out, gq, gk, gv


def spot():
    s, h = lax.axis_index("seq"), lax.axis_index("head")
    return s, h


def routes(k, n, seq, head):
    out = []
    for s in range(seq):
        for h in range(head):
            to = (n * (h % 2) + (s + k) % n) * head + 2 * (h // 2) + s // n
            out.append((s * head + h, to))
    return out


def scatter(parts):
    n, seq, head = len(parts), lax.axis_size("seq"), lax.axis_size("head")
    return [lax.ppermute(p, ("seq", "head"), routes(k, n, seq, head)) for k, p in enumerate(parts)]


def gather(parts):
    n, seq, head = len(parts), lax.axis_size("seq"), lax.axis_size("head")
    return [
        lax.ppermute(p, ("seq", "head"), [(b, a) for a, b in routes(k, n, seq, head)])
        for k, p in enumerate(parts)
    ]


def pass_on(array, forward):
    pairs = [(h, h + 1) if forward else (h + 1, h) for h in range(0, lax.axis_size("head"), 2)]
    return lax.ppermute(array, "head", pairs)


def lane(index, width):
    return pl.ds(pl.multiple_of(index * width, 128), width)


def pack_kernel(n, q_ref, k_ref, v_ref, om_ref, *rest):
    outs, om_out, sems = rest[:n], rest[n], rest[n + 1]
    s, _ = spot()
    dim = om_ref.shape[1]
    copies = []
    for k in range(n):
        cols = lane(lax.rem(s + k, n), dim)
        for at, ref in enumerate((q_ref, k_ref, v_ref)):
            copies.append((ref.at[:, cols], outs[k].at[at]))
    copies.append((om_ref.at[lax.rem(s, n)], om_out))
    started = [pltpu.make_async_copy(a, b, sems.at[i]) for i, (a, b) in enumerate(copies)]
    for copy in started:
        copy.start()
    for copy in started:
        copy.wait()


def grad_mixed_kernel(n, offsets, *refs):
    blocks, w_ref = refs[: len(offsets)], refs[len(offsets)]
    outs, scr = refs[len(offsets) + 1 : -1], refs[-1]
    s, h = spot()
    width = blocks[0].shape[1]
    dim = outs[0].shape[1]
    total = None
    for offset, ref in zip(offsets, blocks):
        part = mm(ref[...], w_ref[:, lane(h ^ offset, width)], NT)
        total = part if total is None else total + part
    scr[...] = bf(total)
    for k in range(n):
        outs[k][...] = scr[:, lane(lax.rem(s + k, n), dim)]


def first_kernel(n, *refs):
    got, own_om_ref, om_in_ref = refs[:n], refs[n], refs[n + 1]
    qkv_ref, om_ref, kf_ref, state_ref, total_ref = refs[n + 2 :]
    s, h = spot()
    rows, dim = got[0].shape[1:]
    scale = dim ** (-0.25)
    for k in range(n):
        at = pl.ds(pl.multiple_of(lax.rem(s + n - k, n) * rows, 128), rows)
        qkv_ref[:, at, :] = got[k][...]
    mine = lax.div(s, n) == lax.rem(h, 2)
    om = jnp.where(mine, own_om_ref[lax.rem(s, n)], om_in_ref[...])
    om_ref[...] = om
    k_all = qkv_ref[1]
    wide = k_all.astype(jnp.float32)
    half_sq = jnp.sum(wide * wide, axis=1, keepdims=True) * (scale * scale * 0.5)
    kf = bf(jnp.exp(mm(k_all, om) * scale - half_sq))
    kf_ref[...] = kf
    total = jnp.zeros(total_ref.shape, jnp.float32)
    for t in range(n):
        at = pl.ds(t * rows, rows)
        state_ref[t] = bf(total)
        total = total + mm(qkv_ref[2, at, :], kf[t * rows : (t + 1) * rows], TN)
    total_ref[...] = bf(total)


def inner_kernel(n, qkv_ref, om_ref, kf_ref, state_ref, qf_ref, scores_ref, num_ref):
    dim = om_ref.shape[0]
    rows = scores_ref.shape[1]
    scale = dim ** (-0.25)
    causal = causal_mask(rows)
    qf_ref[...] = bf(jnp.exp(mm(qkv_ref[0], om_ref[...]) * scale))
    for t in range(n):
        at = pl.ds(t * rows, rows)
        qf = qf_ref[at, :]
        scores = bf(jnp.where(causal, mm(qf, kf_ref[at, :], NT), 0.0))
        scores_ref[t] = scores
        num_ref[at, :] = mm(scores, qkv_ref[2, at, :]) + mm(qf, state_ref[t], NT)


def turn_kernel(n, *refs):
    gm_in, (qf_ref, num_ref, carried_ref) = refs[:n], refs[n : n + 3]
    gn_ref, state_ref, total_ref = refs[n + 3 : n + 6]
    outs, scr = refs[n + 6 : -1], refs[-1]
    s, _ = spot()
    rows = gm_in[0].shape[0]
    places = [
        pl.ds(pl.multiple_of(lax.rem(s + n - k, n) * rows, 128), rows) for k in range(n)
    ]
    for k in range(n):
        scr[places[k], :] = gm_in[k][...]
    num = num_ref[...] + mm(qf_ref[...], carried_ref[...], NT)
    inv = lax.rsqrt(jnp.mean(num * num, axis=1, keepdims=True) + EPSILON)
    normed = num * inv
    gm = scr[...].astype(jnp.float32)
    gn = bf((gm - normed * jnp.mean(gm * normed, axis=1, keepdims=True)) * inv)
    gn_ref[...] = gn
    scr[...] = bf(normed)
    for k in range(n):
        outs[k][...] = scr[places[k], :]
    total = jnp.zeros(total_ref.shape, jnp.float32)
    for t in reversed(range(n)):
        state_ref[t] = bf(total)
        at = pl.ds(t * rows, rows)
        total = total + mm(gn[t * rows : (t + 1) * rows], qf_ref[at, :], TN)
    total_ref[...] = bf(total)


def back_kernel(n, qkv_ref, om_ref, kf_ref, qf_ref, scores_ref, gn_ref, state_ref, carried_ref,
                later_ref, gq_ref, gv_ref, gkf_ref, gqf_scr):
    dim = om_ref.shape[0]
    rows = scores_ref.shape[1]
    scale = dim ** (-0.25)
    causal = causal_mask(rows)
    gqf_scr[...] = mm(gn_ref[...], carried_ref[...])
    for t in range(n):
        at = pl.ds(t * rows, rows)
        qf, kf, gn, v = qf_ref[at, :], kf_ref[at, :], gn_ref[at, :], qkv_ref[2, at, :]
        gs = bf(jnp.where(causal, mm(gn, v, NT), 0.0))
        gqf = gqf_scr[at, :] + mm(gs, kf) + mm(gn, state_ref[t])
        terms = bf(gqf * qf.astype(jnp.float32))
        gq_ref[at, :] = bf(mm(terms, om_ref[...], NT) * scale)
        later = later_ref[t]
        gv_ref[at, :] = mm(scores_ref[t], gn, TN) + mm(kf, later, NT)
        gkf_ref[at, :] = mm(gs, qf, TN) + mm(v, later)


def end_kernel(n, qkv_ref, om_ref, kf_ref, gq_ref, gv_ref, gkf_ref, after_ref, *rest):
    outs, gk_scr, gv_scr = rest[:n], rest[n], rest[n + 1]
    s, _ = spot()
    dim = om_ref.shape[0]
    rows = outs[0].shape[1]
    scale = dim ** (-0.25)
    kf, after = kf_ref[...], after_ref[...]
    gv_scr[...] = bf(gv_ref[...] + mm(kf, after, NT))
    gkf = gkf_ref[...] + mm(qkv_ref[2], after)
    terms = bf(gkf * kf.astype(jnp.float32))
    total = jnp.sum(terms.astype(jnp.float32), axis=1, keepdims=True)
    wide = qkv_ref[1].astype(jnp.float32)
    gk_scr[...] = bf(mm(terms, om_ref[...], NT) * scale - total * wide * (scale * scale))
    for k in range(n):
        at = pl.ds(pl.multiple_of(lax.rem(s + n - k, n) * rows, 128), rows)
        outs[k][0] = gq_ref[at, :]
        outs[k][1] = gk_scr[at, :]
        outs[k][2] = gv_scr[at, :]


def mixed_project_kernel(n, offsets, *refs):
    mixed_in, w_ref, own_ref, sent_ref, scr = refs[:n], *refs[n:]
    s, h = spot()
    width = own_ref.shape[2]
    dim = mixed_in[0].shape[1]
    half = len(offsets) // 2
    for k in range(n):
        scr[:, lane(lax.rem(s + k, n), dim)] = mixed_in[k][...]
    mixed = scr[...]
    for at, offset in enumerate(offsets):
        part = bf(mm(mixed, w_ref[:, lane(h ^ offset, width)]))
        if at < half:
            own_ref[at] = part
        else:
            sent_ref[at - half] = part


def unpack_kernel(n, *refs):
    got, outs = refs[:n], refs[n:]
    s, _ = spot()
    dim = got[0].shape[2]
    for k in range(n):
        cols = lane(lax.rem(s + k, n), dim)
        for at, out in enumerate(outs):
            out[:, cols] = got[k][at]


def head_per_pair(queries, key_vectors, value_vectors, feature_proj, out_weight, grad_output):
    n, dim, feats = feature_proj.shape
    rows, width = grad_output.shape
    split = lax.axis_size("head")
    bits = bits_of(split)
    long = n * rows
    macs = long * dim * feats * 2
    f32 = jnp.float32

    *sends, om_sent = call(
        functools.partial(pack_kernel, n),
        [struct((3, rows, dim))] * n + [struct((dim, feats))],
        queries, key_vectors, value_vectors, feature_proj,
        specs=[HBM] * 4, scratch=[pltpu.SemaphoreType.DMA((3 * n + 1,))],
    )
    offsets, blocks = [0], [grad_output]
    for bit in reversed(bits):
        blocks = blocks + [swap(b, "head", bit) for b in blocks]
        offsets = offsets + [o ^ bit for o in offsets]
    om_in = swap(om_sent, "head", 1)
    got = scatter(sends)
    gm_parts = call(
        functools.partial(grad_mixed_kernel, n, offsets),
        [struct((rows, dim))] * n,
        *blocks, out_weight, flops=2 * rows * out_weight.size,
        scratch=[pltpu.VMEM((rows, n * dim), jnp.bfloat16)],
    )
    gm_in = scatter(gm_parts)
    qkv, om, kf, state, total = call(
        functools.partial(first_kernel, n),
        [
            struct((3, long, dim)),
            struct((dim, feats)),
            struct((long, feats)),
            struct((n, dim, feats)),
            struct((dim, feats)),
        ],
        *got, feature_proj, om_in, flops=2 * macs,
    )
    carried = pass_on(total, True)
    qf, scores, num = call(
        functools.partial(inner_kernel, n),
        [struct((long, feats)), struct((n, rows, rows)), struct((long, dim), f32)],
        qkv, om, kf, state, flops=4 * macs,
    )
    gn, later, later_total, *mixed_parts = call(
        functools.partial(turn_kernel, n),
        [struct((long, dim)), struct((n, dim, feats)), struct((dim, feats))]
        + [struct((rows, dim))] * n,
        *gm_in, qf, num, carried, flops=2 * macs,
        scratch=[pltpu.VMEM((long, dim), jnp.bfloat16)],
    )
    after_b = pass_on(later_total, False)
    mixed_in = gather(mixed_parts)
    gq, gv_part, gkf_part = call(
        functools.partial(back_kernel, n),
        [struct((long, dim)), struct((long, dim), f32), struct((long, feats), f32)],
        qkv, om, kf, qf, scores, gn, state, carried, later, flops=8 * macs,
        scratch=[pltpu.VMEM((long, feats), f32)],
    )
    grads = call(
        functools.partial(end_kernel, n),
        [struct((3, rows, dim))] * n,
        qkv, om, kf, gq, gv_part, gkf_part, after_b, flops=3 * macs,
        scratch=[pltpu.VMEM((long, dim), jnp.bfloat16)] * 2,
    )
    grads_in = gather(grads)

    order = [o for o in range(split) if not o & 1] + [o for o in range(split) if o & 1]
    own, sent = call(
        functools.partial(mixed_project_kernel, n, order),
        [struct((split // 2, rows, width))] * 2,
        *mixed_in, out_weight, flops=2 * rows * out_weight.size,
        scratch=[pltpu.VMEM((rows, n * dim), jnp.bfloat16)],
    )
    layer_out = reduce_blocks(own, sent, bits)
    gq, gk, gv = call(
        functools.partial(unpack_kernel, n), [struct((rows, n * dim))] * 3, *grads_in
    )
    return layer_out, gq, gk, gv


def solution(mesh):
    placed = (
        P("seq", "head"),
        P("seq", "head"),
        P("seq", "head"),
        P("head", None, None),
        P("head", None),
        P("seq", "head"),
    )

    def local(queries, key_vectors, value_vectors, feature_proj, out_weight, grad_output):
        paired = mesh.shape["seq"] == 2 * feature_proj.shape[0] and mesh.shape["head"] % 2 == 0
        body = head_per_pair if paired else scanned
        return body(
            queries, key_vectors, value_vectors, feature_proj, out_weight, grad_output
        )

    return jax.shard_map(
        local,
        mesh=mesh,
        in_specs=placed,
        out_specs=(P("seq", "head"),) * 4,
        check_vma=False,
    )
```

```python
import functools

import jax
import jax.numpy as jnp
from jax import lax
from jax.experimental import pallas as pl
from jax.experimental.pallas import tpu as pltpu
from jax.sharding import PartitionSpec as P

EPSILON = 1e-05
VMEM = pl.BlockSpec(memory_space=pltpu.VMEM)
SMEM = pl.BlockSpec(memory_space=pltpu.SMEM)
ANY = pl.BlockSpec(memory_space=pl.ANY)
HBM = pl.BlockSpec(memory_space=pltpu.HBM)
NN = (((1,), (0,)), ((), ()))
NT = (((1,), (1,)), ((), ()))
TN = (((0,), (0,)), ((), ()))


def mm(a, b, dims=NN):
    return lax.dot_general(a, b, dims, preferred_element_type=jnp.float32)


def bf(x):
    return x.astype(jnp.bfloat16)


def call(body, outs, *args, flops=0, specs=None, scratch=(), vmem=32):
    size = sum(a.size * a.dtype.itemsize for a in args)
    size += sum(o.size * o.dtype.itemsize for o in outs)
    return pl.pallas_call(
        body,
        out_shape=outs,
        in_specs=specs or [VMEM] * len(args),
        out_specs=[VMEM] * len(outs),
        scratch_shapes=list(scratch),
        cost_estimate=pl.CostEstimate(flops=flops, bytes_accessed=size, transcendentals=0),
        compiler_params=pltpu.CompilerParams(vmem_limit_bytes=vmem * 1024 * 1024),
    )(*args)


def struct(shape, dtype=jnp.bfloat16):
    return jax.ShapeDtypeStruct(shape, dtype)


def causal_mask(rows):
    row = lax.broadcasted_iota(jnp.int32, (rows, rows), 0)
    col = lax.broadcasted_iota(jnp.int32, (rows, rows), 1)
    return col <= row


def key_kernel(heads, k_ref, v_ref, om_ref, kf_ref, state_ref):
    dim, feats = om_ref.shape[1:]
    scale = dim ** (-0.25)
    for h in range(heads):
        cols, fcols = pl.ds(h * dim, dim), pl.ds(h * feats, feats)
        k = k_ref[:, cols]
        wide = k.astype(jnp.float32)
        half_sq = jnp.sum(wide * wide, axis=1, keepdims=True) * (scale * scale * 0.5)
        kf = bf(jnp.exp(mm(k, om_ref[h]) * scale - half_sq))
        kf_ref[:, fcols] = kf
        state_ref[cols, :] = bf(mm(v_ref[:, cols], kf, TN))


def local_kernel(heads, offsets, me_ref, q_ref, v_ref, om_ref, kf_ref, go_ref, w_ref,
                 qf_ref, scores_ref, num_ref, gm_ref):
    rows = q_ref.shape[0]
    dim, feats = om_ref.shape[1:]
    width = go_ref.shape[2]
    scale = dim ** (-0.25)
    causal = causal_mask(rows)
    for h in range(heads):
        cols, fcols = pl.ds(h * dim, dim), pl.ds(h * feats, feats)
        qf = bf(jnp.exp(mm(q_ref[:, cols], om_ref[h]) * scale))
        qf_ref[:, fcols] = qf
        scores = bf(jnp.where(causal, mm(qf, kf_ref[:, fcols], NT), 0.0))
        scores_ref[h] = scores
        num_ref[:, cols] = mm(scores, v_ref[:, cols])
    total = None
    for at, offset in enumerate(offsets):
        block = me_ref[0] ^ offset
        part = mm(go_ref[at], w_ref[:, pl.ds(pl.multiple_of(block * width, 128), width)], NT)
        total = part if total is None else total + part
    gm_ref[...] = total


def middle_kernel(heads, qf_ref, num_ref, gm_ref, carried_ref, mixed_ref, gn_ref, later_ref):
    dim = carried_ref.shape[0] // heads
    feats = carried_ref.shape[1]
    for h in range(heads):
        cols, fcols = pl.ds(h * dim, dim), pl.ds(h * feats, feats)
        qf = qf_ref[:, fcols]
        num = num_ref[:, cols] + mm(qf, carried_ref[cols, :], NT)
        inv = lax.rsqrt(jnp.mean(num * num, axis=1, keepdims=True) + EPSILON)
        normed = num * inv
        mixed_ref[:, cols] = bf(normed)
        gm = gm_ref[:, cols]
        gn = bf((gm - normed * jnp.mean(gm * normed, axis=1, keepdims=True)) * inv)
        gn_ref[:, cols] = gn
        later_ref[cols, :] = bf(mm(gn, qf, TN))


def project_kernel(offsets, me_ref, mixed_ref, w_ref, own_ref, sent_ref):
    width = own_ref.shape[2]
    half = len(offsets) // 2
    mixed = mixed_ref[...]
    for at, offset in enumerate(offsets):
        block = me_ref[0] ^ offset
        part = bf(mm(mixed, w_ref[:, pl.ds(pl.multiple_of(block * width, 128), width)]))
        if at < half:
            own_ref[at] = part
        else:
            sent_ref[at - half] = part


def query_kernel(heads, qf_ref, kf_ref, v_ref, om_ref, scores_ref, gn_ref, carried_ref,
                 gq_ref, gv_ref, gkf_ref):
    rows = qf_ref.shape[0]
    dim, feats = om_ref.shape[1:]
    scale = dim ** (-0.25)
    causal = causal_mask(rows)
    for h in range(heads):
        cols, fcols = pl.ds(h * dim, dim), pl.ds(h * feats, feats)
        qf, kf, gn = qf_ref[:, fcols], kf_ref[:, fcols], gn_ref[:, cols]
        gs = bf(jnp.where(causal, mm(gn, v_ref[:, cols], NT), 0.0))
        gqf = mm(gs, kf) + mm(gn, carried_ref[cols, :])
        terms = bf(gqf * qf.astype(jnp.float32))
        gq_ref[:, cols] = bf(mm(terms, om_ref[h], NT) * scale)
        gv_ref[:, cols] = mm(scores_ref[h], gn, TN)
        gkf_ref[:, fcols] = mm(gs, qf, TN)


def last_kernel(heads, k_ref, v_ref, om_ref, kf_ref, gv_in_ref, gkf_ref, after_ref,
                gk_ref, gv_ref):
    dim, feats = om_ref.shape[1:]
    scale = dim ** (-0.25)
    for h in range(heads):
        cols, fcols = pl.ds(h * dim, dim), pl.ds(h * feats, feats)
        kf, after = kf_ref[:, fcols], after_ref[cols, :]
        gv_ref[:, cols] = bf(gv_in_ref[:, cols] + mm(kf, after, NT))
        gkf = gkf_ref[:, fcols] + mm(v_ref[:, cols], after)
        terms = bf(gkf * kf.astype(jnp.float32))
        total = jnp.sum(terms.astype(jnp.float32), axis=1, keepdims=True)
        wide = k_ref[:, cols].astype(jnp.float32)
        gk_ref[:, cols] = bf(
            mm(terms, om_ref[h], NT) * scale - total * wide * (scale * scale)
        )


def prefix_kernel(in_ref, out_ref):
    total = jnp.zeros(in_ref.shape[1:], jnp.float32)
    for at in range(in_ref.shape[0]):
        out_ref[at] = bf(total)
        total = total + in_ref[at].astype(jnp.float32)


def swap(array, axis, bit):
    size = lax.axis_size(axis)
    return lax.ppermute(array, axis, [(i, i ^ bit) for i in range(size)])


def bits_of(size):
    return [1 << b for b in range(size.bit_length() - 1)]


def before(state, axis):
    size = lax.axis_size(axis)
    parts = state.reshape((size, state.shape[0] // size) + state.shape[1:])
    mine = lax.all_to_all(parts, axis, 0, 0)
    (sums,) = call(prefix_kernel, [struct(mine.shape)], mine)
    return lax.all_to_all(sums, axis, 0, 0).reshape(state.shape)


def after(state, axis):
    size = lax.axis_size(axis)
    step, inclusive, exclusive = 1, state.astype(jnp.float32), None
    while step < size:
        got = lax.ppermute(
            bf(inclusive), axis, [(i, i - step) for i in range(step, size)]
        ).astype(jnp.float32)
        exclusive = got if exclusive is None else exclusive + got
        inclusive = inclusive + got
        step *= 2
    return bf(exclusive)


def reduce_blocks(own, sent, bits):
    got = swap(sent, "head", 1)
    for bit in bits[1:]:
        total = own.astype(jnp.float32) + got.astype(jnp.float32)
        pairs = total.reshape((total.shape[0] // 2, 2) + total.shape[1:])
        own, got = pairs[:, 0], swap(bf(pairs[:, 1]), "head", bit)
    return own[0].astype(jnp.float32), got[0]


def scanned(queries, key_vectors, value_vectors, feature_proj, out_weight, grad_output):
    heads, dim, feats = feature_proj.shape
    rows, width = grad_output.shape
    split = lax.axis_size("head")
    bits = bits_of(split)
    me = lax.axis_index("head").astype(jnp.int32).reshape(1)
    macs = rows * dim * feats * heads * 2

    kf, state = call(
        functools.partial(key_kernel, heads),
        [struct((rows, heads * feats)), struct((heads * dim, feats))],
        key_vectors, value_vectors, feature_proj, flops=2 * macs,
    )
    carried = before(state, "seq")

    offsets, gathered = [0], grad_output[None]
    for bit in reversed(bits):
        gathered = jnp.concatenate([gathered, swap(gathered, "head", bit)], axis=0)
        offsets = offsets + [o ^ bit for o in offsets]
    qf, scores, num, gm = call(
        functools.partial(local_kernel, heads, offsets),
        [
            struct((rows, heads * feats)),
            struct((heads, rows, rows)),
            struct((rows, heads * dim), jnp.float32),
            struct((rows, heads * dim), jnp.float32),
        ],
        me, queries, value_vectors, feature_proj, kf, gathered, out_weight,
        flops=3 * macs + 2 * rows * out_weight.size, specs=[SMEM] + [VMEM] * 6,
    )
    mixed, gn, later = call(
        functools.partial(middle_kernel, heads),
        [
            struct((rows, heads * dim)),
            struct((rows, heads * dim)),
            struct((heads * dim, feats)),
        ],
        qf, num, gm, carried, flops=2 * macs,
    )
    after_b = after(later, "seq")

    order = [o for o in range(split) if not o & 1] + [o for o in range(split) if o & 1]
    own, sent = call(
        functools.partial(project_kernel, order),
        [struct((split // 2, rows, width))] * 2,
        me, mixed, out_weight, flops=2 * rows * out_weight.size, specs=[SMEM, VMEM, VMEM],
    )
    part, last = reduce_blocks(own, sent, bits)
    layer_out = bf(part + last.astype(jnp.float32))

    gq, gv_part, gkf_part = call(
        functools.partial(query_kernel, heads),
        [
            struct((rows, heads * dim)),
            struct((rows, heads * dim), jnp.float32),
            struct((rows, heads * feats), jnp.float32),
        ],
        qf, kf, value_vectors, feature_proj, scores, gn, carried, flops=5 * macs,
    )
    gk, gv = call(
        functools.partial(last_kernel, heads),
        [struct((rows, heads * dim))] * 2,
        key_vectors, value_vectors, feature_proj, kf, gv_part, gkf_part, after_b,
        flops=3 * macs,
    )
    return layer_out, gq, gk, gv


def spot():
    s, h = lax.axis_index("seq"), lax.axis_index("head")
    return s, h


def routes(k, n, seq, head):
    out = []
    for s in range(seq):
        for h in range(head):
            to = (n * (h % 2) + (s + k) % n) * head + 2 * (h // 2) + s // n
            out.append((s * head + h, to))
    return out


def scatter(parts):
    n, seq, head = len(parts), lax.axis_size("seq"), lax.axis_size("head")
    return [lax.ppermute(p, ("seq", "head"), routes(k, n, seq, head)) for k, p in enumerate(parts)]


def gather(parts):
    n, seq, head = len(parts), lax.axis_size("seq"), lax.axis_size("head")
    return [
        lax.ppermute(p, ("seq", "head"), [(b, a) for a, b in routes(k, n, seq, head)])
        for k, p in enumerate(parts)
    ]


def pass_on(array, forward):
    pairs = [(h, h + 1) if forward else (h + 1, h) for h in range(0, lax.axis_size("head"), 2)]
    return lax.ppermute(array, "head", pairs)


def lane(index, width):
    return pl.ds(pl.multiple_of(index * width, 128), width)


def pack_kernel(n, q_ref, k_ref, v_ref, om_ref, go_ref, *rest):
    outs, om_out, go_out, sems = rest[:n], rest[n], rest[n + 1], rest[n + 2]
    s, _ = spot()
    dim = om_ref.shape[1]
    copies = [(go_ref, go_out)]
    for k in range(n):
        cols = lane(lax.rem(s + k, n), dim)
        for at, ref in enumerate((q_ref, k_ref, v_ref)):
            copies.append((ref.at[:, cols], outs[k].at[at]))
    copies.append((om_ref.at[lax.rem(s, n)], om_out))
    started = [pltpu.make_async_copy(a, b, sems.at[i]) for i, (a, b) in enumerate(copies)]
    for copy in started:
        copy.start()
    for copy in started:
        copy.wait()


def grad_mixed_kernel(n, offsets, *refs):
    blocks, w_ref = refs[: len(offsets)], refs[len(offsets)]
    outs, (scr, w_scr, sems) = refs[len(offsets) + 1 : -3], refs[-3:]
    s, h = spot()
    width = blocks[0].shape[1]
    dim = outs[0].shape[1]
    copies = [
        pltpu.make_async_copy(w_ref.at[:, lane(h ^ offset, width)], w_scr.at[at], sems.at[at])
        for at, offset in enumerate(offsets)
    ]
    for copy in copies:
        copy.start()
    total = None
    for at, ref in enumerate(blocks):
        copies[at].wait()
        part = mm(ref[...], w_scr[at], NT)
        total = part if total is None else total + part
    scr[...] = bf(total)
    for k in range(n):
        outs[k][...] = scr[:, lane(lax.rem(s + k, n), dim)]


def first_kernel(n, *refs):
    got, own_om_ref, om_in_ref = refs[:n], refs[n], refs[n + 1]
    qkv_ref, om_ref, kf_ref, state_ref, total_ref = refs[n + 3 :]
    s, h = spot()
    rows, dim = got[0].shape[1:]
    scale = dim ** (-0.25)
    for k in range(n):
        at = pl.ds(pl.multiple_of(lax.rem(s + n - k, n) * rows, 128), rows)
        qkv_ref[:, at, :] = got[k][...]
    mine = lax.div(s, n) == lax.rem(h, 2)
    om = jnp.where(mine, own_om_ref[...], om_in_ref[...])
    om_ref[...] = om
    k_all = qkv_ref[1]
    wide = k_all.astype(jnp.float32)
    half_sq = jnp.sum(wide * wide, axis=1, keepdims=True) * (scale * scale * 0.5)
    kf = bf(jnp.exp(mm(k_all, om) * scale - half_sq))
    kf_ref[...] = kf
    total = jnp.zeros(total_ref.shape, jnp.float32)
    for t in range(n):
        at = pl.ds(t * rows, rows)
        state_ref[t] = bf(total)
        total = total + mm(qkv_ref[2, at, :], kf[t * rows : (t + 1) * rows], TN)
    total_ref[...] = bf(total)


def inner_kernel(n, qkv_ref, om_ref, kf_ref, state_ref, qf_ref, scores_ref, num_ref):
    dim = om_ref.shape[0]
    rows = scores_ref.shape[1]
    scale = dim ** (-0.25)
    causal = causal_mask(rows)
    qf_ref[...] = bf(jnp.exp(mm(qkv_ref[0], om_ref[...]) * scale))
    for t in range(n):
        at = pl.ds(t * rows, rows)
        qf = qf_ref[at, :]
        scores = bf(jnp.where(causal, mm(qf, kf_ref[at, :], NT), 0.0))
        scores_ref[t] = scores
        num_ref[at, :] = mm(scores, qkv_ref[2, at, :]) + mm(qf, state_ref[t], NT)


def turn_kernel(n, *refs):
    gm_in, (qf_ref, num_ref, carried_ref) = refs[:n], refs[n : n + 3]
    gn_ref, state_ref, total_ref = refs[n + 3 : n + 6]
    outs, scr = refs[n + 6 : -1], refs[-1]
    s, _ = spot()
    rows = gm_in[0].shape[0]
    places = [
        pl.ds(pl.multiple_of(lax.rem(s + n - k, n) * rows, 128), rows) for k in range(n)
    ]
    for k in range(n):
        scr[places[k], :] = gm_in[k][...]
    num = num_ref[...] + mm(qf_ref[...], carried_ref[...], NT)
    inv = lax.rsqrt(jnp.mean(num * num, axis=1, keepdims=True) + EPSILON)
    normed = num * inv
    gm = scr[...].astype(jnp.float32)
    gn = bf((gm - normed * jnp.mean(gm * normed, axis=1, keepdims=True)) * inv)
    gn_ref[...] = gn
    scr[...] = bf(normed)
    for k in range(n):
        outs[k][...] = scr[places[k], :]
    total = jnp.zeros(total_ref.shape, jnp.float32)
    for t in reversed(range(n)):
        state_ref[t] = bf(total)
        at = pl.ds(t * rows, rows)
        total = total + mm(gn[t * rows : (t + 1) * rows], qf_ref[at, :], TN)
    total_ref[...] = bf(total)


def back_kernel(n, qkv_ref, om_ref, kf_ref, qf_ref, scores_ref, gn_ref, state_ref, carried_ref,
                later_ref, gq_ref, gv_ref, gkf_ref, gqf_scr):
    dim = om_ref.shape[0]
    rows = scores_ref.shape[1]
    scale = dim ** (-0.25)
    causal = causal_mask(rows)
    gqf_scr[...] = mm(gn_ref[...], carried_ref[...])
    for t in range(n):
        at = pl.ds(t * rows, rows)
        qf, kf, gn, v = qf_ref[at, :], kf_ref[at, :], gn_ref[at, :], qkv_ref[2, at, :]
        gs = bf(jnp.where(causal, mm(gn, v, NT), 0.0))
        gqf = gqf_scr[at, :] + mm(gs, kf) + mm(gn, state_ref[t])
        terms = bf(gqf * qf.astype(jnp.float32))
        gq_ref[at, :] = bf(mm(terms, om_ref[...], NT) * scale)
        later = later_ref[t]
        gv_ref[at, :] = mm(scores_ref[t], gn, TN) + mm(kf, later, NT)
        gkf_ref[at, :] = mm(gs, qf, TN) + mm(v, later)


def end_kernel(n, qkv_ref, om_ref, kf_ref, gq_ref, gv_ref, gkf_ref, after_ref, *rest):
    outs, gk_scr, gv_scr = rest[:n], rest[n], rest[n + 1]
    s, _ = spot()
    dim = om_ref.shape[0]
    rows = outs[0].shape[1]
    scale = dim ** (-0.25)
    kf, after = kf_ref[...], after_ref[...]
    gv_scr[...] = bf(gv_ref[...] + mm(kf, after, NT))
    gkf = gkf_ref[...] + mm(qkv_ref[2], after)
    terms = bf(gkf * kf.astype(jnp.float32))
    total = jnp.sum(terms.astype(jnp.float32), axis=1, keepdims=True)
    wide = qkv_ref[1].astype(jnp.float32)
    gk_scr[...] = bf(mm(terms, om_ref[...], NT) * scale - total * wide * (scale * scale))
    for k in range(n):
        at = pl.ds(pl.multiple_of(lax.rem(s + n - k, n) * rows, 128), rows)
        outs[k][0] = gq_ref[at, :]
        outs[k][1] = gk_scr[at, :]
        outs[k][2] = gv_scr[at, :]


def mixed_project_kernel(n, offsets, *refs):
    mixed_in, (w_ref, _, own_ref, sent_ref, scr) = refs[:n], refs[n:]
    s, h = spot()
    width = own_ref.shape[2]
    dim = mixed_in[0].shape[1]
    half = len(offsets) // 2
    for k in range(n):
        scr[:, lane(lax.rem(s + k, n), dim)] = mixed_in[k][...]
    mixed = scr[...]
    for at, offset in enumerate(offsets):
        part = bf(mm(mixed, w_ref[:, lane(h ^ offset, width)]))
        if at < half:
            own_ref[at] = part
        else:
            sent_ref[at - half] = part


def unpack_kernel(n, *refs):
    got, (part_ref, last_ref), (out_ref, *outs) = refs[:n], refs[n : n + 2], refs[n + 2 :]
    s, _ = spot()
    dim = got[0].shape[2]
    out_ref[...] = bf(part_ref[...] + last_ref[...].astype(jnp.float32))
    for k in range(n):
        cols = lane(lax.rem(s + k, n), dim)
        for at, out in enumerate(outs):
            out[:, cols] = got[k][at]


def head_per_pair(queries, key_vectors, value_vectors, feature_proj, out_weight, grad_output):
    n, dim, feats = feature_proj.shape
    rows, width = grad_output.shape
    split = lax.axis_size("head")
    bits = bits_of(split)
    long = n * rows
    macs = long * dim * feats * 2
    f32 = jnp.float32

    *sends, om_own, go = call(
        functools.partial(pack_kernel, n),
        [struct((3, rows, dim))] * n + [struct((dim, feats)), struct(grad_output.shape)],
        queries, key_vectors, value_vectors, feature_proj, grad_output,
        specs=[HBM] * 5, scratch=[pltpu.SemaphoreType.DMA((3 * n + 2,))], vmem=60,
    )
    offsets, blocks = [0], [go]
    for bit in reversed(bits):
        blocks = blocks + [swap(b, "head", bit) for b in blocks]
        offsets = offsets + [o ^ bit for o in offsets]
    om_in = swap(om_own, "head", 1)
    got = scatter(sends)
    gm_parts = call(
        functools.partial(grad_mixed_kernel, n, offsets),
        [struct((rows, dim))] * n,
        *blocks, out_weight, flops=2 * rows * out_weight.size,
        specs=[VMEM] * split + [HBM], vmem=59,
        scratch=[
            pltpu.VMEM((rows, n * dim), jnp.bfloat16),
            pltpu.VMEM((split, n * dim, width), jnp.bfloat16),
            pltpu.SemaphoreType.DMA((split,)),
        ],
    )
    gm_in = scatter(gm_parts)
    qkv, om, kf, state, total = call(
        functools.partial(first_kernel, n),
        [
            struct((3, long, dim)),
            struct((dim, feats)),
            struct((long, feats)),
            struct((n, dim, feats)),
            struct((dim, feats)),
        ],
        *got, om_own, om_in, gm_parts[0], flops=2 * macs,
        specs=[VMEM] * (n + 2) + [ANY],
    )
    carried = pass_on(total, True)
    qf, scores, num = call(
        functools.partial(inner_kernel, n),
        [struct((long, feats)), struct((n, rows, rows)), struct((long, dim), f32)],
        qkv, om, kf, state, flops=4 * macs,
    )
    gn, later, later_total, *mixed_parts = call(
        functools.partial(turn_kernel, n),
        [struct((long, dim)), struct((n, dim, feats)), struct((dim, feats))]
        + [struct((rows, dim))] * n,
        *gm_in, qf, num, carried, flops=2 * macs,
        scratch=[pltpu.VMEM((long, dim), jnp.bfloat16)],
    )
    after_b = pass_on(later_total, False)
    mixed_in = gather(mixed_parts)
    gq, gv_part, gkf_part = call(
        functools.partial(back_kernel, n),
        [struct((long, dim)), struct((long, dim), f32), struct((long, feats), f32)],
        qkv, om, kf, qf, scores, gn, state, carried, later, flops=8 * macs,
        scratch=[pltpu.VMEM((long, feats), f32)],
    )
    grads = call(
        functools.partial(end_kernel, n),
        [struct((3, rows, dim))] * n,
        qkv, om, kf, gq, gv_part, gkf_part, after_b, flops=3 * macs,
        scratch=[pltpu.VMEM((long, dim), jnp.bfloat16)] * 2,
    )
    grads_in = gather(grads)

    order = [o for o in range(split) if not o & 1] + [o for o in range(split) if o & 1]
    own, sent = call(
        functools.partial(mixed_project_kernel, n, order),
        [struct((split // 2, rows, width))] * 2,
        *mixed_in, out_weight, grads[0], flops=2 * rows * out_weight.size,
        specs=[VMEM] * (n + 1) + [ANY],
        scratch=[pltpu.VMEM((rows, n * dim), jnp.bfloat16)],
    )
    part, last = reduce_blocks(own, sent, bits)
    return call(
        functools.partial(unpack_kernel, n),
        [struct((rows, width))] + [struct((rows, n * dim))] * 3,
        *grads_in, part, last,
    )


def solution(mesh):
    placed = (
        P("seq", "head"),
        P("seq", "head"),
        P("seq", "head"),
        P("head", None, None),
        P("head", None),
        P("seq", "head"),
    )

    def local(queries, key_vectors, value_vectors, feature_proj, out_weight, grad_output):
        paired = mesh.shape["seq"] == 2 * feature_proj.shape[0] and mesh.shape["head"] % 2 == 0
        body = head_per_pair if paired else scanned
        return body(
            queries, key_vectors, value_vectors, feature_proj, out_weight, grad_output
        )

    return jax.shard_map(
        local,
        mesh=mesh,
        in_specs=placed,
        out_specs=(P("seq", "head"),) * 4,
        check_vma=False,
    )
```

```python
import functools

import jax
import jax.numpy as jnp
from jax import lax
from jax.experimental import pallas as pl
from jax.experimental.pallas import tpu as pltpu
from jax.sharding import PartitionSpec as P

EPSILON = 1e-05
VMEM = pl.BlockSpec(memory_space=pltpu.VMEM)
SMEM = pl.BlockSpec(memory_space=pltpu.SMEM)
ANY = pl.BlockSpec(memory_space=pl.ANY)
NN = (((1,), (0,)), ((), ()))
NT = (((1,), (1,)), ((), ()))
TN = (((0,), (0,)), ((), ()))


def mm(a, b, dims=NN):
    return lax.dot_general(a, b, dims, preferred_element_type=jnp.float32)


def bf(x):
    return x.astype(jnp.bfloat16)


def call(body, outs, *args, flops=0, specs=None, out_specs=None, scratch=(), vmem=32):
    size = sum(a.size * a.dtype.itemsize for a in args)
    size += sum(o.size * o.dtype.itemsize for o in outs)
    return pl.pallas_call(
        body,
        out_shape=outs,
        in_specs=specs or [VMEM] * len(args),
        out_specs=out_specs or [VMEM] * len(outs),
        scratch_shapes=list(scratch),
        cost_estimate=pl.CostEstimate(flops=flops, bytes_accessed=size, transcendentals=0),
        compiler_params=pltpu.CompilerParams(vmem_limit_bytes=vmem * 1024 * 1024),
    )(*args)


def struct(shape, dtype=jnp.bfloat16):
    return jax.ShapeDtypeStruct(shape, dtype)


def causal_mask(rows):
    row = lax.broadcasted_iota(jnp.int32, (rows, rows), 0)
    col = lax.broadcasted_iota(jnp.int32, (rows, rows), 1)
    return col <= row


def key_kernel(heads, k_ref, v_ref, om_ref, kf_ref, state_ref):
    dim, feats = om_ref.shape[1:]
    scale = dim ** (-0.25)
    for h in range(heads):
        cols, fcols = pl.ds(h * dim, dim), pl.ds(h * feats, feats)
        k = k_ref[:, cols]
        wide = k.astype(jnp.float32)
        half_sq = jnp.sum(wide * wide, axis=1, keepdims=True) * (scale * scale * 0.5)
        kf = bf(jnp.exp(mm(k, om_ref[h]) * scale - half_sq))
        kf_ref[:, fcols] = kf
        state_ref[cols, :] = bf(mm(v_ref[:, cols], kf, TN))


def local_kernel(heads, offsets, me_ref, q_ref, v_ref, om_ref, kf_ref, go_ref, w_ref,
                 qf_ref, scores_ref, num_ref, gm_ref):
    rows = q_ref.shape[0]
    dim, feats = om_ref.shape[1:]
    width = go_ref.shape[2]
    scale = dim ** (-0.25)
    causal = causal_mask(rows)
    for h in range(heads):
        cols, fcols = pl.ds(h * dim, dim), pl.ds(h * feats, feats)
        qf = bf(jnp.exp(mm(q_ref[:, cols], om_ref[h]) * scale))
        qf_ref[:, fcols] = qf
        scores = bf(jnp.where(causal, mm(qf, kf_ref[:, fcols], NT), 0.0))
        scores_ref[h] = scores
        num_ref[:, cols] = mm(scores, v_ref[:, cols])
    total = None
    for at, offset in enumerate(offsets):
        block = me_ref[0] ^ offset
        part = mm(go_ref[at], w_ref[:, pl.ds(pl.multiple_of(block * width, 128), width)], NT)
        total = part if total is None else total + part
    gm_ref[...] = total


def middle_kernel(heads, qf_ref, num_ref, gm_ref, carried_ref, mixed_ref, gn_ref, later_ref):
    dim = carried_ref.shape[0] // heads
    feats = carried_ref.shape[1]
    for h in range(heads):
        cols, fcols = pl.ds(h * dim, dim), pl.ds(h * feats, feats)
        qf = qf_ref[:, fcols]
        num = num_ref[:, cols] + mm(qf, carried_ref[cols, :], NT)
        inv = lax.rsqrt(jnp.mean(num * num, axis=1, keepdims=True) + EPSILON)
        normed = num * inv
        mixed_ref[:, cols] = bf(normed)
        gm = gm_ref[:, cols]
        gn = bf((gm - normed * jnp.mean(gm * normed, axis=1, keepdims=True)) * inv)
        gn_ref[:, cols] = gn
        later_ref[cols, :] = bf(mm(gn, qf, TN))


def project_kernel(offsets, me_ref, mixed_ref, w_ref, own_ref, sent_ref):
    width = own_ref.shape[2]
    half = len(offsets) // 2
    mixed = mixed_ref[...]
    for at, offset in enumerate(offsets):
        block = me_ref[0] ^ offset
        part = bf(mm(mixed, w_ref[:, pl.ds(pl.multiple_of(block * width, 128), width)]))
        if at < half:
            own_ref[at] = part
        else:
            sent_ref[at - half] = part


def query_kernel(heads, qf_ref, kf_ref, v_ref, om_ref, scores_ref, gn_ref, carried_ref,
                 gq_ref, gv_ref, gkf_ref):
    rows = qf_ref.shape[0]
    dim, feats = om_ref.shape[1:]
    scale = dim ** (-0.25)
    causal = causal_mask(rows)
    for h in range(heads):
        cols, fcols = pl.ds(h * dim, dim), pl.ds(h * feats, feats)
        qf, kf, gn = qf_ref[:, fcols], kf_ref[:, fcols], gn_ref[:, cols]
        gs = bf(jnp.where(causal, mm(gn, v_ref[:, cols], NT), 0.0))
        gqf = mm(gs, kf) + mm(gn, carried_ref[cols, :])
        terms = bf(gqf * qf.astype(jnp.float32))
        gq_ref[:, cols] = bf(mm(terms, om_ref[h], NT) * scale)
        gv_ref[:, cols] = mm(scores_ref[h], gn, TN)
        gkf_ref[:, fcols] = mm(gs, qf, TN)


def last_kernel(heads, k_ref, v_ref, om_ref, kf_ref, gv_in_ref, gkf_ref, after_ref,
                gk_ref, gv_ref):
    dim, feats = om_ref.shape[1:]
    scale = dim ** (-0.25)
    for h in range(heads):
        cols, fcols = pl.ds(h * dim, dim), pl.ds(h * feats, feats)
        kf, after = kf_ref[:, fcols], after_ref[cols, :]
        gv_ref[:, cols] = bf(gv_in_ref[:, cols] + mm(kf, after, NT))
        gkf = gkf_ref[:, fcols] + mm(v_ref[:, cols], after)
        terms = bf(gkf * kf.astype(jnp.float32))
        total = jnp.sum(terms.astype(jnp.float32), axis=1, keepdims=True)
        wide = k_ref[:, cols].astype(jnp.float32)
        gk_ref[:, cols] = bf(
            mm(terms, om_ref[h], NT) * scale - total * wide * (scale * scale)
        )


def prefix_kernel(in_ref, out_ref):
    total = jnp.zeros(in_ref.shape[1:], jnp.float32)
    for at in range(in_ref.shape[0]):
        out_ref[at] = bf(total)
        total = total + in_ref[at].astype(jnp.float32)


def swap(array, axis, bit):
    size = lax.axis_size(axis)
    return lax.ppermute(array, axis, [(i, i ^ bit) for i in range(size)])


def bits_of(size):
    return [1 << b for b in range(size.bit_length() - 1)]


def before(state, axis):
    size = lax.axis_size(axis)
    parts = state.reshape((size, state.shape[0] // size) + state.shape[1:])
    mine = lax.all_to_all(parts, axis, 0, 0)
    (sums,) = call(prefix_kernel, [struct(mine.shape)], mine)
    return lax.all_to_all(sums, axis, 0, 0).reshape(state.shape)


def after(state, axis):
    size = lax.axis_size(axis)
    step, inclusive, exclusive = 1, state.astype(jnp.float32), None
    while step < size:
        got = lax.ppermute(
            bf(inclusive), axis, [(i, i - step) for i in range(step, size)]
        ).astype(jnp.float32)
        exclusive = got if exclusive is None else exclusive + got
        inclusive = inclusive + got
        step *= 2
    return bf(exclusive)


def reduce_blocks(own, sent, bits):
    got = swap(sent, "head", 1)
    for bit in bits[1:]:
        total = own.astype(jnp.float32) + got.astype(jnp.float32)
        pairs = total.reshape((total.shape[0] // 2, 2) + total.shape[1:])
        own, got = pairs[:, 0], swap(bf(pairs[:, 1]), "head", bit)
    return own[0].astype(jnp.float32), got[0]


def scanned(queries, key_vectors, value_vectors, feature_proj, out_weight, grad_output):
    heads, dim, feats = feature_proj.shape
    rows, width = grad_output.shape
    split = lax.axis_size("head")
    bits = bits_of(split)
    me = lax.axis_index("head").astype(jnp.int32).reshape(1)
    macs = rows * dim * feats * heads * 2

    kf, state = call(
        functools.partial(key_kernel, heads),
        [struct((rows, heads * feats)), struct((heads * dim, feats))],
        key_vectors, value_vectors, feature_proj, flops=2 * macs,
    )
    carried = before(state, "seq")

    offsets, gathered = [0], grad_output[None]
    for bit in reversed(bits):
        gathered = jnp.concatenate([gathered, swap(gathered, "head", bit)], axis=0)
        offsets = offsets + [o ^ bit for o in offsets]
    qf, scores, num, gm = call(
        functools.partial(local_kernel, heads, offsets),
        [
            struct((rows, heads * feats)),
            struct((heads, rows, rows)),
            struct((rows, heads * dim), jnp.float32),
            struct((rows, heads * dim), jnp.float32),
        ],
        me, queries, value_vectors, feature_proj, kf, gathered, out_weight,
        flops=3 * macs + 2 * rows * out_weight.size, specs=[SMEM] + [VMEM] * 6,
    )
    mixed, gn, later = call(
        functools.partial(middle_kernel, heads),
        [
            struct((rows, heads * dim)),
            struct((rows, heads * dim)),
            struct((heads * dim, feats)),
        ],
        qf, num, gm, carried, flops=2 * macs,
    )
    after_b = after(later, "seq")

    order = [o for o in range(split) if not o & 1] + [o for o in range(split) if o & 1]
    own, sent = call(
        functools.partial(project_kernel, order),
        [struct((split // 2, rows, width))] * 2,
        me, mixed, out_weight, flops=2 * rows * out_weight.size, specs=[SMEM, VMEM, VMEM],
    )
    part, last = reduce_blocks(own, sent, bits)
    layer_out = bf(part + last.astype(jnp.float32))

    gq, gv_part, gkf_part = call(
        functools.partial(query_kernel, heads),
        [
            struct((rows, heads * dim)),
            struct((rows, heads * dim), jnp.float32),
            struct((rows, heads * feats), jnp.float32),
        ],
        qf, kf, value_vectors, feature_proj, scores, gn, carried, flops=5 * macs,
    )
    gk, gv = call(
        functools.partial(last_kernel, heads),
        [struct((rows, heads * dim))] * 2,
        key_vectors, value_vectors, feature_proj, kf, gv_part, gkf_part, after_b,
        flops=3 * macs,
    )
    return layer_out, gq, gk, gv


def spot():
    s, h = lax.axis_index("seq"), lax.axis_index("head")
    return s, h


def routes(k, n, seq, head):
    out = []
    for s in range(seq):
        for h in range(head):
            to = (n * (h % 2) + (s + k) % n) * head + 2 * (h // 2) + s // n
            out.append((s * head + h, to))
    return out


def scatter(parts):
    n, seq, head = len(parts), lax.axis_size("seq"), lax.axis_size("head")
    return [lax.ppermute(p, ("seq", "head"), routes(k, n, seq, head)) for k, p in enumerate(parts)]


def gather(parts):
    n, seq, head = len(parts), lax.axis_size("seq"), lax.axis_size("head")
    return [
        lax.ppermute(p, ("seq", "head"), [(b, a) for a, b in routes(k, n, seq, head)])
        for k, p in enumerate(parts)
    ]


def pass_on(array, forward):
    pairs = [(h, h + 1) if forward else (h + 1, h) for h in range(0, lax.axis_size("head"), 2)]
    return lax.ppermute(array, "head", pairs)


def lane(index, width):
    return pl.ds(pl.multiple_of(index * width, 128), width)


def pack_kernel(n, q_ref, k_ref, v_ref, om_ref, go_ref, *rest):
    outs, om_out, go_out, sems = rest[:n], rest[n], rest[n + 1], rest[n + 2]
    s, _ = spot()
    dim = om_ref.shape[1]
    copies = [(go_ref, go_out)]
    for k in range(n):
        cols = lane(lax.rem(s + k, n), dim)
        for at, ref in enumerate((q_ref, k_ref, v_ref)):
            copies.append((ref.at[:, cols], outs[k].at[at]))
    copies.append((om_ref.at[lax.rem(s, n)], om_out))
    started = [pltpu.make_async_copy(a, b, sems.at[i]) for i, (a, b) in enumerate(copies)]
    for copy in started:
        copy.start()
    for copy in started:
        copy.wait()


def grad_mixed_kernel(n, *refs):
    blocks, w_ref, outs, scr = refs[: -n - 2], refs[-n - 2], refs[-n - 1 : -1], refs[-1]
    s, h = spot()
    width = blocks[0].shape[1]
    dim = outs[0].shape[1]
    total = None
    for offset, ref in enumerate(blocks):
        part = mm(ref[...], w_ref[:, lane(h ^ offset, width)], NT)
        total = part if total is None else total + part
    scr[...] = bf(total)
    for k in range(n):
        outs[k][...] = scr[:, lane(lax.rem(s + k, n), dim)]


def first_kernel(n, *refs):
    got, own_om_ref, om_in_ref = refs[:n], refs[n], refs[n + 1]
    qkv_ref, om_ref, kf_ref, state_ref, total_ref = refs[n + 3 :]
    s, h = spot()
    rows, dim = got[0].shape[1:]
    scale = dim ** (-0.25)
    for k in range(n):
        at = pl.ds(pl.multiple_of(lax.rem(s + n - k, n) * rows, 128), rows)
        qkv_ref[:, at, :] = got[k][...]
    mine = lax.div(s, n) == lax.rem(h, 2)
    om = jnp.where(mine, own_om_ref[...], om_in_ref[...])
    om_ref[...] = om
    k_all = qkv_ref[1]
    wide = k_all.astype(jnp.float32)
    half_sq = jnp.sum(wide * wide, axis=1, keepdims=True) * (scale * scale * 0.5)
    kf = bf(jnp.exp(mm(k_all, om) * scale - half_sq))
    kf_ref[...] = kf
    total = jnp.zeros(total_ref.shape, jnp.float32)
    for t in range(n):
        at = pl.ds(t * rows, rows)
        state_ref[t] = bf(total)
        total = total + mm(qkv_ref[2, at, :], kf[t * rows : (t + 1) * rows], TN)
    total_ref[...] = bf(total)


def inner_kernel(n, qkv_ref, om_ref, kf_ref, state_ref, qf_ref, scores_ref, num_ref):
    dim = om_ref.shape[0]
    rows = scores_ref.shape[1]
    scale = dim ** (-0.25)
    causal = causal_mask(rows)
    qf_ref[...] = bf(jnp.exp(mm(qkv_ref[0], om_ref[...]) * scale))
    for t in range(n):
        at = pl.ds(t * rows, rows)
        qf = qf_ref[at, :]
        scores = bf(jnp.where(causal, mm(qf, kf_ref[at, :], NT), 0.0))
        scores_ref[t] = scores
        num_ref[at, :] = mm(scores, qkv_ref[2, at, :]) + mm(qf, state_ref[t], NT)


def turn_kernel(n, *refs):
    gm_in, (qf_ref, num_ref, carried_ref) = refs[:n], refs[n : n + 3]
    gn_ref, state_ref, total_ref = refs[n + 3 : n + 6]
    outs, scr = refs[n + 6 : -1], refs[-1]
    s, _ = spot()
    rows = gm_in[0].shape[0]
    places = [
        pl.ds(pl.multiple_of(lax.rem(s + n - k, n) * rows, 128), rows) for k in range(n)
    ]
    for k in range(n):
        scr[places[k], :] = gm_in[k][...]
    num = num_ref[...] + mm(qf_ref[...], carried_ref[...], NT)
    inv = lax.rsqrt(jnp.mean(num * num, axis=1, keepdims=True) + EPSILON)
    normed = num * inv
    gm = scr[...].astype(jnp.float32)
    gn = bf((gm - normed * jnp.mean(gm * normed, axis=1, keepdims=True)) * inv)
    gn_ref[...] = gn
    scr[...] = bf(normed)
    for k in range(n):
        outs[k][...] = scr[places[k], :]
    total = jnp.zeros(total_ref.shape, jnp.float32)
    for t in reversed(range(n)):
        state_ref[t] = bf(total)
        at = pl.ds(t * rows, rows)
        total = total + mm(gn[t * rows : (t + 1) * rows], qf_ref[at, :], TN)
    total_ref[...] = bf(total)


def back_kernel(n, qkv_ref, om_ref, kf_ref, qf_ref, scores_ref, gn_ref, state_ref, carried_ref,
                later_ref, gq_ref, gv_ref, gkf_ref, gqf_scr):
    dim = om_ref.shape[0]
    rows = scores_ref.shape[1]
    scale = dim ** (-0.25)
    causal = causal_mask(rows)
    gqf_scr[...] = mm(gn_ref[...], carried_ref[...])
    for t in range(n):
        at = pl.ds(t * rows, rows)
        qf, kf, gn, v = qf_ref[at, :], kf_ref[at, :], gn_ref[at, :], qkv_ref[2, at, :]
        gs = bf(jnp.where(causal, mm(gn, v, NT), 0.0))
        gqf = gqf_scr[at, :] + mm(gs, kf) + mm(gn, state_ref[t])
        terms = bf(gqf * qf.astype(jnp.float32))
        gq_ref[at, :] = bf(mm(terms, om_ref[...], NT) * scale)
        later = later_ref[t]
        gv_ref[at, :] = mm(scores_ref[t], gn, TN) + mm(kf, later, NT)
        gkf_ref[at, :] = mm(gs, qf, TN) + mm(v, later)


def end_kernel(n, qkv_ref, om_ref, kf_ref, gq_ref, gv_ref, gkf_ref, after_ref, *rest):
    outs, gk_scr, gv_scr = rest[:n], rest[n], rest[n + 1]
    s, _ = spot()
    dim = om_ref.shape[0]
    rows = outs[0].shape[1]
    scale = dim ** (-0.25)
    kf, after = kf_ref[...], after_ref[...]
    gv_scr[...] = bf(gv_ref[...] + mm(kf, after, NT))
    gkf = gkf_ref[...] + mm(qkv_ref[2], after)
    terms = bf(gkf * kf.astype(jnp.float32))
    total = jnp.sum(terms.astype(jnp.float32), axis=1, keepdims=True)
    wide = qkv_ref[1].astype(jnp.float32)
    gk_scr[...] = bf(mm(terms, om_ref[...], NT) * scale - total * wide * (scale * scale))
    for k in range(n):
        at = pl.ds(pl.multiple_of(lax.rem(s + n - k, n) * rows, 128), rows)
        outs[k][0] = gq_ref[at, :]
        outs[k][1] = gk_scr[at, :]
        outs[k][2] = gv_scr[at, :]


def mixed_project_kernel(n, offsets, *refs):
    mixed_in, (w_ref, _, own_ref, sent_ref, scr) = refs[:n], refs[n:]
    s, h = spot()
    width = own_ref.shape[2]
    dim = mixed_in[0].shape[1]
    half = len(offsets) // 2
    for k in range(n):
        scr[:, lane(lax.rem(s + k, n), dim)] = mixed_in[k][...]
    mixed = scr[...]
    for at, offset in enumerate(offsets):
        part = bf(mm(mixed, w_ref[:, lane(h ^ offset, width)]))
        if at < half:
            own_ref[at] = part
        else:
            sent_ref[at - half] = part


def unpack_kernel(n, *refs):
    got, (part_ref, last_ref), (out_ref, *outs) = refs[:n], refs[n : n + 2], refs[n + 2 :]
    s, _ = spot()
    dim = got[0].shape[2]
    out_ref[...] = bf(part_ref[...] + last_ref[...].astype(jnp.float32))
    for k in range(n):
        cols = lane(lax.rem(s + k, n), dim)
        for at, out in enumerate(outs):
            out[:, cols] = got[k][at]


def head_per_pair(queries, key_vectors, value_vectors, feature_proj, out_weight, grad_output):
    n, dim, feats = feature_proj.shape
    rows, width = grad_output.shape
    split = lax.axis_size("head")
    bits = bits_of(split)
    long = n * rows
    macs = long * dim * feats * 2
    f32 = jnp.float32

    *sends, om_own, go = call(
        functools.partial(pack_kernel, n),
        [struct((3, rows, dim))] * n + [struct((dim, feats)), struct(grad_output.shape)],
        queries, key_vectors, value_vectors, feature_proj, grad_output,
        specs=[ANY] * 5, out_specs=[ANY] * (n + 2),
        scratch=[pltpu.SemaphoreType.DMA((3 * n + 2,))], vmem=60,
    )
    blocks = [go] + [swap(go, "head", offset) for offset in range(1, split)]
    om_in = swap(om_own, "head", 1)
    got = scatter(sends)
    gm_parts = call(
        functools.partial(grad_mixed_kernel, n),
        [struct((rows, dim))] * n,
        *blocks, out_weight, flops=2 * rows * out_weight.size,
        scratch=[pltpu.VMEM((rows, n * dim), jnp.bfloat16)],
    )
    gm_in = scatter(gm_parts)
    qkv, om, kf, state, total = call(
        functools.partial(first_kernel, n),
        [
            struct((3, long, dim)),
            struct((dim, feats)),
            struct((long, feats)),
            struct((n, dim, feats)),
            struct((dim, feats)),
        ],
        *got, om_own, om_in, gm_parts[0], flops=2 * macs,
        specs=[VMEM] * (n + 2) + [ANY],
    )
    carried = pass_on(total, True)
    qf, scores, num = call(
        functools.partial(inner_kernel, n),
        [struct((long, feats)), struct((n, rows, rows)), struct((long, dim), f32)],
        qkv, om, kf, state, flops=4 * macs,
    )
    gn, later, later_total, *mixed_parts = call(
        functools.partial(turn_kernel, n),
        [struct((long, dim)), struct((n, dim, feats)), struct((dim, feats))]
        + [struct((rows, dim))] * n,
        *gm_in, qf, num, carried, flops=2 * macs,
        scratch=[pltpu.VMEM((long, dim), jnp.bfloat16)],
    )
    after_b = pass_on(later_total, False)
    mixed_in = gather(mixed_parts)
    gq, gv_part, gkf_part = call(
        functools.partial(back_kernel, n),
        [struct((long, dim)), struct((long, dim), f32), struct((long, feats), f32)],
        qkv, om, kf, qf, scores, gn, state, carried, later, flops=8 * macs,
        scratch=[pltpu.VMEM((long, feats), f32)],
    )
    grads = call(
        functools.partial(end_kernel, n),
        [struct((3, rows, dim))] * n,
        qkv, om, kf, gq, gv_part, gkf_part, after_b, flops=3 * macs,
        scratch=[pltpu.VMEM((long, dim), jnp.bfloat16)] * 2,
    )
    grads_in = gather(grads)

    order = [o for o in range(split) if not o & 1] + [o for o in range(split) if o & 1]
    own, sent = call(
        functools.partial(mixed_project_kernel, n, order),
        [struct((split // 2, rows, width))] * 2,
        *mixed_in, out_weight, grads[0], flops=2 * rows * out_weight.size,
        specs=[VMEM] * (n + 1) + [ANY],
        scratch=[pltpu.VMEM((rows, n * dim), jnp.bfloat16)],
    )
    part, last = reduce_blocks(own, sent, bits)
    return call(
        functools.partial(unpack_kernel, n),
        [struct((rows, width))] + [struct((rows, n * dim))] * 3,
        *grads_in, part, last,
    )


def solution(mesh):
    placed = (
        P("seq", "head"),
        P("seq", "head"),
        P("seq", "head"),
        P("head", None, None),
        P("head", None),
        P("seq", "head"),
    )

    def local(queries, key_vectors, value_vectors, feature_proj, out_weight, grad_output):
        paired = mesh.shape["seq"] == 2 * feature_proj.shape[0] and mesh.shape["head"] % 2 == 0
        body = head_per_pair if paired else scanned
        return body(
            queries, key_vectors, value_vectors, feature_proj, out_weight, grad_output
        )

    return jax.shard_map(
        local,
        mesh=mesh,
        in_specs=placed,
        out_specs=(P("seq", "head"),) * 4,
        check_vma=False,
    )
```

```python
import functools

import jax
import jax.numpy as jnp
from jax import lax
from jax.experimental import pallas as pl
from jax.experimental.pallas import tpu as pltpu
from jax.sharding import PartitionSpec as P

EPSILON = 1e-05
VMEM = pl.BlockSpec(memory_space=pltpu.VMEM)
ANY = pl.BlockSpec(memory_space=pl.ANY)
NN = (((1,), (0,)), ((), ()))
NT = (((1,), (1,)), ((), ()))
TN = (((0,), (0,)), ((), ()))


def mm(a, b, dims=NN):
    return lax.dot_general(a, b, dims, preferred_element_type=jnp.float32)


def bf(x):
    return x.astype(jnp.bfloat16)


def call(body, outs, *args, flops=0, specs=None, scratch=(), vmem=32):
    size = sum(a.size * a.dtype.itemsize for a in args)
    size += sum(o.size * o.dtype.itemsize for o in outs)
    return pl.pallas_call(
        body,
        out_shape=outs,
        in_specs=specs or [VMEM] * len(args),
        out_specs=[VMEM] * len(outs),
        scratch_shapes=list(scratch),
        cost_estimate=pl.CostEstimate(flops=flops, bytes_accessed=size, transcendentals=0),
        compiler_params=pltpu.CompilerParams(vmem_limit_bytes=vmem * 1024 * 1024),
    )(*args)


def struct(shape, dtype=jnp.bfloat16):
    return jax.ShapeDtypeStruct(shape, dtype)


def causal_mask(rows):
    row = lax.broadcasted_iota(jnp.int32, (rows, rows), 0)
    col = lax.broadcasted_iota(jnp.int32, (rows, rows), 1)
    return col <= row


def swap(array, axis, bit):
    size = lax.axis_size(axis)
    return lax.ppermute(array, axis, [(i, i ^ bit) for i in range(size)])


def bits_of(size):
    return [1 << b for b in range(size.bit_length() - 1)]


def reduce_blocks(own, sent, bits):
    got = swap(sent, "head", 1)
    for bit in bits[1:]:
        total = own.astype(jnp.float32) + got.astype(jnp.float32)
        pairs = total.reshape((total.shape[0] // 2, 2) + total.shape[1:])
        own, got = pairs[:, 0], swap(bf(pairs[:, 1]), "head", bit)
    return own[0].astype(jnp.float32), got[0]


def member(n):
    return lax.rem(lax.axis_index("seq"), n)


def exchange(parts):
    n, size = len(parts), lax.axis_size("seq")
    return [parts[0]] + [
        lax.ppermute(parts[k], "seq", [(i, i ^ k) for i in range(size)]) for k in range(1, n)
    ]


def from_groups(total, n, forward):
    size, step, exclusive = lax.axis_size("seq"), n, None
    inclusive = total.astype(jnp.float32)
    while step < size:
        pairs = [(i, i + step) for i in range(size - step)]
        if not forward:
            pairs = [(b, a) for a, b in pairs]
        got = lax.ppermute(bf(inclusive), "seq", pairs).astype(jnp.float32)
        exclusive = got if exclusive is None else exclusive + got
        inclusive = inclusive + got
        step *= 2
    return jnp.zeros_like(total) if exclusive is None else bf(exclusive)


def lane(index, width):
    return pl.ds(pl.multiple_of(index * width, 128), width)


def pack_kernel(n, q_ref, k_ref, v_ref, om_ref, go_ref, *rest):
    outs, om_out, go_out, sems = rest[:n], rest[n], rest[n + 1], rest[n + 2]
    r = member(n)
    dim = om_ref.shape[1]
    copies = [(go_ref, go_out)]
    for k in range(n):
        cols = lane(r ^ k, dim)
        for at, ref in enumerate((q_ref, k_ref, v_ref)):
            copies.append((ref.at[:, cols], outs[k].at[at]))
    copies.append((om_ref.at[r], om_out))
    started = [pltpu.make_async_copy(a, b, sems.at[i]) for i, (a, b) in enumerate(copies)]
    for copy in started:
        copy.start()
    for copy in started:
        copy.wait()


def grad_mixed_kernel(n, *refs):
    blocks, w_ref, outs, scr = refs[: -n - 2], refs[-n - 2], refs[-n - 1 : -1], refs[-1]
    r, h = member(n), lax.axis_index("head")
    width = blocks[0].shape[1]
    dim = outs[0].shape[1]
    total = None
    for offset, ref in enumerate(blocks):
        part = mm(ref[...], w_ref[:, lane(h ^ offset, width)], NT)
        total = part if total is None else total + part
    scr[...] = bf(total)
    for k in range(n):
        outs[k][...] = scr[:, lane(r ^ k, dim)]


def first_kernel(n, *refs):
    got, om_ref, (qkv_ref, kf_ref, state_ref, total_ref) = refs[:n], refs[n], refs[n + 2 :]
    r = member(n)
    rows, dim = got[0].shape[1:]
    scale = dim ** (-0.25)
    for k in range(n):
        at = pl.ds(pl.multiple_of((r ^ k) * rows, 128), rows)
        qkv_ref[:, at, :] = got[k][...]
    k_all = qkv_ref[1]
    wide = k_all.astype(jnp.float32)
    half_sq = jnp.sum(wide * wide, axis=1, keepdims=True) * (scale * scale * 0.5)
    kf = bf(jnp.exp(mm(k_all, om_ref[...]) * scale - half_sq))
    kf_ref[...] = kf
    total = jnp.zeros(total_ref.shape, jnp.float32)
    for t in range(n):
        at = pl.ds(t * rows, rows)
        state_ref[t] = bf(total)
        total = total + mm(qkv_ref[2, at, :], kf[t * rows : (t + 1) * rows], TN)
    total_ref[...] = bf(total)


def inner_kernel(n, qkv_ref, om_ref, kf_ref, state_ref, qf_ref, scores_ref, num_ref):
    dim = om_ref.shape[0]
    rows = scores_ref.shape[1]
    scale = dim ** (-0.25)
    causal = causal_mask(rows)
    qf_ref[...] = bf(jnp.exp(mm(qkv_ref[0], om_ref[...]) * scale))
    for t in range(n):
        at = pl.ds(t * rows, rows)
        qf = qf_ref[at, :]
        scores = bf(jnp.where(causal, mm(qf, kf_ref[at, :], NT), 0.0))
        scores_ref[t] = scores
        num_ref[at, :] = mm(scores, qkv_ref[2, at, :]) + mm(qf, state_ref[t], NT)


def turn_kernel(n, *refs):
    gm_in, (qf_ref, num_ref, carried_ref) = refs[:n], refs[n : n + 3]
    gn_ref, state_ref, total_ref = refs[n + 3 : n + 6]
    outs, scr = refs[n + 6 : -1], refs[-1]
    r = member(n)
    rows = gm_in[0].shape[0]
    places = [
        pl.ds(pl.multiple_of((r ^ k) * rows, 128), rows) for k in range(n)
    ]
    for k in range(n):
        scr[places[k], :] = gm_in[k][...]
    num = num_ref[...] + mm(qf_ref[...], carried_ref[...], NT)
    inv = lax.rsqrt(jnp.mean(num * num, axis=1, keepdims=True) + EPSILON)
    normed = num * inv
    gm = scr[...].astype(jnp.float32)
    gn = bf((gm - normed * jnp.mean(gm * normed, axis=1, keepdims=True)) * inv)
    gn_ref[...] = gn
    scr[...] = bf(normed)
    for k in range(n):
        outs[k][...] = scr[places[k], :]
    total = jnp.zeros(total_ref.shape, jnp.float32)
    for t in reversed(range(n)):
        state_ref[t] = bf(total)
        at = pl.ds(t * rows, rows)
        total = total + mm(gn[t * rows : (t + 1) * rows], qf_ref[at, :], TN)
    total_ref[...] = bf(total)


def back_kernel(n, qkv_ref, om_ref, kf_ref, qf_ref, scores_ref, gn_ref, state_ref, carried_ref,
                later_ref, gq_ref, gv_ref, gkf_ref, gqf_scr):
    dim = om_ref.shape[0]
    rows = scores_ref.shape[1]
    scale = dim ** (-0.25)
    causal = causal_mask(rows)
    gqf_scr[...] = mm(gn_ref[...], carried_ref[...])
    for t in range(n):
        at = pl.ds(t * rows, rows)
        qf, kf, gn, v = qf_ref[at, :], kf_ref[at, :], gn_ref[at, :], qkv_ref[2, at, :]
        gs = bf(jnp.where(causal, mm(gn, v, NT), 0.0))
        gqf = gqf_scr[at, :] + mm(gs, kf) + mm(gn, state_ref[t])
        terms = bf(gqf * qf.astype(jnp.float32))
        gq_ref[at, :] = bf(mm(terms, om_ref[...], NT) * scale)
        later = later_ref[t]
        gv_ref[at, :] = mm(scores_ref[t], gn, TN) + mm(kf, later, NT)
        gkf_ref[at, :] = mm(gs, qf, TN) + mm(v, later)


def end_kernel(n, qkv_ref, om_ref, kf_ref, gq_ref, gv_ref, gkf_ref, after_ref, *rest):
    outs, gk_scr, gv_scr = rest[:n], rest[n], rest[n + 1]
    r = member(n)
    dim = om_ref.shape[0]
    rows = outs[0].shape[1]
    scale = dim ** (-0.25)
    kf, after = kf_ref[...], after_ref[...]
    gv_scr[...] = bf(gv_ref[...] + mm(kf, after, NT))
    gkf = gkf_ref[...] + mm(qkv_ref[2], after)
    terms = bf(gkf * kf.astype(jnp.float32))
    total = jnp.sum(terms.astype(jnp.float32), axis=1, keepdims=True)
    wide = qkv_ref[1].astype(jnp.float32)
    gk_scr[...] = bf(mm(terms, om_ref[...], NT) * scale - total * wide * (scale * scale))
    for k in range(n):
        at = pl.ds(pl.multiple_of((r ^ k) * rows, 128), rows)
        outs[k][0] = gq_ref[at, :]
        outs[k][1] = gk_scr[at, :]
        outs[k][2] = gv_scr[at, :]


def mixed_project_kernel(n, offsets, *refs):
    mixed_in, (w_ref, _, own_ref, sent_ref, scr) = refs[:n], refs[n:]
    r, h = member(n), lax.axis_index("head")
    width = own_ref.shape[2]
    dim = mixed_in[0].shape[1]
    half = len(offsets) // 2
    for k in range(n):
        scr[:, lane(r ^ k, dim)] = mixed_in[k][...]
    mixed = scr[...]
    for at, offset in enumerate(offsets):
        part = bf(mm(mixed, w_ref[:, lane(h ^ offset, width)]))
        if at < half:
            own_ref[at] = part
        else:
            sent_ref[at - half] = part


def unpack_kernel(n, *refs):
    got, (part_ref, last_ref), (out_ref, *outs) = refs[:n], refs[n : n + 2], refs[n + 2 :]
    r = member(n)
    dim = got[0].shape[2]
    out_ref[...] = bf(part_ref[...] + last_ref[...].astype(jnp.float32))
    for k in range(n):
        cols = lane(r ^ k, dim)
        for at, out in enumerate(outs):
            out[:, cols] = got[k][at]


def local(queries, key_vectors, value_vectors, feature_proj, out_weight, grad_output):
    n, dim, feats = feature_proj.shape
    rows, width = grad_output.shape
    split = lax.axis_size("head")
    bits = bits_of(split)
    long = n * rows
    macs = long * dim * feats * 2
    f32 = jnp.float32

    *sends, om, go = call(
        functools.partial(pack_kernel, n),
        [struct((3, rows, dim))] * n + [struct((dim, feats)), struct(grad_output.shape)],
        queries, key_vectors, value_vectors, feature_proj, grad_output,
        specs=[ANY] * 5, scratch=[pltpu.SemaphoreType.DMA((3 * n + 2,))], vmem=60,
    )
    blocks = [go] + [swap(go, "head", offset) for offset in range(1, split)]
    got = exchange(sends)
    gm_parts = call(
        functools.partial(grad_mixed_kernel, n),
        [struct((rows, dim))] * n,
        *blocks, out_weight, flops=2 * rows * out_weight.size,
        scratch=[pltpu.VMEM((rows, n * dim), jnp.bfloat16)],
    )
    gm_in = exchange(gm_parts)
    qkv, kf, state, total = call(
        functools.partial(first_kernel, n),
        [
            struct((3, long, dim)),
            struct((long, feats)),
            struct((n, dim, feats)),
            struct((dim, feats)),
        ],
        *got, om, gm_parts[0], flops=2 * macs, specs=[VMEM] * (n + 1) + [ANY],
    )
    carried = from_groups(total, n, True)
    qf, scores, num = call(
        functools.partial(inner_kernel, n),
        [struct((long, feats)), struct((n, rows, rows)), struct((long, dim), f32)],
        qkv, om, kf, state, flops=4 * macs,
    )
    gn, later, later_total, *mixed_parts = call(
        functools.partial(turn_kernel, n),
        [struct((long, dim)), struct((n, dim, feats)), struct((dim, feats))]
        + [struct((rows, dim))] * n,
        *gm_in, qf, num, carried, flops=2 * macs,
        scratch=[pltpu.VMEM((long, dim), jnp.bfloat16)],
    )
    after_b = from_groups(later_total, n, False)
    mixed_in = exchange(mixed_parts)
    gq, gv_part, gkf_part = call(
        functools.partial(back_kernel, n),
        [struct((long, dim)), struct((long, dim), f32), struct((long, feats), f32)],
        qkv, om, kf, qf, scores, gn, state, carried, later, flops=8 * macs,
        scratch=[pltpu.VMEM((long, feats), f32)],
    )
    grads = call(
        functools.partial(end_kernel, n),
        [struct((3, rows, dim))] * n,
        qkv, om, kf, gq, gv_part, gkf_part, after_b, flops=3 * macs,
        scratch=[pltpu.VMEM((long, dim), jnp.bfloat16)] * 2,
    )
    grads_in = exchange(grads)

    order = [o for o in range(split) if not o & 1] + [o for o in range(split) if o & 1]
    own, sent = call(
        functools.partial(mixed_project_kernel, n, order),
        [struct((split // 2, rows, width))] * 2,
        *mixed_in, out_weight, grads[0], flops=2 * rows * out_weight.size,
        specs=[VMEM] * (n + 1) + [ANY],
        scratch=[pltpu.VMEM((rows, n * dim), jnp.bfloat16)],
    )
    part, last = reduce_blocks(own, sent, bits)
    return call(
        functools.partial(unpack_kernel, n),
        [struct((rows, width))] + [struct((rows, n * dim))] * 3,
        *grads_in, part, last,
    )


def solution(mesh):
    placed = (
        P("seq", "head"),
        P("seq", "head"),
        P("seq", "head"),
        P("head", None, None),
        P("head", None),
        P("seq", "head"),
    )
    return jax.shard_map(
        local,
        mesh=mesh,
        in_specs=placed,
        out_specs=(P("seq", "head"),) * 4,
        check_vma=False,
    )
```

```python
import functools

import jax
import jax.numpy as jnp
from jax import lax
from jax.experimental import pallas as pl
from jax.experimental.pallas import tpu as pltpu
from jax.sharding import PartitionSpec as P

EPSILON = 1e-05
VMEM = pl.BlockSpec(memory_space=pltpu.VMEM)
ANY = pl.BlockSpec(memory_space=pl.ANY)
NN = (((1,), (0,)), ((), ()))
NT = (((1,), (1,)), ((), ()))
TN = (((0,), (0,)), ((), ()))


def mm(a, b, dims=NN):
    return lax.dot_general(a, b, dims, preferred_element_type=jnp.float32)


def bf(x):
    return x.astype(jnp.bfloat16)


def call(body, outs, *args, flops=0, specs=None, scratch=(), vmem=32):
    size = sum(a.size * a.dtype.itemsize for a in args)
    size += sum(o.size * o.dtype.itemsize for o in outs)
    return pl.pallas_call(
        body,
        out_shape=outs,
        in_specs=specs or [VMEM] * len(args),
        out_specs=[VMEM] * len(outs),
        scratch_shapes=list(scratch),
        cost_estimate=pl.CostEstimate(flops=flops, bytes_accessed=size, transcendentals=0),
        compiler_params=pltpu.CompilerParams(vmem_limit_bytes=vmem * 1024 * 1024),
    )(*args)


def struct(shape, dtype=jnp.bfloat16):
    return jax.ShapeDtypeStruct(shape, dtype)


def causal_mask(rows):
    row = lax.broadcasted_iota(jnp.int32, (rows, rows), 0)
    col = lax.broadcasted_iota(jnp.int32, (rows, rows), 1)
    return col <= row


def swap(array, axis, bit):
    size = lax.axis_size(axis)
    return lax.ppermute(array, axis, [(i, i ^ bit) for i in range(size)])


def bits_of(size):
    return [1 << b for b in range(size.bit_length() - 1)]


def reduce_blocks(own, sent, bits):
    got = swap(sent, "head", 1)
    for bit in bits[1:]:
        total = own.astype(jnp.float32) + got.astype(jnp.float32)
        pairs = total.reshape((total.shape[0] // 2, 2) + total.shape[1:])
        own, got = pairs[:, 0], swap(bf(pairs[:, 1]), "head", bit)
    return own[0].astype(jnp.float32), got[0]


def member(n):
    return lax.rem(lax.axis_index("seq"), n)


def exchange(parts):
    n, size = len(parts), lax.axis_size("seq")
    got = [
        lax.ppermute(parts[k], "seq", [(i, i ^ k) for i in range(size)])
        for k in reversed(range(1, n))
    ]
    return [parts[0]] + got[::-1]


def from_groups(total, n, forward):
    size, step, exclusive = lax.axis_size("seq"), n, None
    inclusive = total.astype(jnp.float32)
    while step < size:
        pairs = [(i, i + step) for i in range(size - step)]
        if not forward:
            pairs = [(b, a) for a, b in pairs]
        got = lax.ppermute(bf(inclusive), "seq", pairs).astype(jnp.float32)
        exclusive = got if exclusive is None else exclusive + got
        inclusive = inclusive + got
        step *= 2
    return jnp.zeros_like(total) if exclusive is None else bf(exclusive)


def lane(index, width):
    return pl.ds(pl.multiple_of(index * width, 128), width)


def pack_kernel(n, q_ref, k_ref, v_ref, om_ref, go_ref, *rest):
    outs, om_out, go_out, sems = rest[:n], rest[n], rest[n + 1], rest[n + 2]
    r = member(n)
    dim = om_ref.shape[1]
    copies = [(go_ref, go_out)]
    for k in range(n):
        cols = lane(r ^ k, dim)
        for at, ref in enumerate((q_ref, k_ref, v_ref)):
            copies.append((ref.at[:, cols], outs[k].at[at]))
    copies.append((om_ref.at[r], om_out))
    started = [pltpu.make_async_copy(a, b, sems.at[i]) for i, (a, b) in enumerate(copies)]
    for copy in started:
        copy.start()
    for copy in started:
        copy.wait()


def mark_kernel(_, out_ref):
    out_ref[...] = jnp.zeros(out_ref.shape, out_ref.dtype)


def grad_mixed_kernel(n, *refs):
    blocks, w_ref, outs, scr = refs[: -n - 3], refs[-n - 3], refs[-n - 1 : -1], refs[-1]
    r, h = member(n), lax.axis_index("head")
    width = blocks[0].shape[1]
    dim = outs[0].shape[1]
    total = None
    for offset, ref in enumerate(blocks):
        part = mm(ref[...], w_ref[:, lane(h ^ offset, width)], NT)
        total = part if total is None else total + part
    scr[...] = bf(total)
    for k in range(n):
        outs[k][...] = scr[:, lane(r ^ k, dim)]


def first_kernel(n, *refs):
    got, om_ref, (qkv_ref, kf_ref, state_ref, total_ref) = refs[:n], refs[n], refs[n + 2 :]
    r = member(n)
    rows, dim = got[0].shape[1:]
    scale = dim ** (-0.25)
    for k in range(n):
        at = pl.ds(pl.multiple_of((r ^ k) * rows, 128), rows)
        qkv_ref[:, at, :] = got[k][...]
    k_all = qkv_ref[1]
    wide = k_all.astype(jnp.float32)
    half_sq = jnp.sum(wide * wide, axis=1, keepdims=True) * (scale * scale * 0.5)
    kf = bf(jnp.exp(mm(k_all, om_ref[...]) * scale - half_sq))
    kf_ref[...] = kf
    total = jnp.zeros(total_ref.shape, jnp.float32)
    for t in range(n):
        at = pl.ds(t * rows, rows)
        state_ref[t] = bf(total)
        total = total + mm(qkv_ref[2, at, :], kf[t * rows : (t + 1) * rows], TN)
    total_ref[...] = bf(total)


def inner_kernel(n, qkv_ref, om_ref, kf_ref, state_ref, qf_ref, scores_ref, num_ref):
    dim = om_ref.shape[0]
    rows = scores_ref.shape[1]
    scale = dim ** (-0.25)
    causal = causal_mask(rows)
    qf_ref[...] = bf(jnp.exp(mm(qkv_ref[0], om_ref[...]) * scale))
    for t in range(n):
        at = pl.ds(t * rows, rows)
        qf = qf_ref[at, :]
        scores = bf(jnp.where(causal, mm(qf, kf_ref[at, :], NT), 0.0))
        scores_ref[t] = scores
        num_ref[at, :] = mm(scores, qkv_ref[2, at, :]) + mm(qf, state_ref[t], NT)


def turn_kernel(n, *refs):
    gm_in, (qf_ref, num_ref, carried_ref) = refs[:n], refs[n : n + 3]
    gn_ref, state_ref, total_ref = refs[n + 3 : n + 6]
    outs, scr = refs[n + 6 : -1], refs[-1]
    r = member(n)
    rows = gm_in[0].shape[0]
    places = [
        pl.ds(pl.multiple_of((r ^ k) * rows, 128), rows) for k in range(n)
    ]
    for k in range(n):
        scr[places[k], :] = gm_in[k][...]
    num = num_ref[...] + mm(qf_ref[...], carried_ref[...], NT)
    inv = lax.rsqrt(jnp.mean(num * num, axis=1, keepdims=True) + EPSILON)
    normed = num * inv
    gm = scr[...].astype(jnp.float32)
    gn = bf((gm - normed * jnp.mean(gm * normed, axis=1, keepdims=True)) * inv)
    gn_ref[...] = gn
    scr[...] = bf(normed)
    for k in range(n):
        outs[k][...] = scr[places[k], :]
    total = jnp.zeros(total_ref.shape, jnp.float32)
    for t in reversed(range(n)):
        state_ref[t] = bf(total)
        at = pl.ds(t * rows, rows)
        total = total + mm(gn[t * rows : (t + 1) * rows], qf_ref[at, :], TN)
    total_ref[...] = bf(total)


def back_kernel(n, qkv_ref, om_ref, kf_ref, qf_ref, scores_ref, gn_ref, state_ref, carried_ref,
                later_ref, gq_ref, gv_ref, gkf_ref, gqf_scr):
    dim = om_ref.shape[0]
    rows = scores_ref.shape[1]
    scale = dim ** (-0.25)
    causal = causal_mask(rows)
    gqf_scr[...] = mm(gn_ref[...], carried_ref[...])
    for t in range(n):
        at = pl.ds(t * rows, rows)
        qf, kf, gn, v = qf_ref[at, :], kf_ref[at, :], gn_ref[at, :], qkv_ref[2, at, :]
        gs = bf(jnp.where(causal, mm(gn, v, NT), 0.0))
        gqf = gqf_scr[at, :] + mm(gs, kf) + mm(gn, state_ref[t])
        terms = bf(gqf * qf.astype(jnp.float32))
        gq_ref[at, :] = bf(mm(terms, om_ref[...], NT) * scale)
        later = later_ref[t]
        gv_ref[at, :] = mm(scores_ref[t], gn, TN) + mm(kf, later, NT)
        gkf_ref[at, :] = mm(gs, qf, TN) + mm(v, later)


def end_kernel(n, qkv_ref, om_ref, kf_ref, gq_ref, gv_ref, gkf_ref, after_ref, *rest):
    outs, gk_scr, gv_scr = rest[:n], rest[n], rest[n + 1]
    r = member(n)
    dim = om_ref.shape[0]
    rows = outs[0].shape[1]
    scale = dim ** (-0.25)
    kf, after = kf_ref[...], after_ref[...]
    gv_scr[...] = bf(gv_ref[...] + mm(kf, after, NT))
    gkf = gkf_ref[...] + mm(qkv_ref[2], after)
    terms = bf(gkf * kf.astype(jnp.float32))
    total = jnp.sum(terms.astype(jnp.float32), axis=1, keepdims=True)
    wide = qkv_ref[1].astype(jnp.float32)
    gk_scr[...] = bf(mm(terms, om_ref[...], NT) * scale - total * wide * (scale * scale))
    for k in range(n):
        at = pl.ds(pl.multiple_of((r ^ k) * rows, 128), rows)
        outs[k][0] = gq_ref[at, :]
        outs[k][1] = gk_scr[at, :]
        outs[k][2] = gv_scr[at, :]


def mixed_project_kernel(n, offsets, *refs):
    mixed_in, (w_ref, _, own_ref, sent_ref, scr) = refs[:n], refs[n:]
    r, h = member(n), lax.axis_index("head")
    width = own_ref.shape[2]
    dim = mixed_in[0].shape[1]
    half = len(offsets) // 2
    for k in range(n):
        scr[:, lane(r ^ k, dim)] = mixed_in[k][...]
    mixed = scr[...]
    for at, offset in enumerate(offsets):
        part = bf(mm(mixed, w_ref[:, lane(h ^ offset, width)]))
        if at < half:
            own_ref[at] = part
        else:
            sent_ref[at - half] = part


def unpack_kernel(n, *refs):
    got, (part_ref, last_ref), (out_ref, *outs) = refs[:n], refs[n : n + 2], refs[n + 2 :]
    r = member(n)
    dim = got[0].shape[2]
    out_ref[...] = bf(part_ref[...] + last_ref[...].astype(jnp.float32))
    for k in range(n):
        cols = lane(r ^ k, dim)
        for at, out in enumerate(outs):
            out[:, cols] = got[k][at]


def local(queries, key_vectors, value_vectors, feature_proj, out_weight, grad_output):
    n, dim, feats = feature_proj.shape
    rows, width = grad_output.shape
    split = lax.axis_size("head")
    bits = bits_of(split)
    long = n * rows
    macs = long * dim * feats * 2
    f32 = jnp.float32

    *sends, om, go = call(
        functools.partial(pack_kernel, n),
        [struct((3, rows, dim))] * n + [struct((dim, feats)), struct(grad_output.shape)],
        queries, key_vectors, value_vectors, feature_proj, grad_output,
        specs=[ANY] * 5, scratch=[pltpu.SemaphoreType.DMA((3 * n + 2,))], vmem=60,
    )
    blocks = [go] + [swap(go, "head", offset) for offset in range(1, split)]
    got = exchange(sends)
    (mark,) = call(mark_kernel, [struct((8, 128), f32)], om, specs=[ANY], flops=10**10)
    gm_parts = call(
        functools.partial(grad_mixed_kernel, n),
        [struct((rows, dim))] * n,
        *blocks, out_weight, mark, flops=2 * rows * out_weight.size,
        specs=[VMEM] * (split + 1) + [ANY],
        scratch=[pltpu.VMEM((rows, n * dim), jnp.bfloat16)],
    )
    gm_in = exchange(gm_parts)
    qkv, kf, state, total = call(
        functools.partial(first_kernel, n),
        [
            struct((3, long, dim)),
            struct((long, feats)),
            struct((n, dim, feats)),
            struct((dim, feats)),
        ],
        *got, om, gm_parts[0], flops=2 * macs, specs=[VMEM] * (n + 1) + [ANY],
    )
    carried = from_groups(total, n, True)
    qf, scores, num = call(
        functools.partial(inner_kernel, n),
        [struct((long, feats)), struct((n, rows, rows)), struct((long, dim), f32)],
        qkv, om, kf, state, flops=4 * macs,
    )
    gn, later, later_total, *mixed_parts = call(
        functools.partial(turn_kernel, n),
        [struct((long, dim)), struct((n, dim, feats)), struct((dim, feats))]
        + [struct((rows, dim))] * n,
        *gm_in, qf, num, carried, flops=2 * macs,
        scratch=[pltpu.VMEM((long, dim), jnp.bfloat16)],
    )
    after_b = from_groups(later_total, n, False)
    mixed_in = exchange(mixed_parts)
    gq, gv_part, gkf_part = call(
        functools.partial(back_kernel, n),
        [struct((long, dim)), struct((long, dim), f32), struct((long, feats), f32)],
        qkv, om, kf, qf, scores, gn, state, carried, later, flops=8 * macs,
        scratch=[pltpu.VMEM((long, feats), f32)],
    )
    grads = call(
        functools.partial(end_kernel, n),
        [struct((3, rows, dim))] * n,
        qkv, om, kf, gq, gv_part, gkf_part, after_b, flops=3 * macs,
        scratch=[pltpu.VMEM((long, dim), jnp.bfloat16)] * 2,
    )
    grads_in = exchange(grads)

    order = [o for o in range(split) if not o & 1] + [o for o in range(split) if o & 1]
    own, sent = call(
        functools.partial(mixed_project_kernel, n, order),
        [struct((split // 2, rows, width))] * 2,
        *mixed_in, out_weight, grads[0], flops=2 * rows * out_weight.size,
        specs=[VMEM] * (n + 1) + [ANY],
        scratch=[pltpu.VMEM((rows, n * dim), jnp.bfloat16)],
    )
    part, last = reduce_blocks(own, sent, bits)
    return call(
        functools.partial(unpack_kernel, n),
        [struct((rows, width))] + [struct((rows, n * dim))] * 3,
        *grads_in, part, last,
    )


def solution(mesh):
    placed = (
        P("seq", "head"),
        P("seq", "head"),
        P("seq", "head"),
        P("head", None, None),
        P("head", None),
        P("seq", "head"),
    )
    return jax.shard_map(
        local,
        mesh=mesh,
        in_specs=placed,
        out_specs=(P("seq", "head"),) * 4,
        check_vma=False,
    )
```

```python
import functools

import jax
import jax.numpy as jnp
from jax import lax
from jax.experimental import pallas as pl
from jax.experimental.pallas import tpu as pltpu
from jax.sharding import PartitionSpec as P

EPSILON = 1e-05
VMEM = pl.BlockSpec(memory_space=pltpu.VMEM)
ANY = pl.BlockSpec(memory_space=pl.ANY)
NN = (((1,), (0,)), ((), ()))
NT = (((1,), (1,)), ((), ()))
TN = (((0,), (0,)), ((), ()))


def mm(a, b, dims=NN):
    return lax.dot_general(a, b, dims, preferred_element_type=jnp.float32)


def bf(x):
    return x.astype(jnp.bfloat16)


def call(body, outs, *args, flops=0, specs=None, scratch=(), vmem=32):
    size = sum(a.size * a.dtype.itemsize for a in args)
    size += sum(o.size * o.dtype.itemsize for o in outs)
    return pl.pallas_call(
        body,
        out_shape=outs,
        in_specs=specs or [VMEM] * len(args),
        out_specs=[VMEM] * len(outs),
        scratch_shapes=list(scratch),
        cost_estimate=pl.CostEstimate(flops=flops, bytes_accessed=size, transcendentals=0),
        compiler_params=pltpu.CompilerParams(vmem_limit_bytes=vmem * 1024 * 1024),
    )(*args)


def struct(shape, dtype=jnp.bfloat16):
    return jax.ShapeDtypeStruct(shape, dtype)


def causal_mask(rows):
    row = lax.broadcasted_iota(jnp.int32, (rows, rows), 0)
    col = lax.broadcasted_iota(jnp.int32, (rows, rows), 1)
    return col <= row


def swap(array, axis, bit):
    size = lax.axis_size(axis)
    return lax.ppermute(array, axis, [(i, i ^ bit) for i in range(size)])


def bits_of(size):
    return [1 << b for b in range(size.bit_length() - 1)]


def reduce_blocks(own, sent, bits):
    got = swap(sent, "head", 1)
    for bit in bits[1:]:
        total = own.astype(jnp.float32) + got.astype(jnp.float32)
        pairs = total.reshape((total.shape[0] // 2, 2) + total.shape[1:])
        own, got = pairs[:, 0], swap(bf(pairs[:, 1]), "head", bit)
    return own[0].astype(jnp.float32), got[0]


def member(n):
    return lax.rem(lax.axis_index("seq"), n)


def exchange(parts):
    n, size = len(parts), lax.axis_size("seq")
    return [
        lax.ppermute(parts[k], "seq", [(i, i ^ k) for i in range(size)])
        for k in reversed(range(1, n))
    ] + [parts[0]]


def from_groups(total, n, forward):
    size, step, exclusive = lax.axis_size("seq"), n, None
    inclusive = total.astype(jnp.float32)
    while step < size:
        pairs = [(i, i + step) for i in range(size - step)]
        if not forward:
            pairs = [(b, a) for a, b in pairs]
        got = lax.ppermute(bf(inclusive), "seq", pairs).astype(jnp.float32)
        exclusive = got if exclusive is None else exclusive + got
        inclusive = inclusive + got
        step *= 2
    return jnp.zeros_like(total) if exclusive is None else bf(exclusive)


def lane(index, width):
    return pl.ds(pl.multiple_of(index * width, 128), width)


def pack_kernel(n, q_ref, k_ref, v_ref, *rest):
    outs, sems = rest[:n], rest[n]
    r = member(n)
    dim = outs[0].shape[2]
    copies = []
    for k in range(n):
        cols = lane(r ^ k, dim)
        for at, ref in enumerate((q_ref, k_ref, v_ref)):
            copies.append((ref.at[:, cols], outs[k].at[at]))
    started = [pltpu.make_async_copy(a, b, sems.at[i]) for i, (a, b) in enumerate(copies)]
    for copy in started:
        copy.start()
    for copy in started:
        copy.wait()


def mark_kernel(_, out_ref):
    out_ref[...] = jnp.zeros(out_ref.shape, out_ref.dtype)


def grad_mixed_kernel(n, offsets, *refs):
    blocks, w_ref, outs, scr = refs[: -n - 3], refs[-n - 3], refs[-n - 1 : -1], refs[-1]
    r, h = member(n), lax.axis_index("head")
    width = blocks[0].shape[1]
    dim = outs[0].shape[1]
    total = None
    for offset, ref in zip(offsets, blocks):
        part = mm(ref[...], w_ref[:, lane(h ^ offset, width)], NT)
        total = part if total is None else total + part
    scr[...] = bf(total)
    for k in range(n):
        outs[k][...] = scr[:, lane(r ^ k, dim)]


def first_kernel(n, *refs):
    got, om_ref = refs[:n][::-1], refs[n]
    qkv_ref, kf_ref, state_ref, total_ref = refs[n + 2 :]
    r = member(n)
    rows, dim = got[0].shape[1:]
    scale = dim ** (-0.25)
    for k in range(n):
        at = pl.ds(pl.multiple_of((r ^ k) * rows, 128), rows)
        qkv_ref[:, at, :] = got[k][...]
    k_all = qkv_ref[1]
    wide = k_all.astype(jnp.float32)
    half_sq = jnp.sum(wide * wide, axis=1, keepdims=True) * (scale * scale * 0.5)
    kf = bf(jnp.exp(mm(k_all, om_ref[r]) * scale - half_sq))
    kf_ref[...] = kf
    total = jnp.zeros(total_ref.shape, jnp.float32)
    for t in range(n):
        at = pl.ds(t * rows, rows)
        state_ref[t] = bf(total)
        total = total + mm(qkv_ref[2, at, :], kf[t * rows : (t + 1) * rows], TN)
    total_ref[...] = bf(total)


def inner_kernel(n, qkv_ref, om_ref, kf_ref, state_ref, qf_ref, scores_ref, num_ref):
    r, dim = member(n), om_ref.shape[1]
    rows = scores_ref.shape[1]
    scale = dim ** (-0.25)
    causal = causal_mask(rows)
    qf_ref[...] = bf(jnp.exp(mm(qkv_ref[0], om_ref[r]) * scale))
    for t in range(n):
        at = pl.ds(t * rows, rows)
        qf = qf_ref[at, :]
        scores = bf(jnp.where(causal, mm(qf, kf_ref[at, :], NT), 0.0))
        scores_ref[t] = scores
        num_ref[at, :] = mm(scores, qkv_ref[2, at, :]) + mm(qf, state_ref[t], NT)


def turn_kernel(n, *refs):
    gm_in, (qf_ref, num_ref, carried_ref) = refs[:n][::-1], refs[n : n + 3]
    gn_ref, state_ref, total_ref = refs[n + 3 : n + 6]
    outs, scr = refs[n + 6 : -1], refs[-1]
    r = member(n)
    rows = gm_in[0].shape[0]
    places = [
        pl.ds(pl.multiple_of((r ^ k) * rows, 128), rows) for k in range(n)
    ]
    for k in range(n):
        scr[places[k], :] = gm_in[k][...]
    num = num_ref[...] + mm(qf_ref[...], carried_ref[...], NT)
    inv = lax.rsqrt(jnp.mean(num * num, axis=1, keepdims=True) + EPSILON)
    normed = num * inv
    gm = scr[...].astype(jnp.float32)
    gn = bf((gm - normed * jnp.mean(gm * normed, axis=1, keepdims=True)) * inv)
    gn_ref[...] = gn
    scr[...] = bf(normed)
    for k in range(n):
        outs[k][...] = scr[places[k], :]
    total = jnp.zeros(total_ref.shape, jnp.float32)
    for t in reversed(range(n)):
        state_ref[t] = bf(total)
        at = pl.ds(t * rows, rows)
        total = total + mm(gn[t * rows : (t + 1) * rows], qf_ref[at, :], TN)
    total_ref[...] = bf(total)


def back_kernel(n, qkv_ref, om_ref, kf_ref, qf_ref, scores_ref, gn_ref, state_ref, carried_ref,
                later_ref, gq_ref, gv_ref, gkf_ref, gqf_scr):
    r, dim = member(n), om_ref.shape[1]
    rows = scores_ref.shape[1]
    scale = dim ** (-0.25)
    causal = causal_mask(rows)
    gqf_scr[...] = mm(gn_ref[...], carried_ref[...])
    for t in range(n):
        at = pl.ds(t * rows, rows)
        qf, kf, gn, v = qf_ref[at, :], kf_ref[at, :], gn_ref[at, :], qkv_ref[2, at, :]
        gs = bf(jnp.where(causal, mm(gn, v, NT), 0.0))
        gqf = gqf_scr[at, :] + mm(gs, kf) + mm(gn, state_ref[t])
        terms = bf(gqf * qf.astype(jnp.float32))
        gq_ref[at, :] = bf(mm(terms, om_ref[r], NT) * scale)
        later = later_ref[t]
        gv_ref[at, :] = mm(scores_ref[t], gn, TN) + mm(kf, later, NT)
        gkf_ref[at, :] = mm(gs, qf, TN) + mm(v, later)


def end_kernel(n, qkv_ref, om_ref, kf_ref, gq_ref, gv_ref, gkf_ref, after_ref, *rest):
    outs, gk_scr, gv_scr = rest[:n], rest[n], rest[n + 1]
    r, dim = member(n), om_ref.shape[1]
    rows = outs[0].shape[1]
    scale = dim ** (-0.25)
    kf, after = kf_ref[...], after_ref[...]
    gv_scr[...] = bf(gv_ref[...] + mm(kf, after, NT))
    gkf = gkf_ref[...] + mm(qkv_ref[2], after)
    terms = bf(gkf * kf.astype(jnp.float32))
    total = jnp.sum(terms.astype(jnp.float32), axis=1, keepdims=True)
    wide = qkv_ref[1].astype(jnp.float32)
    gk_scr[...] = bf(mm(terms, om_ref[r], NT) * scale - total * wide * (scale * scale))
    for k in range(n):
        at = pl.ds(pl.multiple_of((r ^ k) * rows, 128), rows)
        outs[k][0] = gq_ref[at, :]
        outs[k][1] = gk_scr[at, :]
        outs[k][2] = gv_scr[at, :]


def mixed_project_kernel(n, offsets, *refs):
    mixed_in, (w_ref, _, own_ref, sent_ref, scr) = refs[:n][::-1], refs[n:]
    r, h = member(n), lax.axis_index("head")
    width = own_ref.shape[2]
    dim = mixed_in[0].shape[1]
    half = len(offsets) // 2
    for k in range(n):
        scr[:, lane(r ^ k, dim)] = mixed_in[k][...]
    mixed = scr[...]
    for at, offset in enumerate(offsets):
        part = bf(mm(mixed, w_ref[:, lane(h ^ offset, width)]))
        if at < half:
            own_ref[at] = part
        else:
            sent_ref[at - half] = part


def unpack_kernel(n, *refs):
    got, (part_ref, last_ref) = refs[:n][::-1], refs[n : n + 2]
    out_ref, *outs = refs[n + 2 :]
    r = member(n)
    dim = got[0].shape[2]
    out_ref[...] = bf(part_ref[...] + last_ref[...].astype(jnp.float32))
    for k in range(n):
        cols = lane(r ^ k, dim)
        for at, out in enumerate(outs):
            out[:, cols] = got[k][at]


def local(queries, key_vectors, value_vectors, feature_proj, out_weight, grad_output):
    n, dim, feats = feature_proj.shape
    rows, width = grad_output.shape
    split = lax.axis_size("head")
    bits = bits_of(split)
    long = n * rows
    macs = long * dim * feats * 2
    f32 = jnp.float32

    offsets, blocks = [0], [grad_output]
    for bit in reversed(bits):
        blocks = blocks + [swap(b, "head", bit) for b in blocks]
        offsets = offsets + [o ^ bit for o in offsets]
    sends = call(
        functools.partial(pack_kernel, n),
        [struct((3, rows, dim))] * n,
        queries, key_vectors, value_vectors,
        specs=[ANY] * 3, scratch=[pltpu.SemaphoreType.DMA((3 * n,))], vmem=60,
    )
    got = exchange(sends)
    (mark,) = call(mark_kernel, [struct((8, 128), f32)], blocks[offsets.index(1)], specs=[ANY], flops=10**10)
    gm_parts = call(
        functools.partial(grad_mixed_kernel, n, offsets),
        [struct((rows, dim))] * n,
        *blocks, out_weight, mark, flops=2 * rows * out_weight.size,
        specs=[VMEM] * (split + 1) + [ANY],
        scratch=[pltpu.VMEM((rows, n * dim), jnp.bfloat16)],
    )
    gm_in = exchange(gm_parts)
    qkv, kf, state, total = call(
        functools.partial(first_kernel, n),
        [
            struct((3, long, dim)),
            struct((long, feats)),
            struct((n, dim, feats)),
            struct((dim, feats)),
        ],
        *got, feature_proj, gm_parts[0], flops=2 * macs, specs=[VMEM] * (n + 1) + [ANY],
    )
    carried = from_groups(total, n, True)
    qf, scores, num = call(
        functools.partial(inner_kernel, n),
        [struct((long, feats)), struct((n, rows, rows)), struct((long, dim), f32)],
        qkv, feature_proj, kf, state, flops=4 * macs,
    )
    gn, later, later_total, *mixed_parts = call(
        functools.partial(turn_kernel, n),
        [struct((long, dim)), struct((n, dim, feats)), struct((dim, feats))]
        + [struct((rows, dim))] * n,
        *gm_in, qf, num, carried, flops=2 * macs,
        scratch=[pltpu.VMEM((long, dim), jnp.bfloat16)],
    )
    after_b = from_groups(later_total, n, False)
    mixed_in = exchange(mixed_parts)
    gq, gv_part, gkf_part = call(
        functools.partial(back_kernel, n),
        [struct((long, dim)), struct((long, dim), f32), struct((long, feats), f32)],
        qkv, feature_proj, kf, qf, scores, gn, state, carried, later, flops=8 * macs,
        scratch=[pltpu.VMEM((long, feats), f32)],
    )
    grads = call(
        functools.partial(end_kernel, n),
        [struct((3, rows, dim))] * n,
        qkv, feature_proj, kf, gq, gv_part, gkf_part, after_b, flops=3 * macs,
        scratch=[pltpu.VMEM((long, dim), jnp.bfloat16)] * 2,
    )
    grads_in = exchange(grads)

    order = [o for o in range(split) if not o & 1] + [o for o in range(split) if o & 1]
    own, sent = call(
        functools.partial(mixed_project_kernel, n, order),
        [struct((split // 2, rows, width))] * 2,
        *mixed_in, out_weight, grads[0], flops=2 * rows * out_weight.size,
        specs=[VMEM] * (n + 1) + [ANY],
        scratch=[pltpu.VMEM((rows, n * dim), jnp.bfloat16)],
    )
    part, last = reduce_blocks(own, sent, bits)
    return call(
        functools.partial(unpack_kernel, n),
        [struct((rows, width))] + [struct((rows, n * dim))] * 3,
        *grads_in, part, last,
    )


def solution(mesh):
    placed = (
        P("seq", "head"),
        P("seq", "head"),
        P("seq", "head"),
        P("head", None, None),
        P("head", None),
        P("seq", "head"),
    )
    return jax.shard_map(
        local,
        mesh=mesh,
        in_specs=placed,
        out_specs=(P("seq", "head"),) * 4,
        check_vma=False,
    )
```

```python
import functools

import jax
import jax.numpy as jnp
from jax import lax
from jax.experimental import pallas as pl
from jax.experimental.pallas import tpu as pltpu
from jax.sharding import PartitionSpec as P

EPSILON = 1e-05
VMEM = pl.BlockSpec(memory_space=pltpu.VMEM)
ANY = pl.BlockSpec(memory_space=pl.ANY)
NN = (((1,), (0,)), ((), ()))
NT = (((1,), (1,)), ((), ()))
TN = (((0,), (0,)), ((), ()))


def mm(a, b, dims=NN):
    return lax.dot_general(a, b, dims, preferred_element_type=jnp.float32)


def bf(x):
    return x.astype(jnp.bfloat16)


def call(body, outs, *args, flops=0, specs=None, scratch=(), vmem=32):
    size = sum(a.size * a.dtype.itemsize for a in args)
    size += sum(o.size * o.dtype.itemsize for o in outs)
    return pl.pallas_call(
        body,
        out_shape=outs,
        in_specs=specs or [VMEM] * len(args),
        out_specs=[VMEM] * len(outs),
        scratch_shapes=list(scratch),
        cost_estimate=pl.CostEstimate(flops=flops, bytes_accessed=size, transcendentals=0),
        compiler_params=pltpu.CompilerParams(vmem_limit_bytes=vmem * 1024 * 1024),
    )(*args)


def struct(shape, dtype=jnp.bfloat16):
    return jax.ShapeDtypeStruct(shape, dtype)


def causal_mask(rows):
    row = lax.broadcasted_iota(jnp.int32, (rows, rows), 0)
    col = lax.broadcasted_iota(jnp.int32, (rows, rows), 1)
    return col <= row


def swap(array, axis, bit):
    size = lax.axis_size(axis)
    return lax.ppermute(array, axis, [(i, i ^ bit) for i in range(size)])


def bits_of(size):
    return [1 << b for b in range(size.bit_length() - 1)]


def reduce_blocks(own, sent, bits):
    got = swap(sent, "head", 1)
    for bit in bits[1:]:
        total = own.astype(jnp.float32) + got.astype(jnp.float32)
        pairs = total.reshape((total.shape[0] // 2, 2) + total.shape[1:])
        own, got = pairs[:, 0], swap(bf(pairs[:, 1]), "head", bit)
    return own[0].astype(jnp.float32), got[0]


def member(n):
    return lax.rem(lax.axis_index("seq"), n)


def exchange(parts):
    return [swap(part, "seq", k) for k, part in enumerate(parts, 1)][::-1]


def swap_totals(total, n):
    size, step, got = lax.axis_size("seq"), n, []
    while step < size:
        got.append(swap(bf(total), "seq", step))
        total = total.astype(jnp.float32) + got[-1].astype(jnp.float32)
        step *= 2
    return got


def sum_of_side(refs, n, earlier):
    group = lax.div(lax.axis_index("seq"), n)
    total = jnp.zeros(refs[0].shape, jnp.float32)
    for at, ref in enumerate(refs):
        from_earlier = lax.rem(lax.shift_right_logical(group, at), 2) == 1
        keep = from_earlier if earlier else jnp.logical_not(from_earlier)
        total = total + jnp.where(keep, ref[...].astype(jnp.float32), 0.0)
    return bf(total)


def lane(index, width):
    return pl.ds(pl.multiple_of(index * width, 128), width)


def pack_kernel(n, q_ref, k_ref, v_ref, *rest):
    outs, sems = rest[:-1], rest[-1]
    r = member(n)
    dim = outs[0].shape[2]
    copies = []
    for k, out in enumerate(outs, 1):
        for at, ref in enumerate((q_ref, k_ref, v_ref)):
            copies.append((ref.at[:, lane(r ^ k, dim)], out.at[at]))
    started = [pltpu.make_async_copy(a, b, sems.at[i]) for i, (a, b) in enumerate(copies)]
    for copy in started:
        copy.start()
    for copy in started:
        copy.wait()


def mark_kernel(_, out_ref):
    out_ref[...] = jnp.zeros(out_ref.shape, out_ref.dtype)


def grad_mixed_kernel(n, offsets, *refs):
    blocks, w_ref, outs, scr = refs[: -n - 3], refs[-n - 3], refs[-n - 1 : -1], refs[-1]
    r, h = member(n), lax.axis_index("head")
    width = blocks[0].shape[1]
    dim = outs[0].shape[1]
    total = None
    for offset, ref in zip(offsets, blocks):
        part = mm(ref[...], w_ref[:, lane(h ^ offset, width)], NT)
        total = part if total is None else total + part
    scr[...] = bf(total)
    for k in range(n):
        outs[k][...] = scr[:, lane(r ^ k, dim)]


def first_kernel(n, *refs):
    got, own, om_ref = refs[: n - 1][::-1], refs[n - 1 : n + 2], refs[n + 2]
    qkv_ref, kf_ref, state_ref, total_ref = refs[n + 4 :]
    r = member(n)
    rows, dim = own[0].shape[0], om_ref.shape[1]
    scale = dim ** (-0.25)
    for k in range(n):
        at = pl.ds(pl.multiple_of((r ^ k) * rows, 128), rows)
        if k:
            qkv_ref[:, at, :] = got[k - 1][...]
        else:
            for i, ref in enumerate(own):
                qkv_ref[i, at, :] = ref[:, lane(r, dim)]
    k_all = qkv_ref[1]
    wide = k_all.astype(jnp.float32)
    half_sq = jnp.sum(wide * wide, axis=1, keepdims=True) * (scale * scale * 0.5)
    kf = bf(jnp.exp(mm(k_all, om_ref[r]) * scale - half_sq))
    kf_ref[...] = kf
    total = jnp.zeros(total_ref.shape, jnp.float32)
    for t in range(n):
        at = pl.ds(t * rows, rows)
        state_ref[t] = bf(total)
        total = total + mm(qkv_ref[2, at, :], kf[t * rows : (t + 1) * rows], TN)
    total_ref[...] = bf(total)


def inner_kernel(n, qkv_ref, om_ref, kf_ref, state_ref, qf_ref, scores_ref, num_ref):
    r, dim = member(n), om_ref.shape[1]
    rows = scores_ref.shape[1]
    scale = dim ** (-0.25)
    causal = causal_mask(rows)
    qf_ref[...] = bf(jnp.exp(mm(qkv_ref[0], om_ref[r]) * scale))
    for t in range(n):
        at = pl.ds(t * rows, rows)
        qf = qf_ref[at, :]
        scores = bf(jnp.where(causal, mm(qf, kf_ref[at, :], NT), 0.0))
        scores_ref[t] = scores
        num_ref[at, :] = mm(scores, qkv_ref[2, at, :]) + mm(qf, state_ref[t], NT)


def turn_kernel(n, *refs):
    gm_in, (qf_ref, num_ref), earlier = refs[:n][::-1], refs[n : n + 2], refs[n + 2 : -n - 5]
    carried_ref, gn_ref, state_ref, total_ref = refs[-n - 5 : -n - 1]
    outs, scr = refs[-n - 1 : -1], refs[-1]
    r = member(n)
    rows = gm_in[0].shape[0]
    places = [
        pl.ds(pl.multiple_of((r ^ k) * rows, 128), rows) for k in range(n)
    ]
    for k in range(n):
        scr[places[k], :] = gm_in[k][...]
    carried = sum_of_side(earlier, n, True)
    carried_ref[...] = carried
    num = num_ref[...] + mm(qf_ref[...], carried, NT)
    inv = lax.rsqrt(jnp.mean(num * num, axis=1, keepdims=True) + EPSILON)
    normed = num * inv
    gm = scr[...].astype(jnp.float32)
    gn = bf((gm - normed * jnp.mean(gm * normed, axis=1, keepdims=True)) * inv)
    gn_ref[...] = gn
    scr[...] = bf(normed)
    for k in range(n):
        outs[k][...] = scr[places[k], :]
    total = jnp.zeros(total_ref.shape, jnp.float32)
    for t in reversed(range(n)):
        state_ref[t] = bf(total)
        at = pl.ds(t * rows, rows)
        total = total + mm(gn[t * rows : (t + 1) * rows], qf_ref[at, :], TN)
    total_ref[...] = bf(total)


def back_kernel(n, qkv_ref, om_ref, kf_ref, qf_ref, scores_ref, gn_ref, state_ref, carried_ref,
                later_ref, gq_ref, gv_ref, gkf_ref, gqf_scr):
    r, dim = member(n), om_ref.shape[1]
    rows = scores_ref.shape[1]
    scale = dim ** (-0.25)
    causal = causal_mask(rows)
    gqf_scr[...] = mm(gn_ref[...], carried_ref[...])
    for t in range(n):
        at = pl.ds(t * rows, rows)
        qf, kf, gn, v = qf_ref[at, :], kf_ref[at, :], gn_ref[at, :], qkv_ref[2, at, :]
        gs = bf(jnp.where(causal, mm(gn, v, NT), 0.0))
        gqf = gqf_scr[at, :] + mm(gs, kf) + mm(gn, state_ref[t])
        terms = bf(gqf * qf.astype(jnp.float32))
        gq_ref[at, :] = bf(mm(terms, om_ref[r], NT) * scale)
        later = later_ref[t]
        gv_ref[at, :] = mm(scores_ref[t], gn, TN) + mm(kf, later, NT)
        gkf_ref[at, :] = mm(gs, qf, TN) + mm(v, later)


def end_kernel(n, qkv_ref, om_ref, kf_ref, gq_ref, gv_ref, gkf_ref, *rest):
    later, outs, (gk_scr, gv_scr) = rest[: -n - 2], rest[-n - 2 : -2], rest[-2:]
    r, dim = member(n), om_ref.shape[1]
    rows = outs[0].shape[1]
    scale = dim ** (-0.25)
    kf, after = kf_ref[...], sum_of_side(later, n, False)
    gv_scr[...] = bf(gv_ref[...] + mm(kf, after, NT))
    gkf = gkf_ref[...] + mm(qkv_ref[2], after)
    terms = bf(gkf * kf.astype(jnp.float32))
    total = jnp.sum(terms.astype(jnp.float32), axis=1, keepdims=True)
    wide = qkv_ref[1].astype(jnp.float32)
    gk_scr[...] = bf(mm(terms, om_ref[r], NT) * scale - total * wide * (scale * scale))
    for k in range(n):
        at = pl.ds(pl.multiple_of((r ^ k) * rows, 128), rows)
        outs[k][0] = gq_ref[at, :]
        outs[k][1] = gk_scr[at, :]
        outs[k][2] = gv_scr[at, :]


def mixed_project_kernel(n, offsets, *refs):
    mixed_in, (w_ref, _, own_ref, sent_ref, scr) = refs[:n][::-1], refs[n:]
    r, h = member(n), lax.axis_index("head")
    width = own_ref.shape[2]
    dim = mixed_in[0].shape[1]
    half = len(offsets) // 2
    for k in range(n):
        scr[:, lane(r ^ k, dim)] = mixed_in[k][...]
    mixed = scr[...]
    for at, offset in enumerate(offsets):
        part = bf(mm(mixed, w_ref[:, lane(h ^ offset, width)]))
        if at < half:
            own_ref[at] = part
        else:
            sent_ref[at - half] = part


def unpack_kernel(n, *refs):
    got, (part_ref, last_ref) = refs[:n][::-1], refs[n : n + 2]
    out_ref, *outs = refs[n + 2 :]
    r = member(n)
    dim = got[0].shape[2]
    out_ref[...] = bf(part_ref[...] + last_ref[...].astype(jnp.float32))
    for k in range(n):
        cols = lane(r ^ k, dim)
        for at, out in enumerate(outs):
            out[:, cols] = got[k][at]


def local(queries, key_vectors, value_vectors, feature_proj, out_weight, grad_output):
    n, dim, feats = feature_proj.shape
    rows, width = grad_output.shape
    split = lax.axis_size("head")
    bits = bits_of(split)
    long = n * rows
    macs = long * dim * feats * 2
    f32 = jnp.float32

    offsets, blocks = [0], [grad_output]
    for bit in reversed(bits):
        blocks = blocks + [swap(b, "head", bit) for b in blocks]
        offsets = offsets + [o ^ bit for o in offsets]
    sends = call(
        functools.partial(pack_kernel, n),
        [struct((3, rows, dim))] * (n - 1),
        queries, key_vectors, value_vectors,
        specs=[ANY] * 3, scratch=[pltpu.SemaphoreType.DMA((3 * n - 3,))], vmem=60,
    )
    got = exchange(sends)
    (mark,) = call(mark_kernel, [struct((8, 128), f32)], blocks[offsets.index(1)], specs=[ANY], flops=10**10)
    gm_parts = call(
        functools.partial(grad_mixed_kernel, n, offsets),
        [struct((rows, dim))] * n,
        *blocks, out_weight, mark, flops=2 * rows * out_weight.size,
        specs=[VMEM] * (split + 1) + [ANY],
        scratch=[pltpu.VMEM((rows, n * dim), jnp.bfloat16)],
    )
    gm_in = exchange(gm_parts[1:]) + [gm_parts[0]]
    qkv, kf, state, total = call(
        functools.partial(first_kernel, n),
        [
            struct((3, long, dim)),
            struct((long, feats)),
            struct((n, dim, feats)),
            struct((dim, feats)),
        ],
        *got, queries, key_vectors, value_vectors, feature_proj, gm_parts[0],
        flops=2 * macs, specs=[VMEM] * (n + 3) + [ANY],
    )
    earlier = swap_totals(total, n)
    qf, scores, num = call(
        functools.partial(inner_kernel, n),
        [struct((long, feats)), struct((n, rows, rows)), struct((long, dim), f32)],
        qkv, feature_proj, kf, state, flops=4 * macs,
    )
    carried, gn, later, later_total, *mixed_parts = call(
        functools.partial(turn_kernel, n),
        [
            struct((dim, feats)),
            struct((long, dim)),
            struct((n, dim, feats)),
            struct((dim, feats)),
        ]
        + [struct((rows, dim))] * n,
        *gm_in, qf, num, *earlier, flops=2 * macs,
        scratch=[pltpu.VMEM((long, dim), jnp.bfloat16)],
    )
    after = swap_totals(later_total, n)
    mixed_in = exchange(mixed_parts[1:]) + [mixed_parts[0]]
    gq, gv_part, gkf_part = call(
        functools.partial(back_kernel, n),
        [struct((long, dim)), struct((long, dim), f32), struct((long, feats), f32)],
        qkv, feature_proj, kf, qf, scores, gn, state, carried, later, flops=8 * macs,
        scratch=[pltpu.VMEM((long, feats), f32)],
    )
    grads = call(
        functools.partial(end_kernel, n),
        [struct((3, rows, dim))] * n,
        qkv, feature_proj, kf, gq, gv_part, gkf_part, *after, flops=3 * macs,
        scratch=[pltpu.VMEM((long, dim), jnp.bfloat16)] * 2,
    )
    grads_in = exchange(grads[1:]) + [grads[0]]

    order = [o for o in range(split) if not o & 1] + [o for o in range(split) if o & 1]
    own, sent = call(
        functools.partial(mixed_project_kernel, n, order),
        [struct((split // 2, rows, width))] * 2,
        *mixed_in, out_weight, grads[0], flops=2 * rows * out_weight.size,
        specs=[VMEM] * (n + 1) + [ANY],
        scratch=[pltpu.VMEM((rows, n * dim), jnp.bfloat16)],
    )
    part, last = reduce_blocks(own, sent, bits)
    return call(
        functools.partial(unpack_kernel, n),
        [struct((rows, width))] + [struct((rows, n * dim))] * 3,
        *grads_in, part, last,
    )


def solution(mesh):
    placed = (
        P("seq", "head"),
        P("seq", "head"),
        P("seq", "head"),
        P("head", None, None),
        P("head", None),
        P("seq", "head"),
    )
    return jax.shard_map(
        local,
        mesh=mesh,
        in_specs=placed,
        out_specs=(P("seq", "head"),) * 4,
        check_vma=False,
    )
```

```python
import functools

import jax
import jax.numpy as jnp
from jax import lax
from jax.experimental import pallas as pl
from jax.experimental.pallas import tpu as pltpu
from jax.sharding import PartitionSpec as P

EPSILON = 1e-05
VMEM = pl.BlockSpec(memory_space=pltpu.VMEM)
ANY = pl.BlockSpec(memory_space=pl.ANY)
NN = (((1,), (0,)), ((), ()))
NT = (((1,), (1,)), ((), ()))
TN = (((0,), (0,)), ((), ()))


def mm(a, b, dims=NN):
    return lax.dot_general(a, b, dims, preferred_element_type=jnp.float32)


def bf(x):
    return x.astype(jnp.bfloat16)


def call(body, outs, *args, flops=0, specs=None, scratch=(), vmem=32):
    size = sum(a.size * a.dtype.itemsize for a in args)
    size += sum(o.size * o.dtype.itemsize for o in outs)
    return pl.pallas_call(
        body,
        out_shape=outs,
        in_specs=specs or [VMEM] * len(args),
        out_specs=[VMEM] * len(outs),
        scratch_shapes=list(scratch),
        cost_estimate=pl.CostEstimate(flops=flops, bytes_accessed=size, transcendentals=0),
        compiler_params=pltpu.CompilerParams(vmem_limit_bytes=vmem * 1024 * 1024),
    )(*args)


def struct(shape, dtype=jnp.bfloat16):
    return jax.ShapeDtypeStruct(shape, dtype)


def causal_mask(rows):
    row = lax.broadcasted_iota(jnp.int32, (rows, rows), 0)
    col = lax.broadcasted_iota(jnp.int32, (rows, rows), 1)
    return col <= row


def swap(array, axis, bit):
    size = lax.axis_size(axis)
    return lax.ppermute(array, axis, [(i, i ^ bit) for i in range(size)])


def bits_of(size):
    return [1 << b for b in range(size.bit_length() - 1)]


def reduce_blocks(own, sent, bits):
    got = swap(sent, "head", 1)
    for bit in bits[1:]:
        total = own.astype(jnp.float32) + got.astype(jnp.float32)
        pairs = total.reshape((total.shape[0] // 2, 2) + total.shape[1:])
        own, got = pairs[:, 0], swap(bf(pairs[:, 1]), "head", bit)
    return own[0].astype(jnp.float32), got[0]


def exchange(parts):
    return lax.all_to_all(parts, "member", 0, 0)


def swap_totals(total):
    got = []
    for bit in bits_of(lax.axis_size("group")):
        got.append(swap(bf(total), "group", bit))
        total = total.astype(jnp.float32) + got[-1].astype(jnp.float32)
    return got


def sum_of_side(refs, shape, earlier):
    group = lax.axis_index("group")
    total = jnp.zeros(shape, jnp.float32)
    for at, ref in enumerate(refs):
        from_earlier = lax.rem(lax.shift_right_logical(group, at), 2) == 1
        keep = from_earlier if earlier else jnp.logical_not(from_earlier)
        total = total + jnp.where(keep, ref[...].astype(jnp.float32), 0.0)
    return bf(total)


def lane(index, width):
    return pl.ds(pl.multiple_of(index * width, 128), width)


def pack_kernel(q_ref, k_ref, v_ref, out_ref, sems):
    n, _, _, dim = out_ref.shape
    copies = [
        pltpu.make_async_copy(
            ref.at[:, pl.ds(j * dim, dim)], out_ref.at[j, at], sems.at[j, at]
        )
        for j in range(n)
        for at, ref in enumerate((q_ref, k_ref, v_ref))
    ]
    for copy in copies:
        copy.start()
    for copy in copies:
        copy.wait()


def mark_kernel(_, out_ref):
    out_ref[...] = jnp.zeros(out_ref.shape, out_ref.dtype)


def grad_mixed_kernel(n, offsets, *refs):
    blocks, w_ref, out_ref = refs[:-3], refs[-3], refs[-1]
    h = lax.axis_index("head")
    width = blocks[0].shape[1]
    dim = out_ref.shape[2]
    total = None
    for offset, ref in zip(offsets, blocks):
        part = mm(ref[...], w_ref[:, lane(h ^ offset, width)], NT)
        total = part if total is None else total + part
    for j in range(n):
        out_ref[j] = bf(total[:, j * dim : (j + 1) * dim])


def first_kernel(n, got_ref, om_ref, _, qkv_ref, kf_ref, state_ref, total_ref):
    rows, dim = got_ref.shape[2:]
    r = lax.axis_index("member")
    scale = dim ** (-0.25)
    for t in range(n):
        qkv_ref[:, t * rows : (t + 1) * rows, :] = got_ref[t]
    k_all = qkv_ref[1]
    wide = k_all.astype(jnp.float32)
    half_sq = jnp.sum(wide * wide, axis=1, keepdims=True) * (scale * scale * 0.5)
    kf = bf(jnp.exp(mm(k_all, om_ref[r]) * scale - half_sq))
    kf_ref[...] = kf
    total = jnp.zeros(total_ref.shape, jnp.float32)
    for t in range(n):
        at = pl.ds(t * rows, rows)
        state_ref[t] = bf(total)
        total = total + mm(qkv_ref[2, at, :], kf[t * rows : (t + 1) * rows], TN)
    total_ref[...] = bf(total)


def inner_kernel(n, qkv_ref, om_ref, kf_ref, state_ref, qf_ref, scores_ref, num_ref):
    r, dim = lax.axis_index("member"), om_ref.shape[1]
    rows = scores_ref.shape[1]
    scale = dim ** (-0.25)
    causal = causal_mask(rows)
    qf_ref[...] = bf(jnp.exp(mm(qkv_ref[0], om_ref[r]) * scale))
    for t in range(n):
        at = pl.ds(t * rows, rows)
        qf = qf_ref[at, :]
        scores = bf(jnp.where(causal, mm(qf, kf_ref[at, :], NT), 0.0))
        scores_ref[t] = scores
        num_ref[at, :] = mm(scores, qkv_ref[2, at, :]) + mm(qf, state_ref[t], NT)


def turn_kernel(n, gm_ref, qf_ref, num_ref, *refs):
    earlier, (carried_ref, gn_ref, state_ref, total_ref, out_ref) = refs[:-5], refs[-5:]
    rows, dim = gm_ref.shape[1:]
    carried = sum_of_side(earlier, total_ref.shape, True)
    carried_ref[...] = carried
    num = num_ref[...] + mm(qf_ref[...], carried, NT)
    inv = lax.rsqrt(jnp.mean(num * num, axis=1, keepdims=True) + EPSILON)
    normed = num * inv
    gm = gm_ref[...].reshape(n * rows, dim).astype(jnp.float32)
    gn = bf((gm - normed * jnp.mean(gm * normed, axis=1, keepdims=True)) * inv)
    gn_ref[...] = gn
    out_ref[...] = bf(normed).reshape(out_ref.shape)
    total = jnp.zeros(total_ref.shape, jnp.float32)
    for t in reversed(range(n)):
        state_ref[t] = bf(total)
        at = pl.ds(t * rows, rows)
        total = total + mm(gn[t * rows : (t + 1) * rows], qf_ref[at, :], TN)
    total_ref[...] = bf(total)


def back_kernel(n, qkv_ref, om_ref, kf_ref, qf_ref, scores_ref, gn_ref, state_ref, carried_ref,
                later_ref, gq_ref, gv_ref, gkf_ref, gqf_scr):
    r, dim = lax.axis_index("member"), om_ref.shape[1]
    rows = scores_ref.shape[1]
    scale = dim ** (-0.25)
    causal = causal_mask(rows)
    gqf_scr[...] = mm(gn_ref[...], carried_ref[...])
    for t in range(n):
        at = pl.ds(t * rows, rows)
        qf, kf, gn, v = qf_ref[at, :], kf_ref[at, :], gn_ref[at, :], qkv_ref[2, at, :]
        gs = bf(jnp.where(causal, mm(gn, v, NT), 0.0))
        gqf = gqf_scr[at, :] + mm(gs, kf) + mm(gn, state_ref[t])
        terms = bf(gqf * qf.astype(jnp.float32))
        gq_ref[at, :] = bf(mm(terms, om_ref[r], NT) * scale)
        later = later_ref[t]
        gv_ref[at, :] = mm(scores_ref[t], gn, TN) + mm(kf, later, NT)
        gkf_ref[at, :] = mm(gs, qf, TN) + mm(v, later)


def end_kernel(n, qkv_ref, om_ref, kf_ref, gq_ref, gv_ref, gkf_ref, *rest):
    later, out_ref = rest[:-1], rest[-1]
    r, dim = lax.axis_index("member"), om_ref.shape[1]
    rows = out_ref.shape[2]
    scale = dim ** (-0.25)
    kf, after = kf_ref[...], sum_of_side(later, om_ref.shape[1:], False)
    gv = bf(gv_ref[...] + mm(kf, after, NT))
    gkf = gkf_ref[...] + mm(qkv_ref[2], after)
    terms = bf(gkf * kf.astype(jnp.float32))
    total = jnp.sum(terms.astype(jnp.float32), axis=1, keepdims=True)
    wide = qkv_ref[1].astype(jnp.float32)
    gk = bf(mm(terms, om_ref[r], NT) * scale - total * wide * (scale * scale))
    for t in range(n):
        at = slice(t * rows, (t + 1) * rows)
        out_ref[t, 0] = gq_ref[at, :]
        out_ref[t, 1] = gk[at]
        out_ref[t, 2] = gv[at]


def mixed_project_kernel(n, offsets, mixed_ref, w_ref, _, own_ref, sent_ref):
    h = lax.axis_index("head")
    width = own_ref.shape[2]
    half = len(offsets) // 2
    mixed = jnp.concatenate([mixed_ref[j] for j in range(n)], axis=1)
    for at, offset in enumerate(offsets):
        part = bf(mm(mixed, w_ref[:, lane(h ^ offset, width)]))
        if at < half:
            own_ref[at] = part
        else:
            sent_ref[at - half] = part


def unpack_kernel(n, got_ref, part_ref, last_ref, out_ref, *outs):
    dim = got_ref.shape[3]
    out_ref[...] = bf(part_ref[...] + last_ref[...].astype(jnp.float32))
    for j in range(n):
        for at, out in enumerate(outs):
            out[:, j * dim : (j + 1) * dim] = got_ref[j, at]


def local(queries, key_vectors, value_vectors, feature_proj, out_weight, grad_output):
    n, dim, feats = feature_proj.shape
    rows, width = grad_output.shape
    split = lax.axis_size("head")
    bits = bits_of(split)
    long = n * rows
    macs = long * dim * feats * 2
    f32 = jnp.float32

    offsets, blocks = [0], [grad_output]
    for bit in reversed(bits):
        blocks = blocks + [swap(b, "head", bit) for b in blocks]
        offsets = offsets + [o ^ bit for o in offsets]
    (packed,) = call(
        pack_kernel,
        [struct((n, 3, rows, dim))],
        queries, key_vectors, value_vectors,
        specs=[ANY] * 3, scratch=[pltpu.SemaphoreType.DMA((n, 3))], vmem=60,
    )
    got = exchange(packed)
    (mark,) = call(mark_kernel, [struct((8, 128), f32)], blocks[offsets.index(1)], specs=[ANY], flops=10**10)
    (gm_sent,) = call(
        functools.partial(grad_mixed_kernel, n, offsets),
        [struct((n, rows, dim))],
        *blocks, out_weight, mark, flops=2 * rows * out_weight.size,
        specs=[VMEM] * (split + 1) + [ANY],
    )
    gm = exchange(gm_sent)
    qkv, kf, state, total = call(
        functools.partial(first_kernel, n),
        [
            struct((3, long, dim)),
            struct((long, feats)),
            struct((n, dim, feats)),
            struct((dim, feats)),
        ],
        got, feature_proj, gm_sent, flops=2 * macs, specs=[VMEM, VMEM, ANY],
    )
    earlier = swap_totals(total)
    qf, scores, num = call(
        functools.partial(inner_kernel, n),
        [struct((long, feats)), struct((n, rows, rows)), struct((long, dim), f32)],
        qkv, feature_proj, kf, state, flops=4 * macs,
    )
    carried, gn, later, later_total, mixed_sent = call(
        functools.partial(turn_kernel, n),
        [
            struct((dim, feats)),
            struct((long, dim)),
            struct((n, dim, feats)),
            struct((dim, feats)),
            struct((n, rows, dim)),
        ],
        gm, qf, num, *earlier, flops=2 * macs,
    )
    after = swap_totals(later_total)
    mixed = exchange(mixed_sent)
    gq, gv_part, gkf_part = call(
        functools.partial(back_kernel, n),
        [struct((long, dim)), struct((long, dim), f32), struct((long, feats), f32)],
        qkv, feature_proj, kf, qf, scores, gn, state, carried, later, flops=8 * macs,
        scratch=[pltpu.VMEM((long, feats), f32)],
    )
    (grads_sent,) = call(
        functools.partial(end_kernel, n),
        [struct((n, 3, rows, dim))],
        qkv, feature_proj, kf, gq, gv_part, gkf_part, *after, flops=3 * macs,
    )
    grads = exchange(grads_sent)

    order = [o for o in range(split) if not o & 1] + [o for o in range(split) if o & 1]
    own, sent = call(
        functools.partial(mixed_project_kernel, n, order),
        [struct((split // 2, rows, width))] * 2,
        mixed, out_weight, grads_sent, flops=2 * rows * out_weight.size,
        specs=[VMEM, VMEM, ANY],
    )
    part, last = reduce_blocks(own, sent, bits)
    return call(
        functools.partial(unpack_kernel, n),
        [struct((rows, width))] + [struct((rows, n * dim))] * 3,
        grads, part, last,
    )


def solution(mesh):
    placed = (
        P(("group", "member"), "head"),
        P(("group", "member"), "head"),
        P(("group", "member"), "head"),
        P("head", None, None),
        P("head", None),
        P(("group", "member"), "head"),
    )

    def whole(*arrays):
        seq, head = mesh.shape["seq"], mesh.shape["head"]
        members = arrays[3].shape[0] // head
        split = jax.sharding.Mesh(
            mesh.devices.reshape(seq // members, members, head), ("group", "member", "head")
        )
        return jax.shard_map(
            local,
            mesh=split,
            in_specs=placed,
            out_specs=(P(("group", "member"), "head"),) * 4,
            check_vma=False,
        )(*arrays)

    return whole
```

```python
import functools

import jax
import jax.numpy as jnp
from jax import lax
from jax.experimental import pallas as pl
from jax.experimental.pallas import tpu as pltpu
from jax.sharding import PartitionSpec as P

EPSILON = 1e-05
VMEM = pl.BlockSpec(memory_space=pltpu.VMEM)
ANY = pl.BlockSpec(memory_space=pl.ANY)
NN = (((1,), (0,)), ((), ()))
NT = (((1,), (1,)), ((), ()))
TN = (((0,), (0,)), ((), ()))


def mm(a, b, dims=NN):
    return lax.dot_general(a, b, dims, preferred_element_type=jnp.float32)


def bf(x):
    return x.astype(jnp.bfloat16)


def call(body, outs, *args, flops=0, specs=None, out_specs=None, scratch=(), vmem=32):
    size = sum(a.size * a.dtype.itemsize for a in args)
    size += sum(o.size * o.dtype.itemsize for o in outs)
    return pl.pallas_call(
        body,
        out_shape=outs,
        in_specs=specs or [VMEM] * len(args),
        out_specs=out_specs or [VMEM] * len(outs),
        scratch_shapes=list(scratch),
        cost_estimate=pl.CostEstimate(flops=flops, bytes_accessed=size, transcendentals=0),
        compiler_params=pltpu.CompilerParams(vmem_limit_bytes=vmem * 1024 * 1024),
    )(*args)


def struct(shape, dtype=jnp.bfloat16):
    return jax.ShapeDtypeStruct(shape, dtype)


def tiles(long, rows):
    size = 256 if long % 256 == 0 else rows
    return [(at, at + size) for at in range(0, long, size)]


def causal(scores):
    row = lax.broadcasted_iota(jnp.int32, scores.shape, 0)
    col = lax.broadcasted_iota(jnp.int32, scores.shape, 1)
    return jnp.where(col <= row, scores, 0.0)


def lower(left, right, spans):
    out = {}
    for i, (a, b) in enumerate(spans):
        for j, (c, d) in enumerate(spans[: i + 1]):
            tile = mm(left[a:b], right[c:d], NT)
            out[i, j] = bf(causal(tile) if i == j else tile)
    return out


def times(tile_at, right, spans):
    return [
        sum(mm(tile_at(i, j), right[c:d]) for j, (c, d) in enumerate(spans[: i + 1]))
        for i in range(len(spans))
    ]


def transposed_times(tile_at, right, spans):
    return [
        sum(mm(tile_at(i, j), right[a:b], TN) for i, (a, b) in enumerate(spans) if i >= j)
        for j in range(len(spans))
    ]


def swap(array, axis, bit):
    size = lax.axis_size(axis)
    return lax.ppermute(array, axis, [(i, i ^ bit) for i in range(size)])


def bits_of(size):
    return [1 << b for b in range(size.bit_length() - 1)]


def reduce_blocks(own, sent, bits):
    got = swap(sent, "head", 1)
    for bit in bits[1:]:
        total = own.astype(jnp.float32) + got.astype(jnp.float32)
        pairs = total.reshape((total.shape[0] // 2, 2) + total.shape[1:])
        own, got = pairs[:, 0], swap(bf(pairs[:, 1]), "head", bit)
    return own[0].astype(jnp.float32), got[0]


def member(n):
    return lax.rem(lax.axis_index("seq"), n)


def exchange(parts):
    return [swap(part, "seq", k) for k, part in enumerate(parts, 1)][::-1]


def swap_totals(total, n):
    size, step, got = lax.axis_size("seq"), n, []
    while step < size:
        got.append(swap(bf(total), "seq", step))
        total = total.astype(jnp.float32) + got[-1].astype(jnp.float32)
        step *= 2
    return got


def sum_of_side(refs, n, earlier):
    group = lax.div(lax.axis_index("seq"), n)
    total = jnp.zeros(refs[0].shape, jnp.float32)
    for at, ref in enumerate(refs):
        from_earlier = lax.rem(lax.shift_right_logical(group, at), 2) == 1
        keep = from_earlier if earlier else jnp.logical_not(from_earlier)
        total = total + jnp.where(keep, ref[...].astype(jnp.float32), 0.0)
    return bf(total)


def lane(index, width):
    return pl.ds(pl.multiple_of(index * width, 128), width)


def pack_kernel(n, q_ref, k_ref, v_ref, *rest):
    outs, (scr, in_sems, out_sems) = rest[:-3], rest[-3:]
    r = member(n)
    dim = scr.shape[3]
    loads, stores = [], []
    for k, out in enumerate(outs, 1):
        for at, ref in enumerate((q_ref, k_ref, v_ref)):
            here = scr.at[k - 1, at]
            loads.append(
                pltpu.make_async_copy(ref.at[:, lane(r ^ k, dim)], here, in_sems.at[k - 1, at])
            )
            stores.append(pltpu.make_async_copy(here, out.at[at], out_sems.at[k - 1, at]))
    for load in loads:
        load.start()
    for load, store in zip(loads, stores):
        load.wait()
        store.start()
    for store in stores:
        store.wait()


def mark_kernel(_, out_ref):
    out_ref[...] = jnp.zeros(out_ref.shape, out_ref.dtype)


def grad_mixed_kernel(n, offsets, *refs):
    blocks, w_ref, outs, scr = refs[: -n - 3], refs[-n - 3], refs[-n - 1 : -1], refs[-1]
    r, h = member(n), lax.axis_index("head")
    width = blocks[0].shape[1]
    dim = outs[0].shape[1]
    total = None
    for offset, ref in zip(offsets, blocks):
        part = mm(ref[...], w_ref[:, lane(h ^ offset, width)], NT)
        total = part if total is None else total + part
    scr[...] = bf(total)
    for k in range(n):
        outs[k][...] = scr[:, lane(r ^ k, dim)]


def first_kernel(n, *refs):
    got, own, om_ref = refs[: n - 1][::-1], refs[n - 1 : n + 2], refs[n + 2]
    qkv_ref, kf_ref, total_ref = refs[n + 4 :]
    r = member(n)
    rows, dim = own[0].shape[0], om_ref.shape[1]
    scale = dim ** (-0.25)
    for k in range(n):
        at = pl.ds(pl.multiple_of((r ^ k) * rows, 128), rows)
        if k:
            qkv_ref[:, at, :] = got[k - 1][...]
        else:
            for i, ref in enumerate(own):
                qkv_ref[i, at, :] = ref[:, lane(r, dim)]
    k_all = qkv_ref[1]
    wide = k_all.astype(jnp.float32)
    half_sq = jnp.sum(wide * wide, axis=1, keepdims=True) * (scale * scale * 0.5)
    kf = bf(jnp.exp(mm(k_all, om_ref[r]) * scale - half_sq))
    kf_ref[...] = kf
    total_ref[...] = bf(mm(qkv_ref[2], kf, TN))


def inner_kernel(rows, qkv_ref, om_ref, kf_ref, qf_ref, scores_ref, num_ref):
    long, dim = num_ref.shape
    n = long // rows
    scale = dim ** (-0.25)
    spans = tiles(long, rows)
    qf = bf(jnp.exp(mm(qkv_ref[0], om_ref[member(n)]) * scale))
    qf_ref[...] = qf
    scores = lower(qf, kf_ref[...], spans)
    for (i, j), tile in scores.items():
        scores_ref[slice(*spans[i]), slice(*spans[j])] = tile
    for (a, b), part in zip(spans, times(lambda i, j: scores[i, j], qkv_ref[2], spans)):
        num_ref[a:b, :] = part


def turn_kernel(n, *refs):
    gm_in, (qf_ref, num_ref), earlier = refs[:n][::-1], refs[n : n + 2], refs[n + 2 : -n - 4]
    carried_ref, gn_ref, total_ref = refs[-n - 4 : -n - 1]
    outs, scr = refs[-n - 1 : -1], refs[-1]
    r = member(n)
    rows = gm_in[0].shape[0]
    places = [
        pl.ds(pl.multiple_of((r ^ k) * rows, 128), rows) for k in range(n)
    ]
    for k in range(n):
        scr[places[k], :] = gm_in[k][...]
    carried = sum_of_side(earlier, n, True)
    carried_ref[...] = carried
    num = num_ref[...] + mm(qf_ref[...], carried, NT)
    inv = lax.rsqrt(jnp.mean(num * num, axis=1, keepdims=True) + EPSILON)
    normed = num * inv
    gm = scr[...].astype(jnp.float32)
    gn = bf((gm - normed * jnp.mean(gm * normed, axis=1, keepdims=True)) * inv)
    gn_ref[...] = gn
    scr[...] = bf(normed)
    for k in range(n):
        outs[k][...] = scr[places[k], :]
    total_ref[...] = bf(mm(gn, qf_ref[...], TN))


def back_kernel(rows, qkv_ref, om_ref, kf_ref, qf_ref, scores_ref, gn_ref, carried_ref,
                gq_ref, gv_ref, gkf_ref):
    long, dim = gn_ref.shape
    r = member(long // rows)
    scale = dim ** (-0.25)
    spans = tiles(long, rows)
    gn, qf = gn_ref[...], qf_ref[...]
    gs = lower(gn, qkv_ref[2], spans)
    cross = mm(gn, carried_ref[...])
    for (a, b), part in zip(spans, times(lambda i, j: gs[i, j], kf_ref[...], spans)):
        terms = bf((cross[a:b] + part) * qf[a:b].astype(jnp.float32))
        gq_ref[a:b, :] = bf(mm(terms, om_ref[r], NT) * scale)
    for (a, b), part in zip(spans, transposed_times(lambda i, j: gs[i, j], qf, spans)):
        gkf_ref[a:b, :] = part

    def scores_at(i, j):
        return scores_ref[slice(*spans[i]), slice(*spans[j])]

    for (a, b), part in zip(spans, transposed_times(scores_at, gn, spans)):
        gv_ref[a:b, :] = part


def end_kernel(n, qkv_ref, om_ref, kf_ref, gq_ref, gv_ref, gkf_ref, *rest):
    later, outs, (gk_scr, gv_scr) = rest[: -n - 2], rest[-n - 2 : -2], rest[-2:]
    r, dim = member(n), om_ref.shape[1]
    rows = outs[0].shape[1]
    scale = dim ** (-0.25)
    kf, after = kf_ref[...], sum_of_side(later, n, False)
    gv_scr[...] = bf(gv_ref[...] + mm(kf, after, NT))
    gkf = gkf_ref[...] + mm(qkv_ref[2], after)
    terms = bf(gkf * kf.astype(jnp.float32))
    total = jnp.sum(terms.astype(jnp.float32), axis=1, keepdims=True)
    wide = qkv_ref[1].astype(jnp.float32)
    gk_scr[...] = bf(mm(terms, om_ref[r], NT) * scale - total * wide * (scale * scale))
    for k in range(n):
        at = pl.ds(pl.multiple_of((r ^ k) * rows, 128), rows)
        outs[k][0] = gq_ref[at, :]
        outs[k][1] = gk_scr[at, :]
        outs[k][2] = gv_scr[at, :]


def mixed_project_kernel(n, offsets, *refs):
    mixed_in, (w_ref, _, own_ref, sent_ref, scr) = refs[:n][::-1], refs[n:]
    r, h = member(n), lax.axis_index("head")
    width = own_ref.shape[2]
    dim = mixed_in[0].shape[1]
    half = len(offsets) // 2
    for k in range(n):
        scr[:, lane(r ^ k, dim)] = mixed_in[k][...]
    mixed = scr[...]
    for at, offset in enumerate(offsets):
        part = bf(mm(mixed, w_ref[:, lane(h ^ offset, width)]))
        if at < half:
            own_ref[at] = part
        else:
            sent_ref[at - half] = part


def unpack_kernel(n, *refs):
    got, (part_ref, last_ref) = refs[:n][::-1], refs[n : n + 2]
    (out_ref, *outs), (scr, sems, last_sem) = refs[n + 2 : -3], refs[-3:]
    r = member(n)
    dim = got[0].shape[2]
    copies = [
        pltpu.make_async_copy(got[k].at[at], out.at[:, lane(r ^ k, dim)], sems.at[k, at])
        for k in range(n)
        for at, out in enumerate(outs)
    ]
    for copy in copies:
        copy.start()
    scr[...] = bf(part_ref[...] + last_ref[...].astype(jnp.float32))
    copies.append(pltpu.make_async_copy(scr, out_ref, last_sem))
    copies[-1].start()
    for copy in copies:
        copy.wait()


def local(queries, key_vectors, value_vectors, feature_proj, out_weight, grad_output):
    n, dim, feats = feature_proj.shape
    rows, width = grad_output.shape
    split = lax.axis_size("head")
    bits = bits_of(split)
    long = n * rows
    macs = long * dim * feats * 2
    f32 = jnp.float32

    offsets, blocks = [0], [grad_output]
    for bit in reversed(bits):
        blocks = blocks + [swap(b, "head", bit) for b in blocks]
        offsets = offsets + [o ^ bit for o in offsets]
    sends = call(
        functools.partial(pack_kernel, n),
        [struct((3, rows, dim))] * (n - 1),
        queries, key_vectors, value_vectors,
        specs=[ANY] * 3, out_specs=[ANY] * (n - 1), vmem=60,
        scratch=[
            pltpu.VMEM((n - 1, 3, rows, dim), jnp.bfloat16),
            pltpu.SemaphoreType.DMA((n - 1, 3)),
            pltpu.SemaphoreType.DMA((n - 1, 3)),
        ],
    )
    got = exchange(sends)
    (mark,) = call(mark_kernel, [struct((8, 128), f32)], blocks[offsets.index(1)], specs=[ANY], flops=10**10)
    gm_parts = call(
        functools.partial(grad_mixed_kernel, n, offsets),
        [struct((rows, dim))] * n,
        *blocks, out_weight, mark, flops=2 * rows * out_weight.size,
        specs=[VMEM] * (split + 1) + [ANY],
        scratch=[pltpu.VMEM((rows, n * dim), jnp.bfloat16)],
    )
    gm_in = exchange(gm_parts[1:]) + [gm_parts[0]]
    qkv, kf, total = call(
        functools.partial(first_kernel, n),
        [
            struct((3, long, dim)),
            struct((long, feats)),
            struct((dim, feats)),
        ],
        *got, queries, key_vectors, value_vectors, feature_proj, gm_parts[0],
        flops=2 * macs, specs=[VMEM] * (n + 3) + [ANY],
    )
    earlier = swap_totals(total, n)
    qf, scores, num = call(
        functools.partial(inner_kernel, rows),
        [struct((long, feats)), struct((long, long)), struct((long, dim), f32)],
        qkv, feature_proj, kf, flops=4 * macs,
    )
    carried, gn, later_total, *mixed_parts = call(
        functools.partial(turn_kernel, n),
        [
            struct((dim, feats)),
            struct((long, dim)),
            struct((dim, feats)),
        ]
        + [struct((rows, dim))] * n,
        *gm_in, qf, num, *earlier, flops=2 * macs,
        scratch=[pltpu.VMEM((long, dim), jnp.bfloat16)],
    )
    after = swap_totals(later_total, n)
    mixed_in = exchange(mixed_parts[1:]) + [mixed_parts[0]]
    gq, gv_part, gkf_part = call(
        functools.partial(back_kernel, rows),
        [struct((long, dim)), struct((long, dim), f32), struct((long, feats), f32)],
        qkv, feature_proj, kf, qf, scores, gn, carried, flops=8 * macs,
    )
    grads = call(
        functools.partial(end_kernel, n),
        [struct((3, rows, dim))] * n,
        qkv, feature_proj, kf, gq, gv_part, gkf_part, *after, flops=3 * macs,
        scratch=[pltpu.VMEM((long, dim), jnp.bfloat16)] * 2,
    )
    grads_in = exchange(grads[1:]) + [grads[0]]

    order = [o for o in range(split) if not o & 1] + [o for o in range(split) if o & 1]
    own, sent = call(
        functools.partial(mixed_project_kernel, n, order),
        [struct((split // 2, rows, width))] * 2,
        *mixed_in, out_weight, grads[0], flops=2 * rows * out_weight.size,
        specs=[VMEM] * (n + 1) + [ANY],
        scratch=[pltpu.VMEM((rows, n * dim), jnp.bfloat16)],
    )
    part, last = reduce_blocks(own, sent, bits)
    return call(
        functools.partial(unpack_kernel, n),
        [struct((rows, width))] + [struct((rows, n * dim))] * 3,
        *grads_in, part, last,
        out_specs=[ANY] * 4,
        scratch=[
            pltpu.VMEM((rows, width), jnp.bfloat16),
            pltpu.SemaphoreType.DMA((n, 3)),
            pltpu.SemaphoreType.DMA,
        ],
    )


def solution(mesh):
    placed = (
        P("seq", "head"),
        P("seq", "head"),
        P("seq", "head"),
        P("head", None, None),
        P("head", None),
        P("seq", "head"),
    )
    return jax.shard_map(
        local,
        mesh=mesh,
        in_specs=placed,
        out_specs=(P("seq", "head"),) * 4,
        check_vma=False,
    )
```

```python
import functools

import jax
import jax.numpy as jnp
from jax import lax
from jax.experimental import pallas as pl
from jax.experimental.pallas import tpu as pltpu
from jax.sharding import PartitionSpec as P

EPSILON = 1e-05
VMEM = pl.BlockSpec(memory_space=pltpu.VMEM)
ANY = pl.BlockSpec(memory_space=pl.ANY)
NN = (((1,), (0,)), ((), ()))
NT = (((1,), (1,)), ((), ()))
TN = (((0,), (0,)), ((), ()))


def mm(a, b, dims=NN):
    return lax.dot_general(a, b, dims, preferred_element_type=jnp.float32)


def bf(x):
    return x.astype(jnp.bfloat16)


def call(body, outs, *args, flops=0, specs=None, out_specs=None, scratch=(), vmem=32):
    size = sum(a.size * a.dtype.itemsize for a in args)
    size += sum(o.size * o.dtype.itemsize for o in outs)
    return pl.pallas_call(
        body,
        out_shape=outs,
        in_specs=specs or [VMEM] * len(args),
        out_specs=out_specs or [VMEM] * len(outs),
        scratch_shapes=list(scratch),
        cost_estimate=pl.CostEstimate(flops=flops, bytes_accessed=size, transcendentals=0),
        compiler_params=pltpu.CompilerParams(vmem_limit_bytes=int(vmem * 1024 * 1024)),
    )(*args)


def struct(shape, dtype=jnp.bfloat16):
    return jax.ShapeDtypeStruct(shape, dtype)


def tiles(long, rows):
    size = 256 if long % 256 == 0 else rows
    return [(at, at + size) for at in range(0, long, size)]


def causal(scores):
    row = lax.broadcasted_iota(jnp.int32, scores.shape, 0)
    col = lax.broadcasted_iota(jnp.int32, scores.shape, 1)
    return jnp.where(col <= row, scores, 0.0)


def lower(left, right, spans):
    out = {}
    for i, (a, b) in enumerate(spans):
        for j, (c, d) in enumerate(spans[: i + 1]):
            tile = mm(left[a:b], right[c:d], NT)
            out[i, j] = bf(causal(tile) if i == j else tile)
    return out


def times(tile_at, right, spans):
    return [
        sum(mm(tile_at(i, j), right[c:d]) for j, (c, d) in enumerate(spans[: i + 1]))
        for i in range(len(spans))
    ]


def transposed_times(tile_at, right, spans):
    return [
        sum(mm(tile_at(i, j), right[a:b], TN) for i, (a, b) in enumerate(spans) if i >= j)
        for j in range(len(spans))
    ]


def swap(array, axis, bit):
    size = lax.axis_size(axis)
    return lax.ppermute(array, axis, [(i, i ^ bit) for i in range(size)])


def bits_of(size):
    return [1 << b for b in range(size.bit_length() - 1)]


def reduce_blocks(own, sent, bits):
    got = swap(sent, "head", 1)
    for bit in bits[1:]:
        total = own.astype(jnp.float32) + got.astype(jnp.float32)
        pairs = total.reshape((total.shape[0] // 2, 2) + total.shape[1:])
        own, got = pairs[:, 0], swap(bf(pairs[:, 1]), "head", bit)
    return own[0].astype(jnp.float32), got[0]


def member(n):
    return lax.rem(lax.axis_index("seq"), n)


def exchange(parts):
    return [swap(part, "seq", k) for k, part in enumerate(parts, 1)][::-1]


def swap_totals(total, n):
    size, step, got = lax.axis_size("seq"), n, []
    while step < size:
        got.append(swap(bf(total), "seq", step))
        total = total.astype(jnp.float32) + got[-1].astype(jnp.float32)
        step *= 2
    return got


def sum_of_side(refs, n, earlier):
    group = lax.div(lax.axis_index("seq"), n)
    total = jnp.zeros(refs[0].shape, jnp.float32)
    for at, ref in enumerate(refs):
        from_earlier = lax.rem(lax.shift_right_logical(group, at), 2) == 1
        keep = from_earlier if earlier else jnp.logical_not(from_earlier)
        total = total + jnp.where(keep, ref[...].astype(jnp.float32), 0.0)
    return bf(total)


def lane(index, width):
    return pl.ds(pl.multiple_of(index * width, 128), width)


def pack_kernel(n, q_ref, k_ref, v_ref, *rest):
    outs, sems = rest[:-1], rest[-1]
    r = member(n)
    dim = outs[0].shape[2]
    copies = [
        pltpu.make_async_copy(ref.at[:, lane(r ^ k, dim)], out.at[at], sems.at[k - 1, at])
        for k, out in enumerate(outs, 1)
        for at, ref in enumerate((q_ref, k_ref, v_ref))
    ]
    for copy in copies:
        copy.start()
    for copy in copies:
        copy.wait()


def mark_kernel(_, out_ref):
    out_ref[...] = jnp.zeros(out_ref.shape, out_ref.dtype)


def grad_mixed_kernel(n, offsets, *refs):
    blocks, w_ref, outs, scr = refs[: -n - 3], refs[-n - 3], refs[-n - 1 : -1], refs[-1]
    r, h = member(n), lax.axis_index("head")
    width = blocks[0].shape[1]
    dim = outs[0].shape[1]
    total = None
    for offset, ref in zip(offsets, blocks):
        part = mm(ref[...], w_ref[:, lane(h ^ offset, width)], NT)
        total = part if total is None else total + part
    scr[...] = bf(total)
    for k in range(n):
        outs[k][...] = scr[:, lane(r ^ k, dim)]


def first_kernel(n, *refs):
    got, own, om_ref = refs[: n - 1][::-1], refs[n - 1 : n + 2], refs[n + 2]
    qkv_ref, kf_ref, total_ref = refs[n + 4 :]
    r = member(n)
    rows, dim = own[0].shape[0], om_ref.shape[1]
    scale = dim ** (-0.25)
    for k in range(n):
        at = pl.ds(pl.multiple_of((r ^ k) * rows, 128), rows)
        if k:
            qkv_ref[:, at, :] = got[k - 1][...]
        else:
            for i, ref in enumerate(own):
                qkv_ref[i, at, :] = ref[:, lane(r, dim)]
    k_all = qkv_ref[1]
    wide = k_all.astype(jnp.float32)
    half_sq = jnp.sum(wide * wide, axis=1, keepdims=True) * (scale * scale * 0.5)
    kf = bf(jnp.exp(mm(k_all, om_ref[r]) * scale - half_sq))
    kf_ref[...] = kf
    total_ref[...] = bf(mm(qkv_ref[2], kf, TN))


def inner_kernel(rows, qkv_ref, om_ref, kf_ref, qf_ref, scores_ref, num_ref):
    long, dim = num_ref.shape
    n = long // rows
    scale = dim ** (-0.25)
    spans = tiles(long, rows)
    qf = bf(jnp.exp(mm(qkv_ref[0], om_ref[member(n)]) * scale))
    qf_ref[...] = qf
    scores = lower(qf, kf_ref[...], spans)
    for (i, j), tile in scores.items():
        scores_ref[slice(*spans[i]), slice(*spans[j])] = tile
    for (a, b), part in zip(spans, times(lambda i, j: scores[i, j], qkv_ref[2], spans)):
        num_ref[a:b, :] = part


def turn_kernel(n, *refs):
    gm_in, (qf_ref, num_ref), earlier = refs[:n][::-1], refs[n : n + 2], refs[n + 2 : -n - 4]
    carried_ref, gn_ref, total_ref = refs[-n - 4 : -n - 1]
    outs, scr = refs[-n - 1 : -1], refs[-1]
    r = member(n)
    rows = gm_in[0].shape[0]
    places = [
        pl.ds(pl.multiple_of((r ^ k) * rows, 128), rows) for k in range(n)
    ]
    for k in range(n):
        scr[places[k], :] = gm_in[k][...]
    carried = sum_of_side(earlier, n, True)
    carried_ref[...] = carried
    num = num_ref[...] + mm(qf_ref[...], carried, NT)
    inv = lax.rsqrt(jnp.mean(num * num, axis=1, keepdims=True) + EPSILON)
    normed = num * inv
    gm = scr[...].astype(jnp.float32)
    gn = bf((gm - normed * jnp.mean(gm * normed, axis=1, keepdims=True)) * inv)
    gn_ref[...] = gn
    scr[...] = bf(normed)
    for k in range(n):
        outs[k][...] = scr[places[k], :]
    total_ref[...] = bf(mm(gn, qf_ref[...], TN))


def back_kernel(rows, qkv_ref, om_ref, kf_ref, qf_ref, scores_ref, gn_ref, carried_ref,
                gq_ref, gv_ref, gkf_ref):
    long, dim = gn_ref.shape
    r = member(long // rows)
    scale = dim ** (-0.25)
    spans = tiles(long, rows)
    gn, qf = gn_ref[...], qf_ref[...]
    gs = lower(gn, qkv_ref[2], spans)
    cross = mm(gn, carried_ref[...])
    for (a, b), part in zip(spans, times(lambda i, j: gs[i, j], kf_ref[...], spans)):
        terms = bf((cross[a:b] + part) * qf[a:b].astype(jnp.float32))
        gq_ref[a:b, :] = bf(mm(terms, om_ref[r], NT) * scale)
    for (a, b), part in zip(spans, transposed_times(lambda i, j: gs[i, j], qf, spans)):
        gkf_ref[a:b, :] = part

    def scores_at(i, j):
        return scores_ref[slice(*spans[i]), slice(*spans[j])]

    for (a, b), part in zip(spans, transposed_times(scores_at, gn, spans)):
        gv_ref[a:b, :] = part


def end_kernel(n, qkv_ref, om_ref, kf_ref, gq_ref, gv_ref, gkf_ref, *rest):
    later, outs, (gk_scr, gv_scr) = rest[: -n - 2], rest[-n - 2 : -2], rest[-2:]
    r, dim = member(n), om_ref.shape[1]
    rows = outs[0].shape[1]
    scale = dim ** (-0.25)
    kf, after = kf_ref[...], sum_of_side(later, n, False)
    gv_scr[...] = bf(gv_ref[...] + mm(kf, after, NT))
    gkf = gkf_ref[...] + mm(qkv_ref[2], after)
    terms = bf(gkf * kf.astype(jnp.float32))
    total = jnp.sum(terms.astype(jnp.float32), axis=1, keepdims=True)
    wide = qkv_ref[1].astype(jnp.float32)
    gk_scr[...] = bf(mm(terms, om_ref[r], NT) * scale - total * wide * (scale * scale))
    for k in range(n):
        at = pl.ds(pl.multiple_of((r ^ k) * rows, 128), rows)
        outs[k][0] = gq_ref[at, :]
        outs[k][1] = gk_scr[at, :]
        outs[k][2] = gv_scr[at, :]


def mixed_project_kernel(n, offsets, *refs):
    mixed_in, (w_ref, _, own_ref, sent_ref, scr) = refs[:n][::-1], refs[n:]
    r, h = member(n), lax.axis_index("head")
    width = own_ref.shape[2]
    dim = mixed_in[0].shape[1]
    half = len(offsets) // 2
    for k in range(n):
        scr[:, lane(r ^ k, dim)] = mixed_in[k][...]
    mixed = scr[...]
    for at, offset in enumerate(offsets):
        part = bf(mm(mixed, w_ref[:, lane(h ^ offset, width)]))
        if at < half:
            own_ref[at] = part
        else:
            sent_ref[at - half] = part


def unpack_kernel(n, *refs):
    got, (part_ref, last_ref) = refs[:n][::-1], refs[n : n + 2]
    (out_ref, *outs), (scr, sems, last_sem) = refs[n + 2 : -3], refs[-3:]
    r = member(n)
    dim = got[0].shape[2]
    copies = [
        pltpu.make_async_copy(got[k].at[at], out.at[:, lane(r ^ k, dim)], sems.at[k, at])
        for k in range(n)
        for at, out in enumerate(outs)
    ]
    for copy in copies:
        copy.start()
    scr[...] = bf(part_ref[...] + last_ref[...].astype(jnp.float32))
    copies.append(pltpu.make_async_copy(scr, out_ref, last_sem))
    copies[-1].start()
    for copy in copies:
        copy.wait()


def local(queries, key_vectors, value_vectors, feature_proj, out_weight, grad_output):
    n, dim, feats = feature_proj.shape
    rows, width = grad_output.shape
    split = lax.axis_size("head")
    bits = bits_of(split)
    long = n * rows
    macs = long * dim * feats * 2
    f32 = jnp.float32

    offsets, blocks = [0], [grad_output]
    for bit in reversed(bits):
        blocks = blocks + [swap(b, "head", bit) for b in blocks]
        offsets = offsets + [o ^ bit for o in offsets]
    sends = call(
        functools.partial(pack_kernel, n),
        [struct((3, rows, dim))] * (n - 1),
        queries, key_vectors, value_vectors,
        specs=[ANY] * 3, scratch=[pltpu.SemaphoreType.DMA((n - 1, 3))], vmem=53.62,
    )
    got = exchange(sends)
    (mark,) = call(mark_kernel, [struct((8, 128), f32)], blocks[offsets.index(1)], specs=[ANY], flops=10**10)
    gm_parts = call(
        functools.partial(grad_mixed_kernel, n, offsets),
        [struct((rows, dim))] * n,
        *blocks, out_weight, mark, flops=2 * rows * out_weight.size,
        specs=[VMEM] * (split + 1) + [ANY],
        scratch=[pltpu.VMEM((rows, n * dim), jnp.bfloat16)],
    )
    gm_in = exchange(gm_parts[1:]) + [gm_parts[0]]
    qkv, kf, total = call(
        functools.partial(first_kernel, n),
        [
            struct((3, long, dim)),
            struct((long, feats)),
            struct((dim, feats)),
        ],
        *got, queries, key_vectors, value_vectors, feature_proj, gm_parts[0],
        flops=2 * macs, specs=[VMEM] * (n + 3) + [ANY],
    )
    earlier = swap_totals(total, n)
    qf, scores, num = call(
        functools.partial(inner_kernel, rows),
        [struct((long, feats)), struct((long, long)), struct((long, dim), f32)],
        qkv, feature_proj, kf, flops=4 * macs,
    )
    carried, gn, later_total, *mixed_parts = call(
        functools.partial(turn_kernel, n),
        [
            struct((dim, feats)),
            struct((long, dim)),
            struct((dim, feats)),
        ]
        + [struct((rows, dim))] * n,
        *gm_in, qf, num, *earlier, flops=2 * macs,
        scratch=[pltpu.VMEM((long, dim), jnp.bfloat16)],
    )
    after = swap_totals(later_total, n)
    mixed_in = exchange(mixed_parts[1:]) + [mixed_parts[0]]
    gq, gv_part, gkf_part = call(
        functools.partial(back_kernel, rows),
        [struct((long, dim)), struct((long, dim), f32), struct((long, feats), f32)],
        qkv, feature_proj, kf, qf, scores, gn, carried, flops=8 * macs,
    )
    grads = call(
        functools.partial(end_kernel, n),
        [struct((3, rows, dim))] * n,
        qkv, feature_proj, kf, gq, gv_part, gkf_part, *after, flops=3 * macs,
        scratch=[pltpu.VMEM((long, dim), jnp.bfloat16)] * 2,
    )
    grads_in = exchange(grads[1:]) + [grads[0]]

    order = [o for o in range(split) if not o & 1] + [o for o in range(split) if o & 1]
    own, sent = call(
        functools.partial(mixed_project_kernel, n, order),
        [struct((split // 2, rows, width))] * 2,
        *mixed_in, out_weight, grads[0], flops=2 * rows * out_weight.size,
        specs=[VMEM] * (n + 1) + [ANY],
        scratch=[pltpu.VMEM((rows, n * dim), jnp.bfloat16)],
    )
    part, last = reduce_blocks(own, sent, bits)
    return call(
        functools.partial(unpack_kernel, n),
        [struct((rows, width))] + [struct((rows, n * dim))] * 3,
        *grads_in, part, last,
        out_specs=[ANY] * 4,
        scratch=[
            pltpu.VMEM((rows, width), jnp.bfloat16),
            pltpu.SemaphoreType.DMA((n, 3)),
            pltpu.SemaphoreType.DMA,
        ],
    )


def solution(mesh):
    placed = (
        P("seq", "head"),
        P("seq", "head"),
        P("seq", "head"),
        P("head", None, None),
        P("head", None),
        P("seq", "head"),
    )
    return jax.shard_map(
        local,
        mesh=mesh,
        in_specs=placed,
        out_specs=(P("seq", "head"),) * 4,
        check_vma=False,
    )
```

```python
import functools

import jax
import jax.numpy as jnp
from jax import lax
from jax.experimental import pallas as pl
from jax.experimental.pallas import tpu as pltpu
from jax.sharding import PartitionSpec as P

EPSILON = 1e-05
VMEM = pl.BlockSpec(memory_space=pltpu.VMEM)
ANY = pl.BlockSpec(memory_space=pl.ANY)
NN = (((1,), (0,)), ((), ()))
NT = (((1,), (1,)), ((), ()))
TN = (((0,), (0,)), ((), ()))


def mm(a, b, dims=NN):
    return lax.dot_general(a, b, dims, preferred_element_type=jnp.float32)


def bf(x):
    return x.astype(jnp.bfloat16)


def call(body, outs, *args, flops=0, specs=None, out_specs=None, scratch=(), vmem=32):
    size = sum(a.size * a.dtype.itemsize for a in args)
    size += sum(o.size * o.dtype.itemsize for o in outs)
    return pl.pallas_call(
        body,
        out_shape=outs,
        in_specs=specs or [VMEM] * len(args),
        out_specs=out_specs or [VMEM] * len(outs),
        scratch_shapes=list(scratch),
        cost_estimate=pl.CostEstimate(flops=flops, bytes_accessed=size, transcendentals=0),
        compiler_params=pltpu.CompilerParams(vmem_limit_bytes=int(vmem * 1024 * 1024)),
    )(*args)


def struct(shape, dtype=jnp.bfloat16):
    return jax.ShapeDtypeStruct(shape, dtype)


def tiles(long, rows):
    size = 256 if long % 256 == 0 else rows
    return [(at, at + size) for at in range(0, long, size)]


def causal(scores):
    row = lax.broadcasted_iota(jnp.int32, scores.shape, 0)
    col = lax.broadcasted_iota(jnp.int32, scores.shape, 1)
    return jnp.where(col <= row, scores, 0.0)


def lower(left, right, spans):
    out = {}
    for i, (a, b) in enumerate(spans):
        for j, (c, d) in enumerate(spans[: i + 1]):
            tile = mm(left[a:b], right[c:d], NT)
            out[i, j] = bf(causal(tile) if i == j else tile)
    return out


def times(tile_at, right, spans):
    return [
        sum(mm(tile_at(i, j), right[c:d]) for j, (c, d) in enumerate(spans[: i + 1]))
        for i in range(len(spans))
    ]


def transposed_times(tile_at, right, spans):
    return [
        sum(mm(tile_at(i, j), right[a:b], TN) for i, (a, b) in enumerate(spans) if i >= j)
        for j in range(len(spans))
    ]


def swap(array, axis, bit):
    size = lax.axis_size(axis)
    return lax.ppermute(array, axis, [(i, i ^ bit) for i in range(size)])


def bits_of(size):
    return [1 << b for b in range(size.bit_length() - 1)]


def reduce_blocks(own, sent, bits):
    got = swap(sent, "head", bits[0])
    for bit in bits[1:]:
        total = own + got.astype(jnp.float32)
        pairs = total.reshape((total.shape[0] // 2, 2) + total.shape[1:])
        own, got = pairs[:, 0], swap(bf(pairs[:, 1]), "head", bit)
    return own[0], got[0]


def member(n):
    return lax.rem(lax.axis_index("seq"), n)


def exchange(parts):
    return [swap(part, "seq", k) for k, part in enumerate(parts, 1)][::-1]


def swap_totals(total, n):
    size, step, got = lax.axis_size("seq"), n, []
    while step < size:
        got.append(swap(bf(total), "seq", step))
        total = total.astype(jnp.float32) + got[-1].astype(jnp.float32)
        step *= 2
    return got


def sum_of_side(refs, n, earlier):
    group = lax.div(lax.axis_index("seq"), n)
    total = jnp.zeros(refs[0].shape, jnp.float32)
    for at, ref in enumerate(refs):
        from_earlier = lax.rem(lax.shift_right_logical(group, at), 2) == 1
        keep = from_earlier if earlier else jnp.logical_not(from_earlier)
        total = total + jnp.where(keep, ref[...].astype(jnp.float32), 0.0)
    return bf(total)


def lane(index, width):
    return pl.ds(pl.multiple_of(index * width, 128), width)


def pack_kernel(n, q_ref, k_ref, v_ref, *rest):
    outs, sems = rest[:-1], rest[-1]
    r = member(n)
    dim = outs[0].shape[2]
    copies = [
        pltpu.make_async_copy(ref.at[:, lane(r ^ k, dim)], out.at[at], sems.at[k - 1, at])
        for k, out in enumerate(outs, 1)
        for at, ref in enumerate((q_ref, k_ref, v_ref))
    ]
    for copy in copies:
        copy.start()
    for copy in copies:
        copy.wait()


def mark_kernel(_, out_ref):
    out_ref[...] = jnp.zeros(out_ref.shape, out_ref.dtype)


def grad_mixed_kernel(n, offsets, *refs):
    blocks, w_ref, outs, scr = refs[: -n - 3], refs[-n - 3], refs[-n - 1 : -1], refs[-1]
    r, h = member(n), lax.axis_index("head")
    width = blocks[0].shape[1]
    dim = outs[0].shape[1]
    total = None
    for offset, ref in zip(offsets, blocks):
        part = mm(ref[...], w_ref[:, lane(h ^ offset, width)], NT)
        total = part if total is None else total + part
    scr[...] = bf(total)
    for k in range(n):
        outs[k][...] = scr[:, lane(r ^ k, dim)]


def first_kernel(n, *refs):
    got, own, om_ref = refs[: n - 1][::-1], refs[n - 1 : n + 2], refs[n + 2]
    qkv_ref, kf_ref, total_ref = refs[n + 4 :]
    r = member(n)
    rows, dim = own[0].shape[0], om_ref.shape[1]
    scale = dim ** (-0.25)
    for k in range(n):
        at = pl.ds(pl.multiple_of((r ^ k) * rows, 128), rows)
        if k:
            qkv_ref[:, at, :] = got[k - 1][...]
        else:
            for i, ref in enumerate(own):
                qkv_ref[i, at, :] = ref[:, lane(r, dim)]
    k_all = qkv_ref[1]
    wide = k_all.astype(jnp.float32)
    half_sq = jnp.sum(wide * wide, axis=1, keepdims=True) * (scale * scale * 0.5)
    kf = bf(jnp.exp(mm(k_all, om_ref[r]) * scale - half_sq))
    kf_ref[...] = kf
    total_ref[...] = bf(mm(qkv_ref[2], kf, TN))


def inner_kernel(rows, qkv_ref, om_ref, kf_ref, qf_ref, scores_ref, num_ref):
    long, dim = num_ref.shape
    n = long // rows
    scale = dim ** (-0.25)
    spans = tiles(long, rows)
    qf = bf(jnp.exp(mm(qkv_ref[0], om_ref[member(n)]) * scale))
    qf_ref[...] = qf
    scores = lower(qf, kf_ref[...], spans)
    for (i, j), tile in scores.items():
        scores_ref[slice(*spans[i]), slice(*spans[j])] = tile
    for (a, b), part in zip(spans, times(lambda i, j: scores[i, j], qkv_ref[2], spans)):
        num_ref[a:b, :] = part


def turn_kernel(n, *refs):
    gm_in, (qf_ref, num_ref), earlier = refs[:n][::-1], refs[n : n + 2], refs[n + 2 : -5]
    carried_ref, gn_ref, total_ref, mixed_ref, scr = refs[-5:]
    r = member(n)
    rows = gm_in[0].shape[0]
    places = [
        pl.ds(pl.multiple_of((r ^ k) * rows, 128), rows) for k in range(n)
    ]
    for k in range(n):
        scr[places[k], :] = gm_in[k][...]
    carried = sum_of_side(earlier, n, True)
    carried_ref[...] = carried
    num = num_ref[...] + mm(qf_ref[...], carried, NT)
    inv = lax.rsqrt(jnp.mean(num * num, axis=1, keepdims=True) + EPSILON)
    normed = num * inv
    gm = scr[...].astype(jnp.float32)
    gn = bf((gm - normed * jnp.mean(gm * normed, axis=1, keepdims=True)) * inv)
    gn_ref[...] = gn
    scr[...] = bf(normed)
    for k in range(n):
        mixed_ref[k] = scr[places[k], :]
    total_ref[...] = bf(mm(gn, qf_ref[...], TN))


def back_kernel(rows, qkv_ref, om_ref, kf_ref, qf_ref, scores_ref, gn_ref, carried_ref,
                mixed_ref, other_ref, gq_ref, gv_ref, gkf_ref, *outs):
    long, dim = gn_ref.shape
    r = member(long // rows)
    for k, out in enumerate(outs):
        out[0] = mixed_ref[k]
        out[1] = other_ref[k]
    scale = dim ** (-0.25)
    spans = tiles(long, rows)
    gn, qf = gn_ref[...], qf_ref[...]
    gs = lower(gn, qkv_ref[2], spans)
    cross = mm(gn, carried_ref[...])
    for (a, b), part in zip(spans, times(lambda i, j: gs[i, j], kf_ref[...], spans)):
        terms = bf((cross[a:b] + part) * qf[a:b].astype(jnp.float32))
        gq_ref[a:b, :] = bf(mm(terms, om_ref[r], NT) * scale)
    for (a, b), part in zip(spans, transposed_times(lambda i, j: gs[i, j], qf, spans)):
        gkf_ref[a:b, :] = part

    def scores_at(i, j):
        return scores_ref[slice(*spans[i]), slice(*spans[j])]

    for (a, b), part in zip(spans, transposed_times(scores_at, gn, spans)):
        gv_ref[a:b, :] = part


def end_kernel(n, qkv_ref, om_ref, kf_ref, gq_ref, gv_ref, gkf_ref, *rest):
    later, outs, (gk_scr, gv_scr) = rest[: -n - 2], rest[-n - 2 : -2], rest[-2:]
    r, dim = member(n), om_ref.shape[1]
    rows = outs[0].shape[1]
    scale = dim ** (-0.25)
    kf, after = kf_ref[...], sum_of_side(later, n, False)
    gv_scr[...] = bf(gv_ref[...] + mm(kf, after, NT))
    gkf = gkf_ref[...] + mm(qkv_ref[2], after)
    terms = bf(gkf * kf.astype(jnp.float32))
    total = jnp.sum(terms.astype(jnp.float32), axis=1, keepdims=True)
    wide = qkv_ref[1].astype(jnp.float32)
    gk_scr[...] = bf(mm(terms, om_ref[r], NT) * scale - total * wide * (scale * scale))
    for k in range(n):
        at = pl.ds(pl.multiple_of((r ^ k) * rows, 128), rows)
        outs[k][0] = gq_ref[at, :]
        outs[k][1] = gk_scr[at, :]
        outs[k][2] = gv_scr[at, :]


def mixed_project_kernel(n, offsets, *refs):
    mixed_in, (w_ref, other_w_ref, _, own_ref, sent_ref, scr) = refs[:n][::-1], refs[n:]
    r, h = member(n), lax.axis_index("head")
    width = own_ref.shape[2]
    dim = mixed_in[0].shape[2]
    half = len(offsets) // 2
    for k in range(n):
        scr[:, :, lane(r ^ k, dim)] = mixed_in[k][...]
    for at, offset in enumerate(offsets):
        cols = lane(h ^ offset, width)
        part = mm(scr[0], w_ref[:, cols]) + mm(scr[1], other_w_ref[:, cols])
        if at < half:
            own_ref[at] = part
        else:
            sent_ref[at - half] = bf(part)


def unpack_kernel(n, *refs):
    got, (*outs, mark_ref, sems) = refs[:n][::-1], refs[n:]
    r = member(n)
    dim = got[0].shape[2]
    copies = [
        pltpu.make_async_copy(got[k].at[at], out.at[:, lane(r ^ k, dim)], sems.at[k, at])
        for k in range(n)
        for at, out in enumerate(outs)
    ]
    for copy in copies:
        copy.start()
    mark_ref[...] = jnp.zeros(mark_ref.shape, mark_ref.dtype)
    for copy in copies:
        copy.wait()


def add_kernel(part_ref, last_ref, _, out_ref):
    out_ref[...] = bf(part_ref[...] + last_ref[...].astype(jnp.float32))


def local(queries, key_vectors, value_vectors, feature_proj, out_weight, grad_output):
    n, dim, feats = feature_proj.shape
    rows, width = grad_output.shape
    split = lax.axis_size("head")
    bits = bits_of(split)
    long = n * rows
    macs = long * dim * feats * 2
    f32 = jnp.float32

    offsets, blocks = [0], [grad_output]
    for bit in reversed(bits):
        blocks = blocks + [swap(b, "head", bit) for b in blocks]
        offsets = offsets + [o ^ bit for o in offsets]
    other_weight = swap(out_weight, "head", 1)
    sends = call(
        functools.partial(pack_kernel, n),
        [struct((3, rows, dim))] * (n - 1),
        queries, key_vectors, value_vectors,
        specs=[ANY] * 3, scratch=[pltpu.SemaphoreType.DMA((n - 1, 3))], vmem=53.62,
    )
    got = exchange(sends)
    (mark,) = call(mark_kernel, [struct((8, 128), f32)], blocks[offsets.index(1)], specs=[ANY], flops=10**10)
    gm_parts = call(
        functools.partial(grad_mixed_kernel, n, offsets),
        [struct((rows, dim))] * n,
        *blocks, out_weight, mark, flops=2 * rows * out_weight.size,
        specs=[VMEM] * (split + 1) + [ANY],
        scratch=[pltpu.VMEM((rows, n * dim), jnp.bfloat16)],
    )
    gm_in = exchange(gm_parts[1:]) + [gm_parts[0]]
    qkv, kf, total = call(
        functools.partial(first_kernel, n),
        [
            struct((3, long, dim)),
            struct((long, feats)),
            struct((dim, feats)),
        ],
        *got, queries, key_vectors, value_vectors, feature_proj, gm_parts[0],
        flops=2 * macs, specs=[VMEM] * (n + 3) + [ANY],
    )
    earlier = swap_totals(total, n)
    qf, scores, num = call(
        functools.partial(inner_kernel, rows),
        [struct((long, feats)), struct((long, long)), struct((long, dim), f32)],
        qkv, feature_proj, kf, flops=4 * macs,
    )
    carried, gn, later_total, mixed = call(
        functools.partial(turn_kernel, n),
        [
            struct((dim, feats)),
            struct((long, dim)),
            struct((dim, feats)),
            struct((n, rows, dim)),
        ],
        *gm_in, qf, num, *earlier, flops=2 * macs,
        scratch=[pltpu.VMEM((long, dim), jnp.bfloat16)],
    )
    after = swap_totals(later_total, n)
    other_mixed = swap(mixed, "head", 1)
    gq, gv_part, gkf_part, *mixed_parts = call(
        functools.partial(back_kernel, rows),
        [struct((long, dim)), struct((long, dim), f32), struct((long, feats), f32)]
        + [struct((2, rows, dim))] * n,
        qkv, feature_proj, kf, qf, scores, gn, carried, mixed, other_mixed, flops=8 * macs,
    )
    mixed_in = exchange(mixed_parts[1:]) + [mixed_parts[0]]
    grads = call(
        functools.partial(end_kernel, n),
        [struct((3, rows, dim))] * n,
        qkv, feature_proj, kf, gq, gv_part, gkf_part, *after, flops=3 * macs,
        scratch=[pltpu.VMEM((long, dim), jnp.bfloat16)] * 2,
    )
    grads_in = exchange(grads[1:]) + [grads[0]]

    order = [o for o in range(0, split, 2) if not o & 2] + [o for o in range(2, split, 4)]
    own, sent = call(
        functools.partial(mixed_project_kernel, n, order),
        [struct((split // 4, rows, width), f32), struct((split // 4, rows, width))],
        *mixed_in, out_weight, other_weight, grads[0], flops=2 * rows * out_weight.size,
        specs=[VMEM] * (n + 2) + [ANY],
        scratch=[pltpu.VMEM((2, rows, n * dim), jnp.bfloat16)],
    )
    part, last = reduce_blocks(own, sent, bits[1:])
    gq, gk, gv, mark = call(
        functools.partial(unpack_kernel, n),
        [struct((rows, n * dim))] * 3 + [struct((8, 128), f32)],
        *grads_in, flops=8 * 10**8,
        out_specs=[ANY] * 3 + [VMEM], scratch=[pltpu.SemaphoreType.DMA((n, 3))],
    )
    (layer_out,) = call(
        add_kernel, [struct((rows, width))], part, last, mark, specs=[VMEM, VMEM, ANY]
    )
    return layer_out, gq, gk, gv


def solution(mesh):
    placed = (
        P("seq", "head"),
        P("seq", "head"),
        P("seq", "head"),
        P("head", None, None),
        P("head", None),
        P("seq", "head"),
    )
    return jax.shard_map(
        local,
        mesh=mesh,
        in_specs=placed,
        out_specs=(P("seq", "head"),) * 4,
        check_vma=False,
    )
```

```python
import functools

import jax
import jax.numpy as jnp
from jax import lax
from jax.experimental import pallas as pl
from jax.experimental.pallas import tpu as pltpu
from jax.sharding import PartitionSpec as P

EPSILON = 1e-05
VMEM = pl.BlockSpec(memory_space=pltpu.VMEM)
ANY = pl.BlockSpec(memory_space=pl.ANY)
NN = (((1,), (0,)), ((), ()))
NT = (((1,), (1,)), ((), ()))
TN = (((0,), (0,)), ((), ()))


def mm(a, b, dims=NN):
    return lax.dot_general(a, b, dims, preferred_element_type=jnp.float32)


def bf(x):
    return x.astype(jnp.bfloat16)


def call(body, outs, *args, flops=0, specs=None, out_specs=None, scratch=(), vmem=32):
    size = sum(a.size * a.dtype.itemsize for a in args)
    size += sum(o.size * o.dtype.itemsize for o in outs)
    return pl.pallas_call(
        body,
        out_shape=outs,
        in_specs=specs or [VMEM] * len(args),
        out_specs=out_specs or [VMEM] * len(outs),
        scratch_shapes=list(scratch),
        cost_estimate=pl.CostEstimate(flops=flops, bytes_accessed=size, transcendentals=0),
        compiler_params=pltpu.CompilerParams(vmem_limit_bytes=int(vmem * 1024 * 1024)),
    )(*args)


def struct(shape, dtype=jnp.bfloat16):
    return jax.ShapeDtypeStruct(shape, dtype)


def tiles(long, rows):
    size = 256 if long % 256 == 0 else rows
    return [(at, at + size) for at in range(0, long, size)]


def causal(scores):
    row = lax.broadcasted_iota(jnp.int32, scores.shape, 0)
    col = lax.broadcasted_iota(jnp.int32, scores.shape, 1)
    return jnp.where(col <= row, scores, 0.0)


def lower(left, right, spans):
    out = {}
    for i, (a, b) in enumerate(spans):
        for j, (c, d) in enumerate(spans[: i + 1]):
            tile = mm(left[a:b], right[c:d], NT)
            out[i, j] = bf(causal(tile) if i == j else tile)
    return out


def times(tile_at, right, spans):
    return [
        sum(mm(tile_at(i, j), right[c:d]) for j, (c, d) in enumerate(spans[: i + 1]))
        for i in range(len(spans))
    ]


def transposed_times(tile_at, right, spans):
    return [
        sum(mm(tile_at(i, j), right[a:b], TN) for i, (a, b) in enumerate(spans) if i >= j)
        for j in range(len(spans))
    ]


def swap(array, axis, bit):
    size = lax.axis_size(axis)
    return lax.ppermute(array, axis, [(i, i ^ bit) for i in range(size)])


def bits_of(size):
    return [1 << b for b in range(size.bit_length() - 1)]


def reduce_blocks(own, sent, bits):
    got = swap(sent, "head", 1)
    for bit in bits[1:]:
        total = own.astype(jnp.float32) + got.astype(jnp.float32)
        pairs = total.reshape((total.shape[0] // 2, 2) + total.shape[1:])
        own, got = pairs[:, 0], swap(bf(pairs[:, 1]), "head", bit)
    return own[0].astype(jnp.float32), got[0]


def member(n):
    return lax.rem(lax.axis_index("seq"), n)


def exchange(parts):
    return [swap(part, "seq", k) for k, part in enumerate(parts, 1)][::-1]


def swap_totals(total, n):
    size, step, got = lax.axis_size("seq"), n, []
    while step < size:
        got.append(swap(bf(total), "seq", step))
        total = total.astype(jnp.float32) + got[-1].astype(jnp.float32)
        step *= 2
    return got


def sum_of_side(refs, n, earlier):
    group = lax.div(lax.axis_index("seq"), n)
    total = jnp.zeros(refs[0].shape, jnp.float32)
    for at, ref in enumerate(refs):
        from_earlier = lax.rem(lax.shift_right_logical(group, at), 2) == 1
        keep = from_earlier if earlier else jnp.logical_not(from_earlier)
        total = total + jnp.where(keep, ref[...].astype(jnp.float32), 0.0)
    return bf(total)


def lane(index, width):
    return pl.ds(pl.multiple_of(index * width, 128), width)


def pack_kernel(n, q_ref, k_ref, v_ref, *rest):
    outs, sems = rest[:-1], rest[-1]
    r = member(n)
    dim = outs[0].shape[2]
    copies = [
        pltpu.make_async_copy(ref.at[:, lane(r ^ k, dim)], out.at[at], sems.at[k - 1, at])
        for k, out in enumerate(outs, 1)
        for at, ref in enumerate((q_ref, k_ref, v_ref))
    ]
    for copy in copies:
        copy.start()
    for copy in copies:
        copy.wait()


def mark_kernel(_, out_ref):
    out_ref[...] = jnp.zeros(out_ref.shape, out_ref.dtype)


def grad_mixed_kernel(n, offsets, *refs):
    blocks, w_ref, outs, scr = refs[: -n - 3], refs[-n - 3], refs[-n - 1 : -1], refs[-1]
    r, h = member(n), lax.axis_index("head")
    width = blocks[0].shape[1]
    dim = outs[0].shape[1]
    total = None
    for offset, ref in zip(offsets, blocks):
        part = mm(ref[...], w_ref[:, lane(h ^ offset, width)], NT)
        total = part if total is None else total + part
    scr[...] = bf(total)
    for k in range(n):
        outs[k][...] = scr[:, lane(r ^ k, dim)]


def first_kernel(n, *refs):
    got, own, om_ref = refs[: n - 1][::-1], refs[n - 1 : n + 2], refs[n + 2]
    qkv_ref, kf_ref, total_ref = refs[n + 4 :]
    r = member(n)
    rows, dim = own[0].shape[0], om_ref.shape[1]
    scale = dim ** (-0.25)
    for k in range(n):
        at = pl.ds(pl.multiple_of((r ^ k) * rows, 128), rows)
        if k:
            qkv_ref[:, at, :] = got[k - 1][...]
        else:
            for i, ref in enumerate(own):
                qkv_ref[i, at, :] = ref[:, lane(r, dim)]
    k_all = qkv_ref[1]
    wide = k_all.astype(jnp.float32)
    half_sq = jnp.sum(wide * wide, axis=1, keepdims=True) * (scale * scale * 0.5)
    kf = bf(jnp.exp(mm(k_all, om_ref[r]) * scale - half_sq))
    kf_ref[...] = kf
    total_ref[...] = bf(mm(qkv_ref[2], kf, TN))


def inner_kernel(n, *refs):
    gm_in, (qkv_ref, om_ref, kf_ref) = refs[:n][::-1], refs[n : n + 3]
    gm_ref, qf_ref, scores_ref, num_ref = refs[n + 3 :]
    long, dim = num_ref.shape
    rows = long // n
    r = member(n)
    for k in range(n):
        gm_ref[pl.ds(pl.multiple_of((r ^ k) * rows, 128), rows), :] = gm_in[k][...]
    scale = dim ** (-0.25)
    spans = tiles(long, rows)
    qf = bf(jnp.exp(mm(qkv_ref[0], om_ref[r]) * scale))
    qf_ref[...] = qf
    scores = lower(qf, kf_ref[...], spans)
    for (i, j), tile in scores.items():
        scores_ref[slice(*spans[i]), slice(*spans[j])] = tile
    for (a, b), part in zip(spans, times(lambda i, j: scores[i, j], qkv_ref[2], spans)):
        num_ref[a:b, :] = part


def turn_kernel(n, *refs):
    gm_ref, qf_ref, num_ref, *earlier = refs[: -n - 4]
    carried_ref, gn_ref, total_ref = refs[-n - 4 : -n - 1]
    outs, scr = refs[-n - 1 : -1], refs[-1]
    r = member(n)
    rows = outs[0].shape[0]
    places = [
        pl.ds(pl.multiple_of((r ^ k) * rows, 128), rows) for k in range(n)
    ]
    carried = sum_of_side(earlier, n, True)
    carried_ref[...] = carried
    num = num_ref[...] + mm(qf_ref[...], carried, NT)
    inv = lax.rsqrt(jnp.mean(num * num, axis=1, keepdims=True) + EPSILON)
    normed = num * inv
    gm = gm_ref[...].astype(jnp.float32)
    gn = bf((gm - normed * jnp.mean(gm * normed, axis=1, keepdims=True)) * inv)
    gn_ref[...] = gn
    scr[...] = bf(normed)
    for k in range(n):
        outs[k][...] = scr[places[k], :]
    total_ref[...] = bf(mm(gn, qf_ref[...], TN))


def back_kernel(rows, qkv_ref, om_ref, kf_ref, qf_ref, scores_ref, gn_ref, carried_ref,
                gq_ref, gv_ref, gkf_ref):
    long, dim = gn_ref.shape
    r = member(long // rows)
    scale = dim ** (-0.25)
    spans = tiles(long, rows)
    gn, qf = gn_ref[...], qf_ref[...]
    gs = lower(gn, qkv_ref[2], spans)
    cross = mm(gn, carried_ref[...])
    for (a, b), part in zip(spans, times(lambda i, j: gs[i, j], kf_ref[...], spans)):
        terms = bf((cross[a:b] + part) * qf[a:b].astype(jnp.float32))
        gq_ref[a:b, :] = bf(mm(terms, om_ref[r], NT) * scale)
    for (a, b), part in zip(spans, transposed_times(lambda i, j: gs[i, j], qf, spans)):
        gkf_ref[a:b, :] = part

    def scores_at(i, j):
        return scores_ref[slice(*spans[i]), slice(*spans[j])]

    for (a, b), part in zip(spans, transposed_times(scores_at, gn, spans)):
        gv_ref[a:b, :] = part


def end_kernel(n, qkv_ref, om_ref, kf_ref, gq_ref, gv_ref, gkf_ref, *rest):
    later, outs, (gk_scr, gv_scr) = rest[: -n - 2], rest[-n - 2 : -2], rest[-2:]
    r, dim = member(n), om_ref.shape[1]
    rows = outs[0].shape[1]
    scale = dim ** (-0.25)
    kf, after = kf_ref[...], sum_of_side(later, n, False)
    gv_scr[...] = bf(gv_ref[...] + mm(kf, after, NT))
    gkf = gkf_ref[...] + mm(qkv_ref[2], after)
    terms = bf(gkf * kf.astype(jnp.float32))
    total = jnp.sum(terms.astype(jnp.float32), axis=1, keepdims=True)
    wide = qkv_ref[1].astype(jnp.float32)
    gk_scr[...] = bf(mm(terms, om_ref[r], NT) * scale - total * wide * (scale * scale))
    for k in range(n):
        at = pl.ds(pl.multiple_of((r ^ k) * rows, 128), rows)
        outs[k][0] = gq_ref[at, :]
        outs[k][1] = gk_scr[at, :]
        outs[k][2] = gv_scr[at, :]


def mixed_project_kernel(n, offsets, *refs):
    mixed_in, (w_ref, _, own_ref, sent_ref, scr) = refs[:n][::-1], refs[n:]
    r, h = member(n), lax.axis_index("head")
    width = own_ref.shape[2]
    dim = mixed_in[0].shape[1]
    half = len(offsets) // 2
    for k in range(n):
        scr[:, lane(r ^ k, dim)] = mixed_in[k][...]
    mixed = scr[...]
    for at, offset in enumerate(offsets):
        part = bf(mm(mixed, w_ref[:, lane(h ^ offset, width)]))
        if at < half:
            own_ref[at] = part
        else:
            sent_ref[at - half] = part


def unpack_kernel(n, *refs):
    got, (part_ref, last_ref) = refs[:n][::-1], refs[n : n + 2]
    (out_ref, *outs), (scr, sems, last_sem) = refs[n + 2 : -3], refs[-3:]
    r = member(n)
    dim = got[0].shape[2]
    copies = [
        pltpu.make_async_copy(got[k].at[at], out.at[:, lane(r ^ k, dim)], sems.at[k, at])
        for k in range(n)
        for at, out in enumerate(outs)
    ]
    for copy in copies:
        copy.start()
    scr[...] = bf(part_ref[...] + last_ref[...].astype(jnp.float32))
    copies.append(pltpu.make_async_copy(scr, out_ref, last_sem))
    copies[-1].start()
    for copy in copies:
        copy.wait()


def local(queries, key_vectors, value_vectors, feature_proj, out_weight, grad_output):
    n, dim, feats = feature_proj.shape
    rows, width = grad_output.shape
    split = lax.axis_size("head")
    bits = bits_of(split)
    long = n * rows
    macs = long * dim * feats * 2
    f32 = jnp.float32

    offsets, blocks = [0], [grad_output]
    for bit in reversed(bits):
        blocks = blocks + [swap(b, "head", bit) for b in blocks]
        offsets = offsets + [o ^ bit for o in offsets]
    sends = call(
        functools.partial(pack_kernel, n),
        [struct((3, rows, dim))] * (n - 1),
        queries, key_vectors, value_vectors,
        specs=[ANY] * 3, scratch=[pltpu.SemaphoreType.DMA((n - 1, 3))], vmem=53.62,
    )
    got = exchange(sends)
    (mark,) = call(mark_kernel, [struct((8, 128), f32)], blocks[offsets.index(1)], specs=[ANY], flops=10**10)
    gm_parts = call(
        functools.partial(grad_mixed_kernel, n, offsets),
        [struct((rows, dim))] * n,
        *blocks, out_weight, mark, flops=2 * rows * out_weight.size,
        specs=[VMEM] * (split + 1) + [ANY],
        scratch=[pltpu.VMEM((rows, n * dim), jnp.bfloat16)],
    )
    gm_in = exchange(gm_parts[1:]) + [gm_parts[0]]
    qkv, kf, total = call(
        functools.partial(first_kernel, n),
        [
            struct((3, long, dim)),
            struct((long, feats)),
            struct((dim, feats)),
        ],
        *got, queries, key_vectors, value_vectors, feature_proj, gm_parts[0],
        flops=2 * macs, specs=[VMEM] * (n + 3) + [ANY],
    )
    earlier = swap_totals(total, n)
    gm, qf, scores, num = call(
        functools.partial(inner_kernel, n),
        [struct((long, dim)), struct((long, feats)), struct((long, long)), struct((long, dim), f32)],
        *gm_in, qkv, feature_proj, kf, flops=16 * macs,
    )
    carried, gn, later_total, *mixed_parts = call(
        functools.partial(turn_kernel, n),
        [
            struct((dim, feats)),
            struct((long, dim)),
            struct((dim, feats)),
        ]
        + [struct((rows, dim))] * n,
        gm, qf, num, *earlier, flops=2 * macs,
        scratch=[pltpu.VMEM((long, dim), jnp.bfloat16)],
    )
    after = swap_totals(later_total, n)
    mixed_in = exchange(mixed_parts[1:]) + [mixed_parts[0]]
    gq, gv_part, gkf_part = call(
        functools.partial(back_kernel, rows),
        [struct((long, dim)), struct((long, dim), f32), struct((long, feats), f32)],
        qkv, feature_proj, kf, qf, scores, gn, carried, flops=8 * macs,
    )
    grads = call(
        functools.partial(end_kernel, n),
        [struct((3, rows, dim))] * n,
        qkv, feature_proj, kf, gq, gv_part, gkf_part, *after, flops=3 * macs,
        scratch=[pltpu.VMEM((long, dim), jnp.bfloat16)] * 2,
    )
    grads_in = exchange(grads[1:]) + [grads[0]]

    order = [o for o in range(split) if not o & 1] + [o for o in range(split) if o & 1]
    own, sent = call(
        functools.partial(mixed_project_kernel, n, order),
        [struct((split // 2, rows, width))] * 2,
        *mixed_in, out_weight, grads[0], flops=2 * rows * out_weight.size,
        specs=[VMEM] * (n + 1) + [ANY],
        scratch=[pltpu.VMEM((rows, n * dim), jnp.bfloat16)],
    )
    part, last = reduce_blocks(own, sent, bits)
    return call(
        functools.partial(unpack_kernel, n),
        [struct((rows, width))] + [struct((rows, n * dim))] * 3,
        *grads_in, part, last,
        out_specs=[ANY] * 4,
        scratch=[
            pltpu.VMEM((rows, width), jnp.bfloat16),
            pltpu.SemaphoreType.DMA((n, 3)),
            pltpu.SemaphoreType.DMA,
        ],
    )


def solution(mesh):
    placed = (
        P("seq", "head"),
        P("seq", "head"),
        P("seq", "head"),
        P("head", None, None),
        P("head", None),
        P("seq", "head"),
    )
    return jax.shard_map(
        local,
        mesh=mesh,
        in_specs=placed,
        out_specs=(P("seq", "head"),) * 4,
        check_vma=False,
    )
```

```python
import functools

import jax
import jax.numpy as jnp
from jax import lax
from jax.experimental import pallas as pl
from jax.experimental.pallas import tpu as pltpu
from jax.sharding import PartitionSpec as P

EPSILON = 1e-05
VMEM = pl.BlockSpec(memory_space=pltpu.VMEM)
ANY = pl.BlockSpec(memory_space=pl.ANY)
NN = (((1,), (0,)), ((), ()))
NT = (((1,), (1,)), ((), ()))
TN = (((0,), (0,)), ((), ()))


def mm(a, b, dims=NN):
    return lax.dot_general(a, b, dims, preferred_element_type=jnp.float32)


def bf(x):
    return x.astype(jnp.bfloat16)


def call(body, outs, *args, flops=0, specs=None, out_specs=None, scratch=(), vmem=32):
    size = sum(a.size * a.dtype.itemsize for a in args)
    size += sum(o.size * o.dtype.itemsize for o in outs)
    return pl.pallas_call(
        body,
        out_shape=outs,
        in_specs=specs or [VMEM] * len(args),
        out_specs=out_specs or [VMEM] * len(outs),
        scratch_shapes=list(scratch),
        cost_estimate=pl.CostEstimate(flops=flops, bytes_accessed=size, transcendentals=0),
        compiler_params=pltpu.CompilerParams(vmem_limit_bytes=int(vmem * 1024 * 1024)),
    )(*args)


def struct(shape, dtype=jnp.bfloat16):
    return jax.ShapeDtypeStruct(shape, dtype)


def tiles(long, rows):
    size = 256 if long % 256 == 0 else rows
    return [(at, at + size) for at in range(0, long, size)]


def causal(scores):
    row = lax.broadcasted_iota(jnp.int32, scores.shape, 0)
    col = lax.broadcasted_iota(jnp.int32, scores.shape, 1)
    return jnp.where(col <= row, scores, 0.0)


def lower(left, right, spans):
    out = {}
    for i, (a, b) in enumerate(spans):
        for j, (c, d) in enumerate(spans[: i + 1]):
            tile = mm(left[a:b], right[c:d], NT)
            out[i, j] = bf(causal(tile) if i == j else tile)
    return out


def times(tile_at, right, spans):
    return [
        sum(mm(tile_at(i, j), right[c:d]) for j, (c, d) in enumerate(spans[: i + 1]))
        for i in range(len(spans))
    ]


def transposed_times(tile_at, right, spans):
    return [
        sum(mm(tile_at(i, j), right[a:b], TN) for i, (a, b) in enumerate(spans) if i >= j)
        for j in range(len(spans))
    ]


def swap(array, axis, bit):
    size = lax.axis_size(axis)
    return lax.ppermute(array, axis, [(i, i ^ bit) for i in range(size)])


def bits_of(size):
    return [1 << b for b in range(size.bit_length() - 1)]


def reduce_blocks(own, sent, bits):
    got = swap(sent, "head", bits[0])
    for bit in bits[1:]:
        total = own + got.astype(jnp.float32)
        pairs = total.reshape((total.shape[0] // 2, 2) + total.shape[1:])
        own, got = pairs[:, 0], swap(bf(pairs[:, 1]), "head", bit)
    return own[0], got[0]


def member(n):
    return lax.rem(lax.axis_index("seq"), n)


def exchange(parts):
    return [swap(part, "seq", k) for k, part in enumerate(parts, 1)][::-1]


def swap_totals(total, n):
    size, step, got = lax.axis_size("seq"), n, []
    while step < size:
        got.append(swap(bf(total), "seq", step))
        total = total.astype(jnp.float32) + got[-1].astype(jnp.float32)
        step *= 2
    return got


def sum_of_side(refs, n, earlier):
    group = lax.div(lax.axis_index("seq"), n)
    total = jnp.zeros(refs[0].shape, jnp.float32)
    for at, ref in enumerate(refs):
        from_earlier = lax.rem(lax.shift_right_logical(group, at), 2) == 1
        keep = from_earlier if earlier else jnp.logical_not(from_earlier)
        total = total + jnp.where(keep, ref[...].astype(jnp.float32), 0.0)
    return bf(total)


def lane(index, width):
    return pl.ds(pl.multiple_of(index * width, 128), width)


def pack_kernel(n, q_ref, k_ref, v_ref, *rest):
    outs, sems = rest[:-1], rest[-1]
    r = member(n)
    dim = outs[0].shape[2]
    copies = [
        pltpu.make_async_copy(ref.at[:, lane(r ^ k, dim)], out.at[at], sems.at[k - 1, at])
        for k, out in enumerate(outs, 1)
        for at, ref in enumerate((q_ref, k_ref, v_ref))
    ]
    for copy in copies:
        copy.start()
    for copy in copies:
        copy.wait()


def mark_kernel(_, out_ref):
    out_ref[...] = jnp.zeros(out_ref.shape, out_ref.dtype)


def grad_mixed_kernel(n, offsets, *refs):
    blocks, w_ref, outs, scr = refs[: -n - 3], refs[-n - 3], refs[-n - 1 : -1], refs[-1]
    r, h = member(n), lax.axis_index("head")
    width = blocks[0].shape[1]
    dim = outs[0].shape[1]
    total = None
    for offset, ref in zip(offsets, blocks):
        part = mm(ref[...], w_ref[:, lane(h ^ offset, width)], NT)
        total = part if total is None else total + part
    scr[...] = bf(total)
    for k in range(n):
        outs[k][...] = scr[:, lane(r ^ k, dim)]


def first_kernel(n, *refs):
    got, own, om_ref = refs[: n - 1][::-1], refs[n - 1 : n + 2], refs[n + 2]
    qkv_ref, kf_ref, total_ref = refs[n + 4 :]
    r = member(n)
    rows, dim = own[0].shape[0], om_ref.shape[1]
    scale = dim ** (-0.25)
    for k in range(n):
        at = pl.ds(pl.multiple_of((r ^ k) * rows, 128), rows)
        if k:
            qkv_ref[:, at, :] = got[k - 1][...]
        else:
            for i, ref in enumerate(own):
                qkv_ref[i, at, :] = ref[:, lane(r, dim)]
    k_all = qkv_ref[1]
    wide = k_all.astype(jnp.float32)
    half_sq = jnp.sum(wide * wide, axis=1, keepdims=True) * (scale * scale * 0.5)
    kf = bf(jnp.exp(mm(k_all, om_ref[r]) * scale - half_sq))
    kf_ref[...] = kf
    total_ref[...] = bf(mm(qkv_ref[2], kf, TN))


def inner_kernel(n, *refs):
    gm_in, (qkv_ref, om_ref, kf_ref) = refs[:n][::-1], refs[n : n + 3]
    gm_ref, qf_ref, scores_ref, num_ref = refs[n + 3 :]
    long, dim = num_ref.shape
    rows = long // n
    r = member(n)
    for k in range(n):
        gm_ref[pl.ds(pl.multiple_of((r ^ k) * rows, 128), rows), :] = gm_in[k][...]
    scale = dim ** (-0.25)
    spans = tiles(long, rows)
    qf = bf(jnp.exp(mm(qkv_ref[0], om_ref[r]) * scale))
    qf_ref[...] = qf
    scores = lower(qf, kf_ref[...], spans)
    for (i, j), tile in scores.items():
        scores_ref[slice(*spans[i]), slice(*spans[j])] = tile
    for (a, b), part in zip(spans, times(lambda i, j: scores[i, j], qkv_ref[2], spans)):
        num_ref[a:b, :] = part


def turn_kernel(n, *refs):
    gm_ref, qf_ref, num_ref, *earlier = refs[:-5]
    carried_ref, gn_ref, total_ref, mixed_ref, scr = refs[-5:]
    r = member(n)
    rows = mixed_ref.shape[1]
    places = [
        pl.ds(pl.multiple_of((r ^ k) * rows, 128), rows) for k in range(n)
    ]
    carried = sum_of_side(earlier, n, True)
    carried_ref[...] = carried
    num = num_ref[...] + mm(qf_ref[...], carried, NT)
    inv = lax.rsqrt(jnp.mean(num * num, axis=1, keepdims=True) + EPSILON)
    normed = num * inv
    gm = gm_ref[...].astype(jnp.float32)
    gn = bf((gm - normed * jnp.mean(gm * normed, axis=1, keepdims=True)) * inv)
    gn_ref[...] = gn
    scr[...] = bf(normed)
    for k in range(n):
        mixed_ref[k] = scr[places[k], :]
    total_ref[...] = bf(mm(gn, qf_ref[...], TN))


def back_kernel(rows, qkv_ref, om_ref, kf_ref, qf_ref, scores_ref, gn_ref, carried_ref,
                mixed_ref, other_ref, gq_ref, gv_ref, gkf_ref, *outs):
    long, dim = gn_ref.shape
    r = member(long // rows)
    for k, out in enumerate(outs):
        out[0] = mixed_ref[k]
        out[1] = other_ref[k]
    scale = dim ** (-0.25)
    spans = tiles(long, rows)
    gn, qf = gn_ref[...], qf_ref[...]
    gs = lower(gn, qkv_ref[2], spans)
    cross = mm(gn, carried_ref[...])
    for (a, b), part in zip(spans, times(lambda i, j: gs[i, j], kf_ref[...], spans)):
        terms = bf((cross[a:b] + part) * qf[a:b].astype(jnp.float32))
        gq_ref[a:b, :] = bf(mm(terms, om_ref[r], NT) * scale)
    for (a, b), part in zip(spans, transposed_times(lambda i, j: gs[i, j], qf, spans)):
        gkf_ref[a:b, :] = part

    def scores_at(i, j):
        return scores_ref[slice(*spans[i]), slice(*spans[j])]

    for (a, b), part in zip(spans, transposed_times(scores_at, gn, spans)):
        gv_ref[a:b, :] = part


def end_kernel(n, qkv_ref, om_ref, kf_ref, gq_ref, gv_ref, gkf_ref, *rest):
    later, outs, (gk_scr, gv_scr) = rest[: -n - 2], rest[-n - 2 : -2], rest[-2:]
    r, dim = member(n), om_ref.shape[1]
    rows = outs[0].shape[1]
    scale = dim ** (-0.25)
    kf, after = kf_ref[...], sum_of_side(later, n, False)
    gv_scr[...] = bf(gv_ref[...] + mm(kf, after, NT))
    gkf = gkf_ref[...] + mm(qkv_ref[2], after)
    terms = bf(gkf * kf.astype(jnp.float32))
    total = jnp.sum(terms.astype(jnp.float32), axis=1, keepdims=True)
    wide = qkv_ref[1].astype(jnp.float32)
    gk_scr[...] = bf(mm(terms, om_ref[r], NT) * scale - total * wide * (scale * scale))
    for k in range(n):
        at = pl.ds(pl.multiple_of((r ^ k) * rows, 128), rows)
        outs[k][0] = gq_ref[at, :]
        outs[k][1] = gk_scr[at, :]
        outs[k][2] = gv_scr[at, :]


def mixed_project_kernel(n, offsets, *refs):
    mixed_in, (w_ref, other_w_ref, _, own_ref, sent_ref, scr) = refs[:n][::-1], refs[n:]
    r, h = member(n), lax.axis_index("head")
    width = own_ref.shape[2]
    dim = mixed_in[0].shape[2]
    half = len(offsets) // 2
    for k in range(n):
        scr[:, :, lane(r ^ k, dim)] = mixed_in[k][...]
    for at, offset in enumerate(offsets):
        cols = lane(h ^ offset, width)
        part = mm(scr[0], w_ref[:, cols]) + mm(scr[1], other_w_ref[:, cols])
        if at < half:
            own_ref[at] = part
        else:
            sent_ref[at - half] = bf(part)


def unpack_kernel(n, *refs):
    got, (*outs, mark_ref, sems) = refs[:n][::-1], refs[n:]
    r = member(n)
    dim = got[0].shape[2]
    copies = [
        pltpu.make_async_copy(got[k].at[at], out.at[:, lane(r ^ k, dim)], sems.at[k, at])
        for k in range(n)
        for at, out in enumerate(outs)
    ]
    for copy in copies:
        copy.start()
    mark_ref[...] = jnp.zeros(mark_ref.shape, mark_ref.dtype)
    for copy in copies:
        copy.wait()


def add_kernel(part_ref, last_ref, _, out_ref):
    out_ref[...] = bf(part_ref[...] + last_ref[...].astype(jnp.float32))


def local(queries, key_vectors, value_vectors, feature_proj, out_weight, grad_output):
    n, dim, feats = feature_proj.shape
    rows, width = grad_output.shape
    split = lax.axis_size("head")
    bits = bits_of(split)
    long = n * rows
    macs = long * dim * feats * 2
    f32 = jnp.float32

    offsets, blocks = [0], [grad_output]
    for bit in reversed(bits):
        blocks = blocks + [swap(b, "head", bit) for b in blocks]
        offsets = offsets + [o ^ bit for o in offsets]
    sends = call(
        functools.partial(pack_kernel, n),
        [struct((3, rows, dim))] * (n - 1),
        queries, key_vectors, value_vectors,
        specs=[ANY] * 3, scratch=[pltpu.SemaphoreType.DMA((n - 1, 3))], vmem=53.62,
    )
    got = exchange(sends)
    (mark,) = call(mark_kernel, [struct((8, 128), f32)], blocks[offsets.index(1)], specs=[ANY], flops=10**10)
    gm_parts = call(
        functools.partial(grad_mixed_kernel, n, offsets),
        [struct((rows, dim))] * n,
        *blocks, out_weight, mark, flops=2 * rows * out_weight.size,
        specs=[VMEM] * (split + 1) + [ANY],
        scratch=[pltpu.VMEM((rows, n * dim), jnp.bfloat16)],
    )
    gm_in = exchange(gm_parts[1:]) + [gm_parts[0]]
    qkv, kf, total = call(
        functools.partial(first_kernel, n),
        [
            struct((3, long, dim)),
            struct((long, feats)),
            struct((dim, feats)),
        ],
        *got, queries, key_vectors, value_vectors, feature_proj, gm_parts[0],
        flops=2 * macs, specs=[VMEM] * (n + 3) + [ANY],
    )
    earlier = swap_totals(total, n)
    gm, qf, scores, num = call(
        functools.partial(inner_kernel, n),
        [struct((long, dim)), struct((long, feats)), struct((long, long)), struct((long, dim), f32)],
        *gm_in, qkv, feature_proj, kf, flops=16 * macs,
    )
    carried, gn, later_total, mixed = call(
        functools.partial(turn_kernel, n),
        [
            struct((dim, feats)),
            struct((long, dim)),
            struct((dim, feats)),
            struct((n, rows, dim)),
        ],
        gm, qf, num, *earlier, flops=2 * macs,
        scratch=[pltpu.VMEM((long, dim), jnp.bfloat16)],
    )
    after = swap_totals(later_total, n)
    other_mixed = swap(mixed, "head", 1)
    gq, gv_part, gkf_part, *mixed_parts = call(
        functools.partial(back_kernel, rows),
        [struct((long, dim)), struct((long, dim), f32), struct((long, feats), f32)]
        + [struct((2, rows, dim))] * n,
        qkv, feature_proj, kf, qf, scores, gn, carried, mixed, other_mixed, flops=8 * macs,
    )
    mixed_in = exchange(mixed_parts[1:]) + [mixed_parts[0]]
    grads = call(
        functools.partial(end_kernel, n),
        [struct((3, rows, dim))] * n,
        qkv, feature_proj, kf, gq, gv_part, gkf_part, *after, flops=3 * macs,
        scratch=[pltpu.VMEM((long, dim), jnp.bfloat16)] * 2,
    )
    grads_in = exchange(grads[1:]) + [grads[0]]

    held, _ = lax.optimization_barrier((out_weight, gn))
    other_weight = swap(held, "head", 1)
    order = [o for o in range(0, split, 2) if not o & 2] + [o for o in range(2, split, 4)]
    own, sent = call(
        functools.partial(mixed_project_kernel, n, order),
        [struct((split // 4, rows, width), f32), struct((split // 4, rows, width))],
        *mixed_in, out_weight, other_weight, grads[0], flops=2 * rows * out_weight.size,
        specs=[VMEM] * (n + 2) + [ANY],
        scratch=[pltpu.VMEM((2, rows, n * dim), jnp.bfloat16)],
    )
    part, last = reduce_blocks(own, sent, bits[1:])
    gq, gk, gv, mark = call(
        functools.partial(unpack_kernel, n),
        [struct((rows, n * dim))] * 3 + [struct((8, 128), f32)],
        *grads_in, flops=8 * 10**8,
        out_specs=[ANY] * 3 + [VMEM], scratch=[pltpu.SemaphoreType.DMA((n, 3))],
    )
    (layer_out,) = call(
        add_kernel, [struct((rows, width))], part, last, mark, specs=[VMEM, VMEM, ANY]
    )
    return layer_out, gq, gk, gv


def solution(mesh):
    placed = (
        P("seq", "head"),
        P("seq", "head"),
        P("seq", "head"),
        P("head", None, None),
        P("head", None),
        P("seq", "head"),
    )
    return jax.shard_map(
        local,
        mesh=mesh,
        in_specs=placed,
        out_specs=(P("seq", "head"),) * 4,
        check_vma=False,
    )
```

```python
import functools

import jax
import jax.numpy as jnp
from jax import lax
from jax.experimental import pallas as pl
from jax.experimental.pallas import tpu as pltpu
from jax.sharding import PartitionSpec as P

EPSILON = 1e-05
VMEM = pl.BlockSpec(memory_space=pltpu.VMEM)
ANY = pl.BlockSpec(memory_space=pl.ANY)
NN = (((1,), (0,)), ((), ()))
NT = (((1,), (1,)), ((), ()))
TN = (((0,), (0,)), ((), ()))


def mm(a, b, dims=NN):
    return lax.dot_general(a, b, dims, preferred_element_type=jnp.float32)


def bf(x):
    return x.astype(jnp.bfloat16)


def call(body, outs, *args, flops=0, specs=None, out_specs=None, scratch=(), vmem=32):
    size = sum(a.size * a.dtype.itemsize for a in args)
    size += sum(o.size * o.dtype.itemsize for o in outs)
    return pl.pallas_call(
        body,
        out_shape=outs,
        in_specs=specs or [VMEM] * len(args),
        out_specs=out_specs or [VMEM] * len(outs),
        scratch_shapes=list(scratch),
        cost_estimate=pl.CostEstimate(flops=flops, bytes_accessed=size, transcendentals=0),
        compiler_params=pltpu.CompilerParams(vmem_limit_bytes=int(vmem * 1024 * 1024)),
    )(*args)


def struct(shape, dtype=jnp.bfloat16):
    return jax.ShapeDtypeStruct(shape, dtype)


def tiles(long, rows):
    size = 256 if long % 256 == 0 else rows
    return [(at, at + size) for at in range(0, long, size)]


def causal(scores):
    row = lax.broadcasted_iota(jnp.int32, scores.shape, 0)
    col = lax.broadcasted_iota(jnp.int32, scores.shape, 1)
    return jnp.where(col <= row, scores, 0.0)


def lower(left, right, spans):
    out = {}
    for i, (a, b) in enumerate(spans):
        for j, (c, d) in enumerate(spans[: i + 1]):
            tile = mm(left[a:b], right[c:d], NT)
            out[i, j] = bf(causal(tile) if i == j else tile)
    return out


def times(tile_at, right, spans):
    return [
        sum(mm(tile_at(i, j), right[c:d]) for j, (c, d) in enumerate(spans[: i + 1]))
        for i in range(len(spans))
    ]


def transposed_times(tile_at, right, spans):
    return [
        sum(mm(tile_at(i, j), right[a:b], TN) for i, (a, b) in enumerate(spans) if i >= j)
        for j in range(len(spans))
    ]


def swap(array, axis, bit):
    size = lax.axis_size(axis)
    return lax.ppermute(array, axis, [(i, i ^ bit) for i in range(size)])


def bits_of(size):
    return [1 << b for b in range(size.bit_length() - 1)]


def reduce_blocks(own, sent, bits):
    got = swap(sent, "head", 1)
    for bit in bits[1:]:
        total = own.astype(jnp.float32) + got.astype(jnp.float32)
        pairs = total.reshape((total.shape[0] // 2, 2) + total.shape[1:])
        own, got = pairs[:, 0], swap(bf(pairs[:, 1]), "head", bit)
    return own[0].astype(jnp.float32), got[0]


def member(n):
    return lax.rem(lax.axis_index("seq"), n)


def exchange(parts):
    return [swap(part, "seq", k) for k, part in enumerate(parts, 1)][::-1]


def swap_totals(total, n):
    size, step, got = lax.axis_size("seq"), n, []
    while step < size:
        got.append(swap(bf(total), "seq", step))
        total = total.astype(jnp.float32) + got[-1].astype(jnp.float32)
        step *= 2
    return got


def sum_of_side(refs, n, earlier):
    group = lax.div(lax.axis_index("seq"), n)
    total = jnp.zeros(refs[0].shape, jnp.float32)
    for at, ref in enumerate(refs):
        from_earlier = lax.rem(lax.shift_right_logical(group, at), 2) == 1
        keep = from_earlier if earlier else jnp.logical_not(from_earlier)
        total = total + jnp.where(keep, ref[...].astype(jnp.float32), 0.0)
    return bf(total)


def lane(index, width):
    return pl.ds(pl.multiple_of(index * width, 128), width)


def pack_kernel(n, q_ref, k_ref, v_ref, *rest):
    outs, sems = rest[:-1], rest[-1]
    r = member(n)
    dim = outs[0].shape[2]
    copies = [
        pltpu.make_async_copy(ref.at[:, lane(r ^ k, dim)], out.at[at], sems.at[k - 1, at])
        for k, out in enumerate(outs, 1)
        for at, ref in enumerate((q_ref, k_ref, v_ref))
    ]
    for copy in copies:
        copy.start()
    for copy in copies:
        copy.wait()


def mark_kernel(_, out_ref):
    out_ref[...] = jnp.zeros(out_ref.shape, out_ref.dtype)


def grad_mixed_kernel(n, offsets, *refs):
    blocks, w_ref, outs, scr = refs[: -n - 3], refs[-n - 3], refs[-n - 1 : -1], refs[-1]
    r, h = member(n), lax.axis_index("head")
    width = blocks[0].shape[1]
    dim = outs[0].shape[1]
    total = None
    for offset, ref in zip(offsets, blocks):
        part = mm(ref[...], w_ref[:, lane(h ^ offset, width)], NT)
        total = part if total is None else total + part
    scr[...] = bf(total)
    for k in range(n):
        outs[k][...] = scr[:, lane(r ^ k, dim)]


def first_kernel(n, *refs):
    got, own, om_ref = refs[: n - 1][::-1], refs[n - 1 : n + 2], refs[n + 2]
    qkv_ref, kf_ref, total_ref = refs[n + 4 :]
    r = member(n)
    rows, dim = own[0].shape[0], om_ref.shape[1]
    scale = dim ** (-0.25)
    for k in range(n):
        at = pl.ds(pl.multiple_of((r ^ k) * rows, 128), rows)
        if k:
            qkv_ref[:, at, :] = got[k - 1][...]
        else:
            for i, ref in enumerate(own):
                qkv_ref[i, at, :] = ref[:, lane(r, dim)]
    k_all = qkv_ref[1]
    wide = k_all.astype(jnp.float32)
    half_sq = jnp.sum(wide * wide, axis=1, keepdims=True) * (scale * scale * 0.5)
    kf = bf(jnp.exp(mm(k_all, om_ref[r]) * scale - half_sq))
    kf_ref[...] = kf
    total_ref[...] = bf(mm(qkv_ref[2], kf, TN))


def inner_kernel(n, *refs):
    own, (qkv_ref, om_ref, kf_ref) = refs[: n - 1][::-1], refs[n - 1 : n + 2]
    gm_in = own[:1] + own
    gm_ref, qf_ref, scores_ref, num_ref = refs[n + 2 :]
    long, dim = num_ref.shape
    rows = long // n
    r = member(n)
    for k in range(n):
        gm_ref[pl.ds(pl.multiple_of((r ^ k) * rows, 128), rows), :] = gm_in[k][...]
    scale = dim ** (-0.25)
    spans = tiles(long, rows)
    qf = bf(jnp.exp(mm(qkv_ref[0], om_ref[r]) * scale))
    qf_ref[...] = qf
    scores = lower(qf, kf_ref[...], spans)
    for (i, j), tile in scores.items():
        scores_ref[slice(*spans[i]), slice(*spans[j])] = tile
    for (a, b), part in zip(spans, times(lambda i, j: scores[i, j], qkv_ref[2], spans)):
        num_ref[a:b, :] = part


def turn_kernel(n, *refs):
    gm_ref, late_ref, qf_ref, num_ref, *earlier = refs[: -n - 4]
    carried_ref, gn_ref, total_ref = refs[-n - 4 : -n - 1]
    outs, scr = refs[-n - 1 : -1], refs[-1]
    r = member(n)
    rows = outs[0].shape[0]
    places = [
        pl.ds(pl.multiple_of((r ^ k) * rows, 128), rows) for k in range(n)
    ]
    scr[...] = gm_ref[...]
    scr[places[1], :] = late_ref[...]
    carried = sum_of_side(earlier, n, True)
    carried_ref[...] = carried
    num = num_ref[...] + mm(qf_ref[...], carried, NT)
    inv = lax.rsqrt(jnp.mean(num * num, axis=1, keepdims=True) + EPSILON)
    normed = num * inv
    gm = scr[...].astype(jnp.float32)
    gn = bf((gm - normed * jnp.mean(gm * normed, axis=1, keepdims=True)) * inv)
    gn_ref[...] = gn
    scr[...] = bf(normed)
    for k in range(n):
        outs[k][...] = scr[places[k], :]
    total_ref[...] = bf(mm(gn, qf_ref[...], TN))


def back_kernel(rows, qkv_ref, om_ref, kf_ref, qf_ref, scores_ref, gn_ref, carried_ref,
                gq_ref, gv_ref, gkf_ref):
    long, dim = gn_ref.shape
    r = member(long // rows)
    scale = dim ** (-0.25)
    spans = tiles(long, rows)
    gn, qf = gn_ref[...], qf_ref[...]
    gs = lower(gn, qkv_ref[2], spans)
    cross = mm(gn, carried_ref[...])
    for (a, b), part in zip(spans, times(lambda i, j: gs[i, j], kf_ref[...], spans)):
        terms = bf((cross[a:b] + part) * qf[a:b].astype(jnp.float32))
        gq_ref[a:b, :] = bf(mm(terms, om_ref[r], NT) * scale)
    for (a, b), part in zip(spans, transposed_times(lambda i, j: gs[i, j], qf, spans)):
        gkf_ref[a:b, :] = part

    def scores_at(i, j):
        return scores_ref[slice(*spans[i]), slice(*spans[j])]

    for (a, b), part in zip(spans, transposed_times(scores_at, gn, spans)):
        gv_ref[a:b, :] = part


def end_kernel(n, qkv_ref, om_ref, kf_ref, gq_ref, gv_ref, gkf_ref, *rest):
    later, outs, (gk_scr, gv_scr) = rest[: -n - 2], rest[-n - 2 : -2], rest[-2:]
    r, dim = member(n), om_ref.shape[1]
    rows = outs[0].shape[1]
    scale = dim ** (-0.25)
    kf, after = kf_ref[...], sum_of_side(later, n, False)
    gv_scr[...] = bf(gv_ref[...] + mm(kf, after, NT))
    gkf = gkf_ref[...] + mm(qkv_ref[2], after)
    terms = bf(gkf * kf.astype(jnp.float32))
    total = jnp.sum(terms.astype(jnp.float32), axis=1, keepdims=True)
    wide = qkv_ref[1].astype(jnp.float32)
    gk_scr[...] = bf(mm(terms, om_ref[r], NT) * scale - total * wide * (scale * scale))
    for k in range(n):
        at = pl.ds(pl.multiple_of((r ^ k) * rows, 128), rows)
        outs[k][0] = gq_ref[at, :]
        outs[k][1] = gk_scr[at, :]
        outs[k][2] = gv_scr[at, :]


def mixed_project_kernel(n, offsets, *refs):
    mixed_in, (w_ref, _, own_ref, sent_ref, scr) = refs[:n][::-1], refs[n:]
    r, h = member(n), lax.axis_index("head")
    width = own_ref.shape[2]
    dim = mixed_in[0].shape[1]
    half = len(offsets) // 2
    for k in range(n):
        scr[:, lane(r ^ k, dim)] = mixed_in[k][...]
    mixed = scr[...]
    for at, offset in enumerate(offsets):
        part = bf(mm(mixed, w_ref[:, lane(h ^ offset, width)]))
        if at < half:
            own_ref[at] = part
        else:
            sent_ref[at - half] = part


def unpack_kernel(n, *refs):
    got, (part_ref, last_ref) = refs[:n][::-1], refs[n : n + 2]
    (out_ref, *outs), (scr, sems, last_sem) = refs[n + 2 : -3], refs[-3:]
    r = member(n)
    dim = got[0].shape[2]
    copies = [
        pltpu.make_async_copy(got[k].at[at], out.at[:, lane(r ^ k, dim)], sems.at[k, at])
        for k in range(n)
        for at, out in enumerate(outs)
    ]
    for copy in copies:
        copy.start()
    scr[...] = bf(part_ref[...] + last_ref[...].astype(jnp.float32))
    copies.append(pltpu.make_async_copy(scr, out_ref, last_sem))
    copies[-1].start()
    for copy in copies:
        copy.wait()


def local(queries, key_vectors, value_vectors, feature_proj, out_weight, grad_output):
    n, dim, feats = feature_proj.shape
    rows, width = grad_output.shape
    split = lax.axis_size("head")
    bits = bits_of(split)
    long = n * rows
    macs = long * dim * feats * 2
    f32 = jnp.float32

    offsets, blocks = [0], [grad_output]
    for bit in reversed(bits):
        blocks = blocks + [swap(b, "head", bit) for b in blocks]
        offsets = offsets + [o ^ bit for o in offsets]
    sends = call(
        functools.partial(pack_kernel, n),
        [struct((3, rows, dim))] * (n - 1),
        queries, key_vectors, value_vectors,
        specs=[ANY] * 3, scratch=[pltpu.SemaphoreType.DMA((n - 1, 3))], vmem=53.62,
    )
    got = exchange(sends)
    (mark,) = call(mark_kernel, [struct((8, 128), f32)], blocks[offsets.index(1)], specs=[ANY], flops=10**10)
    gm_parts = call(
        functools.partial(grad_mixed_kernel, n, offsets),
        [struct((rows, dim))] * n,
        *blocks, out_weight, mark, flops=2 * rows * out_weight.size,
        specs=[VMEM] * (split + 1) + [ANY],
        scratch=[pltpu.VMEM((rows, n * dim), jnp.bfloat16)],
    )
    gm_in = exchange(gm_parts[1:]) + [gm_parts[0]]
    qkv, kf, total = call(
        functools.partial(first_kernel, n),
        [
            struct((3, long, dim)),
            struct((long, feats)),
            struct((dim, feats)),
        ],
        *got, queries, key_vectors, value_vectors, feature_proj, gm_parts[0],
        flops=2 * macs, specs=[VMEM] * (n + 3) + [ANY],
    )
    earlier = swap_totals(total, n)
    gm, qf, scores, num = call(
        functools.partial(inner_kernel, n),
        [struct((long, dim)), struct((long, feats)), struct((long, long)), struct((long, dim), f32)],
        *gm_in[:-2], gm_in[-1], qkv, feature_proj, kf, flops=16 * macs,
    )
    carried, gn, later_total, *mixed_parts = call(
        functools.partial(turn_kernel, n),
        [
            struct((dim, feats)),
            struct((long, dim)),
            struct((dim, feats)),
        ]
        + [struct((rows, dim))] * n,
        gm, gm_in[-2], qf, num, *earlier, flops=2 * macs,
        scratch=[pltpu.VMEM((long, dim), jnp.bfloat16)],
    )
    after = swap_totals(later_total, n)
    mixed_in = exchange(mixed_parts[1:]) + [mixed_parts[0]]
    gq, gv_part, gkf_part = call(
        functools.partial(back_kernel, rows),
        [struct((long, dim)), struct((long, dim), f32), struct((long, feats), f32)],
        qkv, feature_proj, kf, qf, scores, gn, carried, flops=8 * macs,
    )
    grads = call(
        functools.partial(end_kernel, n),
        [struct((3, rows, dim))] * n,
        qkv, feature_proj, kf, gq, gv_part, gkf_part, *after, flops=3 * macs,
        scratch=[pltpu.VMEM((long, dim), jnp.bfloat16)] * 2,
    )
    grads_in = exchange(grads[1:]) + [grads[0]]

    order = [o for o in range(split) if not o & 1] + [o for o in range(split) if o & 1]
    own, sent = call(
        functools.partial(mixed_project_kernel, n, order),
        [struct((split // 2, rows, width))] * 2,
        *mixed_in, out_weight, grads[0], flops=2 * rows * out_weight.size,
        specs=[VMEM] * (n + 1) + [ANY],
        scratch=[pltpu.VMEM((rows, n * dim), jnp.bfloat16)],
    )
    part, last = reduce_blocks(own, sent, bits)
    return call(
        functools.partial(unpack_kernel, n),
        [struct((rows, width))] + [struct((rows, n * dim))] * 3,
        *grads_in, part, last,
        out_specs=[ANY] * 4,
        scratch=[
            pltpu.VMEM((rows, width), jnp.bfloat16),
            pltpu.SemaphoreType.DMA((n, 3)),
            pltpu.SemaphoreType.DMA,
        ],
    )


def solution(mesh):
    placed = (
        P("seq", "head"),
        P("seq", "head"),
        P("seq", "head"),
        P("head", None, None),
        P("head", None),
        P("seq", "head"),
    )
    return jax.shard_map(
        local,
        mesh=mesh,
        in_specs=placed,
        out_specs=(P("seq", "head"),) * 4,
        check_vma=False,
    )
```

```python
import functools

import jax
import jax.numpy as jnp
from jax import lax
from jax.experimental import pallas as pl
from jax.experimental.pallas import tpu as pltpu
from jax.sharding import PartitionSpec as P

EPSILON = 1e-05
VMEM = pl.BlockSpec(memory_space=pltpu.VMEM)
ANY = pl.BlockSpec(memory_space=pl.ANY)
NN = (((1,), (0,)), ((), ()))
NT = (((1,), (1,)), ((), ()))
TN = (((0,), (0,)), ((), ()))


def mm(a, b, dims=NN):
    return lax.dot_general(a, b, dims, preferred_element_type=jnp.float32)


def bf(x):
    return x.astype(jnp.bfloat16)


def call(body, outs, *args, flops=0, specs=None, out_specs=None, scratch=(), vmem=32):
    size = sum(a.size * a.dtype.itemsize for a in args)
    size += sum(o.size * o.dtype.itemsize for o in outs)
    return pl.pallas_call(
        body,
        out_shape=outs,
        in_specs=specs or [VMEM] * len(args),
        out_specs=out_specs or [VMEM] * len(outs),
        scratch_shapes=list(scratch),
        cost_estimate=pl.CostEstimate(flops=flops, bytes_accessed=size, transcendentals=0),
        compiler_params=pltpu.CompilerParams(vmem_limit_bytes=int(vmem * 1024 * 1024)),
    )(*args)


def struct(shape, dtype=jnp.bfloat16):
    return jax.ShapeDtypeStruct(shape, dtype)


def tiles(long, rows):
    size = 256 if long % 256 == 0 else rows
    return [(at, at + size) for at in range(0, long, size)]


def causal(scores):
    row = lax.broadcasted_iota(jnp.int32, scores.shape, 0)
    col = lax.broadcasted_iota(jnp.int32, scores.shape, 1)
    return jnp.where(col <= row, scores, 0.0)


def lower(left, right, spans):
    out = {}
    for i, (a, b) in enumerate(spans):
        for j, (c, d) in enumerate(spans[: i + 1]):
            tile = mm(left[a:b], right[c:d], NT)
            out[i, j] = bf(causal(tile) if i == j else tile)
    return out


def times(tile_at, right, spans):
    return [
        sum(mm(tile_at(i, j), right[c:d]) for j, (c, d) in enumerate(spans[: i + 1]))
        for i in range(len(spans))
    ]


def transposed_times(tile_at, right, spans):
    return [
        sum(mm(tile_at(i, j), right[a:b], TN) for i, (a, b) in enumerate(spans) if i >= j)
        for j in range(len(spans))
    ]


def swap(array, axis, bit):
    size = lax.axis_size(axis)
    return lax.ppermute(array, axis, [(i, i ^ bit) for i in range(size)])


def bits_of(size):
    return [1 << b for b in range(size.bit_length() - 1)]


def reduce_blocks(own, sent, bits):
    got = swap(sent, "head", 1)
    for bit in bits[1:]:
        total = own.astype(jnp.float32) + got.astype(jnp.float32)
        pairs = total.reshape((total.shape[0] // 2, 2) + total.shape[1:])
        own, got = pairs[:, 0], swap(bf(pairs[:, 1]), "head", bit)
    return own[0].astype(jnp.float32), got[0]


def member(n):
    return lax.rem(lax.axis_index("seq"), n)


def exchange(parts):
    return [swap(part, "seq", k) for k, part in enumerate(parts, 1)][::-1]


def swap_totals(total, n):
    size, step, got = lax.axis_size("seq"), n, []
    while step < size:
        got.append(swap(bf(total), "seq", step))
        total = total.astype(jnp.float32) + got[-1].astype(jnp.float32)
        step *= 2
    return got


def sum_of_side(refs, n, earlier):
    group = lax.div(lax.axis_index("seq"), n)
    total = jnp.zeros(refs[0].shape, jnp.float32)
    for at, ref in enumerate(refs):
        from_earlier = lax.rem(lax.shift_right_logical(group, at), 2) == 1
        keep = from_earlier if earlier else jnp.logical_not(from_earlier)
        total = total + jnp.where(keep, ref[...].astype(jnp.float32), 0.0)
    return bf(total)


def lane(index, width):
    return pl.ds(pl.multiple_of(index * width, 128), width)


def pack_kernel(n, q_ref, k_ref, v_ref, *rest):
    outs, sems = rest[:-1], rest[-1]
    r = member(n)
    dim = outs[0].shape[2]
    copies = [
        pltpu.make_async_copy(ref.at[:, lane(r ^ k, dim)], out.at[at], sems.at[k - 1, at])
        for k, out in enumerate(outs, 1)
        for at, ref in enumerate((q_ref, k_ref, v_ref)[-out.shape[0] :])
    ]
    for copy in copies:
        copy.start()
    for copy in copies:
        copy.wait()


def mark_kernel(_, out_ref):
    out_ref[...] = jnp.zeros(out_ref.shape, out_ref.dtype)


def early_blocks_kernel(offsets, *refs):
    blocks, w_ref, total_ref = refs[: len(offsets)], refs[-3], refs[-1]
    h = lax.axis_index("head")
    width = blocks[0].shape[1]
    total = None
    for offset, ref in zip(offsets, blocks):
        part = mm(ref[...], w_ref[:, lane(h ^ offset, width)], NT)
        total = part if total is None else total + part
    total_ref[...] = total


def grad_mixed_kernel(n, offset, q_ref, total_ref, block_ref, w_ref, *refs):
    outs, scr = refs[:-1], refs[-1]
    r, h = member(n), lax.axis_index("head")
    width = block_ref.shape[1]
    dim = outs[0].shape[2]
    scr[...] = bf(total_ref[...] + mm(block_ref[...], w_ref[:, lane(h ^ offset, width)], NT))
    for k in range(n):
        outs[k][0] = scr[:, lane(r ^ k, dim)]
        if k > 1:
            outs[k][1] = q_ref[:, lane(r ^ k, dim)]


def first_kernel(n, *refs):
    got, own, om_ref = refs[: n - 1][::-1], refs[n - 1 : n + 1], refs[n + 1]
    kv_ref, kf_ref, total_ref = refs[n + 3 :]
    r = member(n)
    rows, dim = own[0].shape[0], om_ref.shape[1]
    scale = dim ** (-0.25)
    for k in range(n):
        at = pl.ds(pl.multiple_of((r ^ k) * rows, 128), rows)
        if k:
            kv_ref[:, at, :] = got[k - 1][-2:]
        else:
            for i, ref in enumerate(own):
                kv_ref[i, at, :] = ref[:, lane(r, dim)]
    k_all = kv_ref[0]
    wide = k_all.astype(jnp.float32)
    half_sq = jnp.sum(wide * wide, axis=1, keepdims=True) * (scale * scale * 0.5)
    kf = bf(jnp.exp(mm(k_all, om_ref[r]) * scale - half_sq))
    kf_ref[...] = kf
    total_ref[...] = bf(mm(kv_ref[1], kf, TN))


def inner_kernel(n, *refs):
    parts, (own_ref, first_ref, kv_ref, om_ref, kf_ref) = refs[: n - 1][::-1], refs[n - 1 : n + 4]
    gm_ref, qf_ref, scores_ref, num_ref, q_scr = refs[n + 4 :]
    long, dim = num_ref.shape
    rows = long // n
    r = member(n)
    places = [pl.ds(pl.multiple_of((r ^ k) * rows, 128), rows) for k in range(n)]
    gm_ref[places[0], :] = parts[0][0]
    q_scr[places[0], :] = own_ref[:, lane(r, dim)]
    gm_ref[places[1], :] = jnp.zeros((rows, dim), gm_ref.dtype)
    q_scr[places[1], :] = first_ref[0]
    for k in range(2, n):
        gm_ref[places[k], :] = parts[k - 1][0]
        q_scr[places[k], :] = parts[k - 1][1]
    scale = dim ** (-0.25)
    spans = tiles(long, rows)
    qf = bf(jnp.exp(mm(q_scr[...], om_ref[r]) * scale))
    qf_ref[...] = qf
    scores = lower(qf, kf_ref[...], spans)
    for (i, j), tile in scores.items():
        scores_ref[slice(*spans[i]), slice(*spans[j])] = tile
    for (a, b), part in zip(spans, times(lambda i, j: scores[i, j], kv_ref[1], spans)):
        num_ref[a:b, :] = part


def turn_kernel(n, *refs):
    gm_ref, late_ref, qf_ref, num_ref, *earlier = refs[: -n - 4]
    carried_ref, gn_ref, total_ref = refs[-n - 4 : -n - 1]
    outs, scr = refs[-n - 1 : -1], refs[-1]
    r = member(n)
    rows = outs[0].shape[0]
    places = [
        pl.ds(pl.multiple_of((r ^ k) * rows, 128), rows) for k in range(n)
    ]
    scr[...] = gm_ref[...]
    scr[places[1], :] = late_ref[0]
    carried = sum_of_side(earlier, n, True)
    carried_ref[...] = carried
    num = num_ref[...] + mm(qf_ref[...], carried, NT)
    inv = lax.rsqrt(jnp.mean(num * num, axis=1, keepdims=True) + EPSILON)
    normed = num * inv
    gm = scr[...].astype(jnp.float32)
    gn = bf((gm - normed * jnp.mean(gm * normed, axis=1, keepdims=True)) * inv)
    gn_ref[...] = gn
    scr[...] = bf(normed)
    for k in range(n):
        outs[k][...] = scr[places[k], :]
    total_ref[...] = bf(mm(gn, qf_ref[...], TN))


def back_kernel(rows, kv_ref, om_ref, kf_ref, qf_ref, scores_ref, gn_ref, carried_ref,
                gq_ref, gv_ref, gkf_ref):
    long, dim = gn_ref.shape
    r = member(long // rows)
    scale = dim ** (-0.25)
    spans = tiles(long, rows)
    gn, qf = gn_ref[...], qf_ref[...]
    gs = lower(gn, kv_ref[1], spans)
    cross = mm(gn, carried_ref[...])
    for (a, b), part in zip(spans, times(lambda i, j: gs[i, j], kf_ref[...], spans)):
        terms = bf((cross[a:b] + part) * qf[a:b].astype(jnp.float32))
        gq_ref[a:b, :] = bf(mm(terms, om_ref[r], NT) * scale)
    for (a, b), part in zip(spans, transposed_times(lambda i, j: gs[i, j], qf, spans)):
        gkf_ref[a:b, :] = part

    def scores_at(i, j):
        return scores_ref[slice(*spans[i]), slice(*spans[j])]

    for (a, b), part in zip(spans, transposed_times(scores_at, gn, spans)):
        gv_ref[a:b, :] = part


def end_kernel(n, kv_ref, om_ref, kf_ref, gq_ref, gv_ref, gkf_ref, *rest):
    later, outs, (gk_scr, gv_scr) = rest[: -n - 2], rest[-n - 2 : -2], rest[-2:]
    r, dim = member(n), om_ref.shape[1]
    rows = outs[0].shape[1]
    scale = dim ** (-0.25)
    kf, after = kf_ref[...], sum_of_side(later, n, False)
    gv_scr[...] = bf(gv_ref[...] + mm(kf, after, NT))
    gkf = gkf_ref[...] + mm(kv_ref[1], after)
    terms = bf(gkf * kf.astype(jnp.float32))
    total = jnp.sum(terms.astype(jnp.float32), axis=1, keepdims=True)
    wide = kv_ref[0].astype(jnp.float32)
    gk_scr[...] = bf(mm(terms, om_ref[r], NT) * scale - total * wide * (scale * scale))
    for k in range(n):
        at = pl.ds(pl.multiple_of((r ^ k) * rows, 128), rows)
        outs[k][0] = gq_ref[at, :]
        outs[k][1] = gk_scr[at, :]
        outs[k][2] = gv_scr[at, :]


def mixed_project_kernel(n, offsets, *refs):
    mixed_in, (w_ref, _, own_ref, sent_ref, scr) = refs[:n][::-1], refs[n:]
    r, h = member(n), lax.axis_index("head")
    width = own_ref.shape[2]
    dim = mixed_in[0].shape[1]
    half = len(offsets) // 2
    for k in range(n):
        scr[:, lane(r ^ k, dim)] = mixed_in[k][...]
    mixed = scr[...]
    for at, offset in enumerate(offsets):
        part = bf(mm(mixed, w_ref[:, lane(h ^ offset, width)]))
        if at < half:
            own_ref[at] = part
        else:
            sent_ref[at - half] = part


def unpack_kernel(n, *refs):
    got, (part_ref, last_ref) = refs[:n][::-1], refs[n : n + 2]
    (out_ref, *outs), (scr, sems, last_sem) = refs[n + 2 : -3], refs[-3:]
    r = member(n)
    dim = got[0].shape[2]
    copies = [
        pltpu.make_async_copy(got[k].at[at], out.at[:, lane(r ^ k, dim)], sems.at[k, at])
        for k in range(n)
        for at, out in enumerate(outs)
    ]
    for copy in copies:
        copy.start()
    scr[...] = bf(part_ref[...] + last_ref[...].astype(jnp.float32))
    copies.append(pltpu.make_async_copy(scr, out_ref, last_sem))
    copies[-1].start()
    for copy in copies:
        copy.wait()


def local(queries, key_vectors, value_vectors, feature_proj, out_weight, grad_output):
    n, dim, feats = feature_proj.shape
    rows, width = grad_output.shape
    split = lax.axis_size("head")
    bits = bits_of(split)
    long = n * rows
    macs = long * dim * feats * 2
    f32 = jnp.float32

    offsets, blocks = [0], [grad_output]
    for bit in reversed(bits):
        blocks = blocks + [swap(b, "head", bit) for b in blocks]
        offsets = offsets + [o ^ bit for o in offsets]
    sends = call(
        functools.partial(pack_kernel, n),
        [struct((3 if k == 1 else 2, rows, dim)) for k in range(1, n)],
        queries, key_vectors, value_vectors,
        specs=[ANY] * 3, scratch=[pltpu.SemaphoreType.DMA((n - 1, 3))], vmem=53.68,
    )
    got = exchange(sends)
    (mark,) = call(mark_kernel, [struct((8, 128), f32)], blocks[offsets.index(1)], specs=[ANY], flops=10**10)
    (gm_early,) = call(
        functools.partial(early_blocks_kernel, offsets[:-1]),
        [struct((rows, n * dim), f32)],
        *blocks[:-1], out_weight, mark, flops=2 * rows * out_weight.size,
        specs=[VMEM] * split + [ANY],
    )
    gm_parts = call(
        functools.partial(grad_mixed_kernel, n, offsets[-1]),
        [struct((1 if k < 2 else 2, rows, dim)) for k in range(n)],
        queries, gm_early, blocks[-1], out_weight, flops=2 * rows * out_weight.size,
        scratch=[pltpu.VMEM((rows, n * dim), jnp.bfloat16)],
    )
    gm_in = exchange(gm_parts[1:]) + [gm_parts[0]]
    kv, kf, total = call(
        functools.partial(first_kernel, n),
        [
            struct((2, long, dim)),
            struct((long, feats)),
            struct((dim, feats)),
        ],
        *got, key_vectors, value_vectors, feature_proj, gm_parts[0],
        flops=2 * macs, specs=[VMEM] * (n + 2) + [ANY],
    )
    earlier = swap_totals(total, n)
    gm, qf, scores, num = call(
        functools.partial(inner_kernel, n),
        [struct((long, dim)), struct((long, feats)), struct((long, long)), struct((long, dim), f32)],
        *gm_in[:-2], gm_in[-1], queries, got[-1], kv, feature_proj, kf, flops=16 * macs,
        scratch=[pltpu.VMEM((long, dim), jnp.bfloat16)],
    )
    carried, gn, later_total, *mixed_parts = call(
        functools.partial(turn_kernel, n),
        [
            struct((dim, feats)),
            struct((long, dim)),
            struct((dim, feats)),
        ]
        + [struct((rows, dim))] * n,
        gm, gm_in[-2], qf, num, *earlier, flops=2 * macs,
        scratch=[pltpu.VMEM((long, dim), jnp.bfloat16)],
    )
    after = swap_totals(later_total, n)
    mixed_in = exchange(mixed_parts[1:]) + [mixed_parts[0]]
    gq, gv_part, gkf_part = call(
        functools.partial(back_kernel, rows),
        [struct((long, dim)), struct((long, dim), f32), struct((long, feats), f32)],
        kv, feature_proj, kf, qf, scores, gn, carried, flops=8 * macs,
    )
    grads = call(
        functools.partial(end_kernel, n),
        [struct((3, rows, dim))] * n,
        kv, feature_proj, kf, gq, gv_part, gkf_part, *after, flops=3 * macs,
        scratch=[pltpu.VMEM((long, dim), jnp.bfloat16)] * 2,
    )
    grads_in = exchange(grads[1:]) + [grads[0]]

    order = [o for o in range(split) if not o & 1] + [o for o in range(split) if o & 1]
    own, sent = call(
        functools.partial(mixed_project_kernel, n, order),
        [struct((split // 2, rows, width))] * 2,
        *mixed_in, out_weight, grads[0], flops=2 * rows * out_weight.size,
        specs=[VMEM] * (n + 1) + [ANY],
        scratch=[pltpu.VMEM((rows, n * dim), jnp.bfloat16)],
    )
    part, last = reduce_blocks(own, sent, bits)
    return call(
        functools.partial(unpack_kernel, n),
        [struct((rows, width))] + [struct((rows, n * dim))] * 3,
        *grads_in, part, last,
        out_specs=[ANY] * 4,
        scratch=[
            pltpu.VMEM((rows, width), jnp.bfloat16),
            pltpu.SemaphoreType.DMA((n, 3)),
            pltpu.SemaphoreType.DMA,
        ],
    )


def solution(mesh):
    placed = (
        P("seq", "head"),
        P("seq", "head"),
        P("seq", "head"),
        P("head", None, None),
        P("head", None),
        P("seq", "head"),
    )
    return jax.shard_map(
        local,
        mesh=mesh,
        in_specs=placed,
        out_specs=(P("seq", "head"),) * 4,
        check_vma=False,
    )
```

```python
import functools

import jax
import jax.numpy as jnp
from jax import lax
from jax.experimental import pallas as pl
from jax.experimental.pallas import tpu as pltpu
from jax.sharding import PartitionSpec as P

EPSILON = 1e-05
VMEM = pl.BlockSpec(memory_space=pltpu.VMEM)
ANY = pl.BlockSpec(memory_space=pl.ANY)
NN = (((1,), (0,)), ((), ()))
NT = (((1,), (1,)), ((), ()))
TN = (((0,), (0,)), ((), ()))


def mm(a, b, dims=NN):
    return lax.dot_general(a, b, dims, preferred_element_type=jnp.float32)


def bf(x):
    return x.astype(jnp.bfloat16)


def call(body, outs, *args, flops=0, specs=None, out_specs=None, scratch=(), vmem=32, aliases=None):
    size = sum(a.size * a.dtype.itemsize for a in args)
    size += sum(o.size * o.dtype.itemsize for o in outs)
    return pl.pallas_call(
        body,
        out_shape=outs,
        in_specs=specs or [VMEM] * len(args),
        out_specs=out_specs or [VMEM] * len(outs),
        scratch_shapes=list(scratch),
        input_output_aliases=aliases or {},
        cost_estimate=pl.CostEstimate(flops=flops, bytes_accessed=size, transcendentals=0),
        compiler_params=pltpu.CompilerParams(vmem_limit_bytes=int(vmem * 1024 * 1024)),
    )(*args)


def struct(shape, dtype=jnp.bfloat16):
    return jax.ShapeDtypeStruct(shape, dtype)


def tiles(long, rows):
    size = 256 if long % 256 == 0 else rows
    return [(at, at + size) for at in range(0, long, size)]


def causal(scores):
    row = lax.broadcasted_iota(jnp.int32, scores.shape, 0)
    col = lax.broadcasted_iota(jnp.int32, scores.shape, 1)
    return jnp.where(col <= row, scores, 0.0)


def lower(left, right, spans):
    out = {}
    for i, (a, b) in enumerate(spans):
        for j, (c, d) in enumerate(spans[: i + 1]):
            tile = mm(left[a:b], right[c:d], NT)
            out[i, j] = bf(causal(tile) if i == j else tile)
    return out


def times(tile_at, right, spans):
    return [
        sum(mm(tile_at(i, j), right[c:d]) for j, (c, d) in enumerate(spans[: i + 1]))
        for i in range(len(spans))
    ]


def transposed_times(tile_at, right, spans):
    return [
        sum(mm(tile_at(i, j), right[a:b], TN) for i, (a, b) in enumerate(spans) if i >= j)
        for j in range(len(spans))
    ]


def swap(array, axis, bit):
    size = lax.axis_size(axis)
    return lax.ppermute(array, axis, [(i, i ^ bit) for i in range(size)])


def bits_of(size):
    return [1 << b for b in range(size.bit_length() - 1)]


def sum_kernel(own_ref, *refs):
    got, (kept_ref, sent_ref) = refs[:-2], refs[-2:]
    rows = got[0].shape[1]
    for i, ref in enumerate(got):
        at = slice(i * rows, (i + 1) * rows)
        for j in range(kept_ref.shape[0]):
            kept_ref[j, at, :] = own_ref[2 * j, at, :].astype(jnp.float32) + ref[
                2 * j
            ].astype(jnp.float32)
            sent_ref[j, at, :] = bf(
                own_ref[2 * j + 1, at, :].astype(jnp.float32)
                + ref[2 * j + 1].astype(jnp.float32)
            )


def reduce_blocks(own, sent, bits):
    half = struct((own.shape[0] // 2,) + own.shape[1:])
    got = [swap(x, "head", bits[0]) for x in sent]
    own, sent = call(sum_kernel, [struct(half.shape, jnp.float32), half], own, *got)
    got = swap(sent, "head", bits[1])
    for bit in bits[2:]:
        total = own + got.astype(jnp.float32)
        pairs = total.reshape((total.shape[0] // 2, 2) + total.shape[1:])
        own, got = pairs[:, 0], swap(bf(pairs[:, 1]), "head", bit)
    return own[0], got[0]


def member(n):
    return lax.rem(lax.axis_index("seq"), n)


def exchange(parts):
    return [swap(part, "seq", k) for k, part in enumerate(parts, 1)][::-1]


def swap_totals(total, n):
    size, step, got = lax.axis_size("seq"), n, []
    while step < size:
        got.append(swap(bf(total), "seq", step))
        total = total.astype(jnp.float32) + got[-1].astype(jnp.float32)
        step *= 2
    return got


def sum_of_side(refs, n, earlier):
    group = lax.div(lax.axis_index("seq"), n)
    total = jnp.zeros(refs[0].shape, jnp.float32)
    for at, ref in enumerate(refs):
        from_earlier = lax.rem(lax.shift_right_logical(group, at), 2) == 1
        keep = from_earlier if earlier else jnp.logical_not(from_earlier)
        total = total + jnp.where(keep, ref[...].astype(jnp.float32), 0.0)
    return bf(total)


def lane(index, width):
    return pl.ds(pl.multiple_of(index * width, 128), width)


def pack_kernel(n, q_ref, k_ref, v_ref, *rest):
    outs, sems = rest[:-1], rest[-1]
    r = member(n)
    dim = outs[0].shape[2]
    copies = [
        pltpu.make_async_copy(ref.at[:, lane(r ^ k, dim)], out.at[at], sems.at[k - 1, at])
        for k, out in enumerate(outs, 1)
        for at, ref in enumerate((q_ref, k_ref, v_ref)[-out.shape[0] :])
    ]
    for copy in copies:
        copy.start()
    for copy in copies:
        copy.wait()


def mark_kernel(_, out_ref):
    out_ref[...] = jnp.zeros(out_ref.shape, out_ref.dtype)


def early_blocks_kernel(offsets, *refs):
    blocks, w_ref, total_ref = refs[: len(offsets)], refs[-3], refs[-1]
    h = lax.axis_index("head")
    width = blocks[0].shape[1]
    total = None
    for offset, ref in zip(offsets, blocks):
        part = mm(ref[...], w_ref[:, lane(h ^ offset, width)], NT)
        total = part if total is None else total + part
    total_ref[...] = total


def grad_mixed_kernel(n, offset, q_ref, total_ref, block_ref, w_ref, *refs):
    outs, scr = refs[:-1], refs[-1]
    r, h = member(n), lax.axis_index("head")
    width = block_ref.shape[1]
    dim = outs[0].shape[2]
    scr[...] = bf(total_ref[...] + mm(block_ref[...], w_ref[:, lane(h ^ offset, width)], NT))
    for k in range(n):
        outs[k][0] = scr[:, lane(r ^ k, dim)]
        if k > 1:
            outs[k][1] = q_ref[:, lane(r ^ k, dim)]


def first_kernel(n, *refs):
    got, own, om_ref = refs[: n - 1][::-1], refs[n - 1 : n + 1], refs[n + 1]
    kv_ref, kf_ref, total_ref = refs[n + 3 :]
    r = member(n)
    rows, dim = own[0].shape[0], om_ref.shape[1]
    scale = dim ** (-0.25)
    for k in range(n):
        at = pl.ds(pl.multiple_of((r ^ k) * rows, 128), rows)
        if k:
            kv_ref[:, at, :] = got[k - 1][-2:]
        else:
            for i, ref in enumerate(own):
                kv_ref[i, at, :] = ref[:, lane(r, dim)]
    k_all = kv_ref[0]
    wide = k_all.astype(jnp.float32)
    half_sq = jnp.sum(wide * wide, axis=1, keepdims=True) * (scale * scale * 0.5)
    kf = bf(jnp.exp(mm(k_all, om_ref[r]) * scale - half_sq))
    kf_ref[...] = kf
    total_ref[...] = bf(mm(kv_ref[1], kf, TN))


def inner_kernel(n, *refs):
    parts, (own_ref, first_ref, kv_ref, om_ref, kf_ref) = refs[: n - 1][::-1], refs[n - 1 : n + 4]
    gm_ref, qf_ref, scores_ref, num_ref, q_scr = refs[n + 4 :]
    long, dim = num_ref.shape
    rows = long // n
    r = member(n)
    places = [pl.ds(pl.multiple_of((r ^ k) * rows, 128), rows) for k in range(n)]
    gm_ref[places[0], :] = parts[0][0]
    q_scr[places[0], :] = own_ref[:, lane(r, dim)]
    gm_ref[places[1], :] = jnp.zeros((rows, dim), gm_ref.dtype)
    q_scr[places[1], :] = first_ref[0]
    for k in range(2, n):
        gm_ref[places[k], :] = parts[k - 1][0]
        q_scr[places[k], :] = parts[k - 1][1]
    scale = dim ** (-0.25)
    spans = tiles(long, rows)
    qf = bf(jnp.exp(mm(q_scr[...], om_ref[r]) * scale))
    qf_ref[...] = qf
    scores = lower(qf, kf_ref[...], spans)
    for (i, j), tile in scores.items():
        scores_ref[slice(*spans[i]), slice(*spans[j])] = tile
    for (a, b), part in zip(spans, times(lambda i, j: scores[i, j], kv_ref[1], spans)):
        num_ref[a:b, :] = part


def turn_kernel(n, *refs):
    gm_ref, late_ref, qf_ref, num_ref, *earlier = refs[: -n - 4]
    carried_ref, gn_ref, total_ref = refs[-n - 4 : -n - 1]
    outs, scr = refs[-n - 1 : -1], refs[-1]
    r = member(n)
    rows = outs[0].shape[0]
    places = [
        pl.ds(pl.multiple_of((r ^ k) * rows, 128), rows) for k in range(n)
    ]
    scr[...] = gm_ref[...]
    scr[places[1], :] = late_ref[0]
    carried = sum_of_side(earlier, n, True)
    carried_ref[...] = carried
    num = num_ref[...] + mm(qf_ref[...], carried, NT)
    inv = lax.rsqrt(jnp.mean(num * num, axis=1, keepdims=True) + EPSILON)
    normed = num * inv
    gm = scr[...].astype(jnp.float32)
    gn = bf((gm - normed * jnp.mean(gm * normed, axis=1, keepdims=True)) * inv)
    gn_ref[...] = gn
    scr[...] = bf(normed)
    for k in range(n):
        outs[k][...] = scr[places[k], :]
    total_ref[...] = bf(mm(gn, qf_ref[...], TN))


def back_kernel(rows, kv_ref, om_ref, kf_ref, qf_ref, scores_ref, gn_ref, carried_ref,
                gq_ref, gv_ref, gkf_ref):
    long, dim = gn_ref.shape
    r = member(long // rows)
    scale = dim ** (-0.25)
    spans = tiles(long, rows)
    gn, qf = gn_ref[...], qf_ref[...]
    gs = lower(gn, kv_ref[1], spans)
    cross = mm(gn, carried_ref[...])
    for (a, b), part in zip(spans, times(lambda i, j: gs[i, j], kf_ref[...], spans)):
        terms = bf((cross[a:b] + part) * qf[a:b].astype(jnp.float32))
        gq_ref[a:b, :] = bf(mm(terms, om_ref[r], NT) * scale)
    for (a, b), part in zip(spans, transposed_times(lambda i, j: gs[i, j], qf, spans)):
        gkf_ref[a:b, :] = part

    def scores_at(i, j):
        return scores_ref[slice(*spans[i]), slice(*spans[j])]

    for (a, b), part in zip(spans, transposed_times(scores_at, gn, spans)):
        gv_ref[a:b, :] = part


def end_kernel(n, kv_ref, om_ref, kf_ref, gq_ref, gv_ref, gkf_ref, *rest):
    later, outs, (gk_scr, gv_scr) = rest[: -n - 2], rest[-n - 2 : -2], rest[-2:]
    r, dim = member(n), om_ref.shape[1]
    rows = outs[0].shape[1]
    scale = dim ** (-0.25)
    kf, after = kf_ref[...], sum_of_side(later, n, False)
    gv_scr[...] = bf(gv_ref[...] + mm(kf, after, NT))
    gkf = gkf_ref[...] + mm(kv_ref[1], after)
    terms = bf(gkf * kf.astype(jnp.float32))
    total = jnp.sum(terms.astype(jnp.float32), axis=1, keepdims=True)
    wide = kv_ref[0].astype(jnp.float32)
    gk_scr[...] = bf(mm(terms, om_ref[r], NT) * scale - total * wide * (scale * scale))
    for k in range(n):
        at = pl.ds(pl.multiple_of((r ^ k) * rows, 128), rows)
        outs[k][0] = gq_ref[at, :]
        outs[k][1] = gk_scr[at, :]
        outs[k][2] = gv_scr[at, :]


def mixed_project_kernel(n, offsets, *refs):
    mixed_in, (w_ref, _, own_ref, *sent, scr) = refs[:n][::-1], refs[n:]
    r, h = member(n), lax.axis_index("head")
    width = own_ref.shape[2]
    dim = mixed_in[0].shape[1]
    half = len(offsets) // 2
    for k in range(n):
        scr[:, lane(r ^ k, dim)] = mixed_in[k][...]
    mixed = scr[...]
    for at, offset in enumerate(offsets):
        part = bf(mm(mixed, w_ref[:, lane(h ^ offset, width)]))
        if at < half:
            own_ref[at] = part
        else:
            step = sent[0].shape[1]
            for i, ref in enumerate(sent):
                ref[at - half] = part[i * step : (i + 1) * step]


def unpack_kernel(ks, n, *refs):
    got, (*outs, sems) = refs[: len(ks)], refs[len(ks) :]
    r = member(n)
    dim = got[0].shape[2]
    copies = [
        pltpu.make_async_copy(ref.at[at], out.at[:, lane(r ^ k, dim)], sems.at[i, at])
        for i, (k, ref) in enumerate(zip(ks, got))
        for at, out in enumerate(outs)
    ]
    for copy in copies:
        copy.start()
    for copy in copies:
        copy.wait()


def last_kernel(n, got_ref, part_ref, last_ref, *refs):
    (out_ref, *outs), (scr, sems) = refs[3:-2], refs[-2:]
    r = member(n)
    dim = got_ref.shape[2]
    copies = [
        pltpu.make_async_copy(got_ref.at[at], out.at[:, lane(r ^ 1, dim)], sems.at[at])
        for at, out in enumerate(outs)
    ]
    for copy in copies:
        copy.start()
    scr[...] = bf(part_ref[...] + last_ref[...].astype(jnp.float32))
    copies.append(pltpu.make_async_copy(scr, out_ref, sems.at[3]))
    copies[-1].start()
    for copy in copies:
        copy.wait()


def local(queries, key_vectors, value_vectors, feature_proj, out_weight, grad_output):
    n, dim, feats = feature_proj.shape
    rows, width = grad_output.shape
    split = lax.axis_size("head")
    bits = bits_of(split)
    long = n * rows
    macs = long * dim * feats * 2
    f32 = jnp.float32

    offsets, blocks = [0], [grad_output]
    for bit in reversed(bits):
        blocks = blocks + [swap(b, "head", bit) for b in blocks]
        offsets = offsets + [o ^ bit for o in offsets]
    sends = call(
        functools.partial(pack_kernel, n),
        [struct((3 if k == 1 else 2, rows, dim)) for k in range(1, n)],
        queries, key_vectors, value_vectors,
        specs=[ANY] * 3, scratch=[pltpu.SemaphoreType.DMA((n - 1, 3))], vmem=53.68,
    )
    got = exchange(sends)
    (mark,) = call(mark_kernel, [struct((8, 128), f32)], blocks[offsets.index(1)], specs=[ANY], flops=10**10)
    (gm_early,) = call(
        functools.partial(early_blocks_kernel, offsets[:-1]),
        [struct((rows, n * dim), f32)],
        *blocks[:-1], out_weight, mark, flops=2 * rows * out_weight.size,
        specs=[VMEM] * split + [ANY],
    )
    gm_parts = call(
        functools.partial(grad_mixed_kernel, n, offsets[-1]),
        [struct((1 if k < 2 else 2, rows, dim)) for k in range(n)],
        queries, gm_early, blocks[-1], out_weight, flops=2 * rows * out_weight.size,
        scratch=[pltpu.VMEM((rows, n * dim), jnp.bfloat16)],
    )
    gm_in = exchange(gm_parts[1:]) + [gm_parts[0]]
    kv, kf, total = call(
        functools.partial(first_kernel, n),
        [
            struct((2, long, dim)),
            struct((long, feats)),
            struct((dim, feats)),
        ],
        *got, key_vectors, value_vectors, feature_proj, gm_parts[0],
        flops=2 * macs, specs=[VMEM] * (n + 2) + [ANY],
    )
    earlier = swap_totals(total, n)
    gm, qf, scores, num = call(
        functools.partial(inner_kernel, n),
        [struct((long, dim)), struct((long, feats)), struct((long, long)), struct((long, dim), f32)],
        *gm_in[:-2], gm_in[-1], queries, got[-1], kv, feature_proj, kf, flops=16 * macs,
        scratch=[pltpu.VMEM((long, dim), jnp.bfloat16)],
    )
    carried, gn, later_total, *mixed_parts = call(
        functools.partial(turn_kernel, n),
        [
            struct((dim, feats)),
            struct((long, dim)),
            struct((dim, feats)),
        ]
        + [struct((rows, dim))] * n,
        gm, gm_in[-2], qf, num, *earlier, flops=2 * macs,
        scratch=[pltpu.VMEM((long, dim), jnp.bfloat16)],
    )
    after = swap_totals(later_total, n)
    mixed_in = exchange(mixed_parts[1:]) + [mixed_parts[0]]
    gq, gv_part, gkf_part = call(
        functools.partial(back_kernel, rows),
        [struct((long, dim)), struct((long, dim), f32), struct((long, feats), f32)],
        kv, feature_proj, kf, qf, scores, gn, carried, flops=8 * macs,
    )
    grads = call(
        functools.partial(end_kernel, n),
        [struct((3, rows, dim))] * n,
        kv, feature_proj, kf, gq, gv_part, gkf_part, *after, flops=3 * macs,
        scratch=[pltpu.VMEM((long, dim), jnp.bfloat16)] * 2,
    )
    grads_in = exchange(grads[1:]) + [grads[0]]

    order = [o for o in range(split) if not o & 1] + [o for o in range(split) if o & 1]
    own, *sent = call(
        functools.partial(mixed_project_kernel, n, order),
        [struct((split // 2, rows, width))]
        + [struct((split // 2, rows, width))],
        *mixed_in, out_weight, grads[0], flops=2 * rows * out_weight.size,
        specs=[VMEM] * (n + 1) + [ANY],
        scratch=[pltpu.VMEM((rows, n * dim), jnp.bfloat16)],
    )
    part, last = reduce_blocks(own, sent, bits)
    *early, late, own_grads = grads_in
    ks = [k for k in range(n - 1, 1, -1)] + [0]
    arrays = [struct((rows, n * dim))] * 3
    partial_grads = call(
        functools.partial(unpack_kernel, ks, n), arrays,
        *early, own_grads, flops=6 * 10**8,
        out_specs=[ANY] * 3, scratch=[pltpu.SemaphoreType.DMA((n - 1, 3))],
    )
    return call(
        functools.partial(last_kernel, n),
        [struct((rows, width))] + arrays,
        late, part, last, *partial_grads,
        specs=[VMEM] * 3 + [ANY] * 3, out_specs=[ANY] * 4,
        aliases={3: 1, 4: 2, 5: 3},
        scratch=[pltpu.VMEM((rows, width), jnp.bfloat16), pltpu.SemaphoreType.DMA((4,))],
    )


def solution(mesh):
    placed = (
        P("seq", "head"),
        P("seq", "head"),
        P("seq", "head"),
        P("head", None, None),
        P("head", None),
        P("seq", "head"),
    )
    return jax.shard_map(
        local,
        mesh=mesh,
        in_specs=placed,
        out_specs=(P("seq", "head"),) * 4,
        check_vma=False,
    )
```

```python
import functools

import jax
import jax.numpy as jnp
from jax import lax
from jax.experimental import pallas as pl
from jax.experimental.pallas import tpu as pltpu
from jax.sharding import PartitionSpec as P

EPSILON = 1e-05
VMEM = pl.BlockSpec(memory_space=pltpu.VMEM)
ANY = pl.BlockSpec(memory_space=pl.ANY)
NN = (((1,), (0,)), ((), ()))
NT = (((1,), (1,)), ((), ()))
TN = (((0,), (0,)), ((), ()))


def mm(a, b, dims=NN):
    return lax.dot_general(a, b, dims, preferred_element_type=jnp.float32)


def bf(x):
    return x.astype(jnp.bfloat16)


def call(body, outs, *args, flops=0, specs=None, out_specs=None, scratch=(), vmem=32, aliases=None):
    size = sum(a.size * a.dtype.itemsize for a in args)
    size += sum(o.size * o.dtype.itemsize for o in outs)
    return pl.pallas_call(
        body,
        out_shape=outs,
        in_specs=specs or [VMEM] * len(args),
        out_specs=out_specs or [VMEM] * len(outs),
        scratch_shapes=list(scratch),
        input_output_aliases=aliases or {},
        cost_estimate=pl.CostEstimate(flops=flops, bytes_accessed=size, transcendentals=0),
        compiler_params=pltpu.CompilerParams(vmem_limit_bytes=int(vmem * 1024 * 1024)),
    )(*args)


def struct(shape, dtype=jnp.bfloat16):
    return jax.ShapeDtypeStruct(shape, dtype)


def tiles(long, rows):
    size = 256 if long % 256 == 0 else rows
    return [(at, at + size) for at in range(0, long, size)]


def causal(scores):
    row = lax.broadcasted_iota(jnp.int32, scores.shape, 0)
    col = lax.broadcasted_iota(jnp.int32, scores.shape, 1)
    return jnp.where(col <= row, scores, 0.0)


def lower(left, right, spans):
    out = {}
    for i, (a, b) in enumerate(spans):
        for j, (c, d) in enumerate(spans[: i + 1]):
            tile = mm(left[a:b], right[c:d], NT)
            out[i, j] = bf(causal(tile) if i == j else tile)
    return out


def times(tile_at, right, spans):
    return [
        sum(mm(tile_at(i, j), right[c:d]) for j, (c, d) in enumerate(spans[: i + 1]))
        for i in range(len(spans))
    ]


def transposed_times(tile_at, right, spans):
    return [
        sum(mm(tile_at(i, j), right[a:b], TN) for i, (a, b) in enumerate(spans) if i >= j)
        for j in range(len(spans))
    ]


def swap(array, axis, bit):
    size = lax.axis_size(axis)
    return lax.ppermute(array, axis, [(i, i ^ bit) for i in range(size)])


def bits_of(size):
    return [1 << b for b in range(size.bit_length() - 1)]


def sum_kernel(own_ref, *refs):
    got, (kept_ref, sent_ref) = refs[:-3], refs[-2:]
    rows = got[0].shape[1]
    for i, ref in enumerate(got):
        at = slice(i * rows, (i + 1) * rows)
        for j in range(kept_ref.shape[0]):
            kept_ref[j, at, :] = own_ref[2 * j, at, :].astype(jnp.float32) + ref[
                2 * j
            ].astype(jnp.float32)
            sent_ref[j, at, :] = bf(
                own_ref[2 * j + 1, at, :].astype(jnp.float32)
                + ref[2 * j + 1].astype(jnp.float32)
            )


def reduce_blocks(own, sent, bits):
    half = struct((own.shape[0] // 2,) + own.shape[1:])
    got = [swap(x, "head", bits[0]) for x in sent]
    (mark,) = call(mark_kernel, [struct((8, 128), jnp.float32)], own, specs=[ANY], flops=28 * 10**8)
    own, sent = call(
        sum_kernel, [struct(half.shape, jnp.float32), half], own, *got, mark,
        specs=[VMEM] * (1 + len(got)) + [ANY],
    )
    got = swap(sent, "head", bits[1])
    for bit in bits[2:]:
        total = own + got.astype(jnp.float32)
        pairs = total.reshape((total.shape[0] // 2, 2) + total.shape[1:])
        own, got = pairs[:, 0], swap(bf(pairs[:, 1]), "head", bit)
    return own[0], got[0]


def member(n):
    return lax.rem(lax.axis_index("seq"), n)


def exchange(parts):
    return [swap(part, "seq", k) for k, part in enumerate(parts, 1)][::-1]


def swap_totals(total, n):
    size, step, got = lax.axis_size("seq"), n, []
    while step < size:
        got.append(swap(bf(total), "seq", step))
        total = total.astype(jnp.float32) + got[-1].astype(jnp.float32)
        step *= 2
    return got


def sum_of_side(refs, n, earlier):
    group = lax.div(lax.axis_index("seq"), n)
    total = jnp.zeros(refs[0].shape, jnp.float32)
    for at, ref in enumerate(refs):
        from_earlier = lax.rem(lax.shift_right_logical(group, at), 2) == 1
        keep = from_earlier if earlier else jnp.logical_not(from_earlier)
        total = total + jnp.where(keep, ref[...].astype(jnp.float32), 0.0)
    return bf(total)


def lane(index, width):
    return pl.ds(pl.multiple_of(index * width, 128), width)


def pack_kernel(n, q_ref, k_ref, v_ref, *rest):
    outs, sems = rest[:-1], rest[-1]
    r = member(n)
    dim = outs[0].shape[2]
    copies = [
        pltpu.make_async_copy(ref.at[:, lane(r ^ k, dim)], out.at[at], sems.at[k - 1, at])
        for k, out in enumerate(outs, 1)
        for at, ref in enumerate((q_ref, k_ref, v_ref)[-out.shape[0] :])
    ]
    for copy in copies:
        copy.start()
    for copy in copies:
        copy.wait()


def mark_kernel(_, out_ref):
    out_ref[...] = jnp.zeros(out_ref.shape, out_ref.dtype)


def early_blocks_kernel(offsets, *refs):
    blocks, w_ref, total_ref = refs[: len(offsets)], refs[-3], refs[-1]
    h = lax.axis_index("head")
    width = blocks[0].shape[1]
    total = None
    for offset, ref in zip(offsets, blocks):
        part = mm(ref[...], w_ref[:, lane(h ^ offset, width)], NT)
        total = part if total is None else total + part
    total_ref[...] = total


def grad_mixed_kernel(n, offset, q_ref, total_ref, block_ref, w_ref, *refs):
    outs, scr = refs[:-1], refs[-1]
    r, h = member(n), lax.axis_index("head")
    width = block_ref.shape[1]
    dim = outs[0].shape[2]
    scr[...] = bf(total_ref[...] + mm(block_ref[...], w_ref[:, lane(h ^ offset, width)], NT))
    for k in range(n):
        outs[k][0] = scr[:, lane(r ^ k, dim)]
        if k > 1:
            outs[k][1] = q_ref[:, lane(r ^ k, dim)]


def first_kernel(n, *refs):
    got, own, om_ref = refs[: n - 1][::-1], refs[n - 1 : n + 1], refs[n + 1]
    kv_ref, kf_ref, total_ref = refs[n + 3 :]
    r = member(n)
    rows, dim = own[0].shape[0], om_ref.shape[1]
    scale = dim ** (-0.25)
    for k in range(n):
        at = pl.ds(pl.multiple_of((r ^ k) * rows, 128), rows)
        if k:
            kv_ref[:, at, :] = got[k - 1][-2:]
        else:
            for i, ref in enumerate(own):
                kv_ref[i, at, :] = ref[:, lane(r, dim)]
    k_all = kv_ref[0]
    wide = k_all.astype(jnp.float32)
    half_sq = jnp.sum(wide * wide, axis=1, keepdims=True) * (scale * scale * 0.5)
    kf = bf(jnp.exp(mm(k_all, om_ref[r]) * scale - half_sq))
    kf_ref[...] = kf
    total_ref[...] = bf(mm(kv_ref[1], kf, TN))


def inner_kernel(n, *refs):
    parts, (own_ref, first_ref, kv_ref, om_ref, kf_ref) = refs[: n - 1][::-1], refs[n - 1 : n + 4]
    gm_ref, qf_ref, scores_ref, num_ref, q_scr = refs[n + 4 :]
    long, dim = num_ref.shape
    rows = long // n
    r = member(n)
    places = [pl.ds(pl.multiple_of((r ^ k) * rows, 128), rows) for k in range(n)]
    gm_ref[places[0], :] = parts[0][0]
    q_scr[places[0], :] = own_ref[:, lane(r, dim)]
    gm_ref[places[1], :] = jnp.zeros((rows, dim), gm_ref.dtype)
    q_scr[places[1], :] = first_ref[0]
    for k in range(2, n):
        gm_ref[places[k], :] = parts[k - 1][0]
        q_scr[places[k], :] = parts[k - 1][1]
    scale = dim ** (-0.25)
    spans = tiles(long, rows)
    qf = bf(jnp.exp(mm(q_scr[...], om_ref[r]) * scale))
    qf_ref[...] = qf
    scores = lower(qf, kf_ref[...], spans)
    for (i, j), tile in scores.items():
        scores_ref[slice(*spans[i]), slice(*spans[j])] = tile
    for (a, b), part in zip(spans, times(lambda i, j: scores[i, j], kv_ref[1], spans)):
        num_ref[a:b, :] = part


def turn_kernel(n, *refs):
    gm_ref, late_ref, qf_ref, num_ref, *earlier = refs[: -n - 4]
    carried_ref, gn_ref, total_ref = refs[-n - 4 : -n - 1]
    outs, scr = refs[-n - 1 : -1], refs[-1]
    r = member(n)
    rows = outs[0].shape[0]
    places = [
        pl.ds(pl.multiple_of((r ^ k) * rows, 128), rows) for k in range(n)
    ]
    scr[...] = gm_ref[...]
    scr[places[1], :] = late_ref[0]
    carried = sum_of_side(earlier, n, True)
    carried_ref[...] = carried
    num = num_ref[...] + mm(qf_ref[...], carried, NT)
    inv = lax.rsqrt(jnp.mean(num * num, axis=1, keepdims=True) + EPSILON)
    normed = num * inv
    gm = scr[...].astype(jnp.float32)
    gn = bf((gm - normed * jnp.mean(gm * normed, axis=1, keepdims=True)) * inv)
    gn_ref[...] = gn
    scr[...] = bf(normed)
    for k in range(n):
        outs[k][...] = scr[places[k], :]
    total_ref[...] = bf(mm(gn, qf_ref[...], TN))


def back_kernel(rows, kv_ref, om_ref, kf_ref, qf_ref, scores_ref, gn_ref, carried_ref,
                gq_ref, gv_ref, gkf_ref):
    long, dim = gn_ref.shape
    r = member(long // rows)
    scale = dim ** (-0.25)
    spans = tiles(long, rows)
    gn, qf = gn_ref[...], qf_ref[...]
    gs = lower(gn, kv_ref[1], spans)
    cross = mm(gn, carried_ref[...])
    for (a, b), part in zip(spans, times(lambda i, j: gs[i, j], kf_ref[...], spans)):
        terms = bf((cross[a:b] + part) * qf[a:b].astype(jnp.float32))
        gq_ref[a:b, :] = bf(mm(terms, om_ref[r], NT) * scale)
    for (a, b), part in zip(spans, transposed_times(lambda i, j: gs[i, j], qf, spans)):
        gkf_ref[a:b, :] = part

    def scores_at(i, j):
        return scores_ref[slice(*spans[i]), slice(*spans[j])]

    for (a, b), part in zip(spans, transposed_times(scores_at, gn, spans)):
        gv_ref[a:b, :] = part


def end_kernel(n, kv_ref, om_ref, kf_ref, gq_ref, gv_ref, gkf_ref, *rest):
    later, outs, (gk_scr, gv_scr) = rest[: -n - 2], rest[-n - 2 : -2], rest[-2:]
    r, dim = member(n), om_ref.shape[1]
    rows = outs[0].shape[1]
    scale = dim ** (-0.25)
    kf, after = kf_ref[...], sum_of_side(later, n, False)
    gv_scr[...] = bf(gv_ref[...] + mm(kf, after, NT))
    gkf = gkf_ref[...] + mm(kv_ref[1], after)
    terms = bf(gkf * kf.astype(jnp.float32))
    total = jnp.sum(terms.astype(jnp.float32), axis=1, keepdims=True)
    wide = kv_ref[0].astype(jnp.float32)
    gk_scr[...] = bf(mm(terms, om_ref[r], NT) * scale - total * wide * (scale * scale))
    for k in range(n):
        at = pl.ds(pl.multiple_of((r ^ k) * rows, 128), rows)
        outs[k][0] = gq_ref[at, :]
        outs[k][1] = gk_scr[at, :]
        outs[k][2] = gv_scr[at, :]


def mixed_project_kernel(n, offsets, *refs):
    mixed_in, (w_ref, _, own_ref, *sent, scr) = refs[:n][::-1], refs[n:]
    r, h = member(n), lax.axis_index("head")
    width = own_ref.shape[2]
    dim = mixed_in[0].shape[1]
    half = len(offsets) // 2
    for k in range(n):
        scr[:, lane(r ^ k, dim)] = mixed_in[k][...]
    mixed = scr[...]
    for at, offset in enumerate(offsets):
        part = bf(mm(mixed, w_ref[:, lane(h ^ offset, width)]))
        if at < half:
            own_ref[at] = part
        else:
            step = sent[0].shape[1]
            for i, ref in enumerate(sent):
                ref[at - half] = part[i * step : (i + 1) * step]


def unpack_kernel(ks, n, *refs):
    got, (*outs, sems) = refs[: len(ks)], refs[len(ks) :]
    r = member(n)
    dim = got[0].shape[2]
    copies = [
        pltpu.make_async_copy(ref.at[at], out.at[:, lane(r ^ k, dim)], sems.at[i, at])
        for i, (k, ref) in enumerate(zip(ks, got))
        for at, out in enumerate(outs)
    ]
    for copy in copies:
        copy.start()
    for copy in copies:
        copy.wait()


def last_kernel(n, got_ref, part_ref, last_ref, *refs):
    (out_ref, *outs), (scr, sems) = refs[3:-2], refs[-2:]
    r = member(n)
    dim = got_ref.shape[2]
    copies = [
        pltpu.make_async_copy(got_ref.at[at], out.at[:, lane(r ^ 1, dim)], sems.at[at])
        for at, out in enumerate(outs)
    ]
    for copy in copies:
        copy.start()
    scr[...] = bf(part_ref[...] + last_ref[...].astype(jnp.float32))
    copies.append(pltpu.make_async_copy(scr, out_ref, sems.at[3]))
    copies[-1].start()
    for copy in copies:
        copy.wait()


def local(queries, key_vectors, value_vectors, feature_proj, out_weight, grad_output):
    n, dim, feats = feature_proj.shape
    rows, width = grad_output.shape
    split = lax.axis_size("head")
    bits = bits_of(split)
    long = n * rows
    macs = long * dim * feats * 2
    f32 = jnp.float32

    offsets, blocks = [0], [grad_output]
    for bit in reversed(bits):
        blocks = blocks + [swap(b, "head", bit) for b in blocks]
        offsets = offsets + [o ^ bit for o in offsets]
    sends = call(
        functools.partial(pack_kernel, n),
        [struct((3 if k == 1 else 2, rows, dim)) for k in range(1, n)],
        queries, key_vectors, value_vectors,
        specs=[ANY] * 3, scratch=[pltpu.SemaphoreType.DMA((n - 1, 3))], vmem=53.68,
    )
    got = exchange(sends)
    (mark,) = call(mark_kernel, [struct((8, 128), f32)], blocks[offsets.index(1)], specs=[ANY], flops=10**10)
    (gm_early,) = call(
        functools.partial(early_blocks_kernel, offsets[:-1]),
        [struct((rows, n * dim), f32)],
        *blocks[:-1], out_weight, mark, flops=2 * rows * out_weight.size,
        specs=[VMEM] * split + [ANY],
    )
    gm_parts = call(
        functools.partial(grad_mixed_kernel, n, offsets[-1]),
        [struct((1 if k < 2 else 2, rows, dim)) for k in range(n)],
        queries, gm_early, blocks[-1], out_weight, flops=2 * rows * out_weight.size,
        scratch=[pltpu.VMEM((rows, n * dim), jnp.bfloat16)],
    )
    gm_in = exchange(gm_parts[1:]) + [gm_parts[0]]
    kv, kf, total = call(
        functools.partial(first_kernel, n),
        [
            struct((2, long, dim)),
            struct((long, feats)),
            struct((dim, feats)),
        ],
        *got, key_vectors, value_vectors, feature_proj, gm_parts[0],
        flops=2 * macs, specs=[VMEM] * (n + 2) + [ANY],
    )
    earlier = swap_totals(total, n)
    gm, qf, scores, num = call(
        functools.partial(inner_kernel, n),
        [struct((long, dim)), struct((long, feats)), struct((long, long)), struct((long, dim), f32)],
        *gm_in[:-2], gm_in[-1], queries, got[-1], kv, feature_proj, kf, flops=16 * macs,
        scratch=[pltpu.VMEM((long, dim), jnp.bfloat16)],
    )
    carried, gn, later_total, *mixed_parts = call(
        functools.partial(turn_kernel, n),
        [
            struct((dim, feats)),
            struct((long, dim)),
            struct((dim, feats)),
        ]
        + [struct((rows, dim))] * n,
        gm, gm_in[-2], qf, num, *earlier, flops=2 * macs,
        scratch=[pltpu.VMEM((long, dim), jnp.bfloat16)],
    )
    after = swap_totals(later_total, n)
    mixed_in = exchange(mixed_parts[1:]) + [mixed_parts[0]]
    gq, gv_part, gkf_part = call(
        functools.partial(back_kernel, rows),
        [struct((long, dim)), struct((long, dim), f32), struct((long, feats), f32)],
        kv, feature_proj, kf, qf, scores, gn, carried, flops=8 * macs,
    )
    grads = call(
        functools.partial(end_kernel, n),
        [struct((3, rows, dim))] * n,
        kv, feature_proj, kf, gq, gv_part, gkf_part, *after, flops=3 * macs,
        scratch=[pltpu.VMEM((long, dim), jnp.bfloat16)] * 2,
    )
    grads_in = exchange(grads[1:]) + [grads[0]]

    order = [o for o in range(split) if not o & 1] + [o for o in range(split) if o & 1]
    own, *sent = call(
        functools.partial(mixed_project_kernel, n, order),
        [struct((split // 2, rows, width))]
        + [struct((split // 2, rows, width))],
        *mixed_in, out_weight, grads[0], flops=2 * rows * out_weight.size,
        specs=[VMEM] * (n + 1) + [ANY],
        scratch=[pltpu.VMEM((rows, n * dim), jnp.bfloat16)],
    )
    part, last = reduce_blocks(own, sent, bits)
    *early, late, own_grads = grads_in
    ks = [k for k in range(n - 1, 1, -1)] + [0]
    arrays = [struct((rows, n * dim))] * 3
    partial_grads = call(
        functools.partial(unpack_kernel, ks, n), arrays,
        *early, own_grads, flops=8 * 10**8,
        out_specs=[ANY] * 3, scratch=[pltpu.SemaphoreType.DMA((n - 1, 3))],
    )
    return call(
        functools.partial(last_kernel, n),
        [struct((rows, width))] + arrays,
        late, part, last, *partial_grads,
        specs=[VMEM] * 3 + [ANY] * 3, out_specs=[ANY] * 4,
        aliases={3: 1, 4: 2, 5: 3},
        scratch=[pltpu.VMEM((rows, width), jnp.bfloat16), pltpu.SemaphoreType.DMA((4,))],
    )


def solution(mesh):
    placed = (
        P("seq", "head"),
        P("seq", "head"),
        P("seq", "head"),
        P("head", None, None),
        P("head", None),
        P("seq", "head"),
    )
    return jax.shard_map(
        local,
        mesh=mesh,
        in_specs=placed,
        out_specs=(P("seq", "head"),) * 4,
        check_vma=False,
    )
```

```python
import functools

import jax
import jax.numpy as jnp
from jax import lax
from jax.experimental import pallas as pl
from jax.experimental.pallas import tpu as pltpu
from jax.sharding import PartitionSpec as P

EPSILON = 1e-05
VMEM = pl.BlockSpec(memory_space=pltpu.VMEM)
ANY = pl.BlockSpec(memory_space=pl.ANY)
NN = (((1,), (0,)), ((), ()))
NT = (((1,), (1,)), ((), ()))
TN = (((0,), (0,)), ((), ()))


def mm(a, b, dims=NN):
    return lax.dot_general(a, b, dims, preferred_element_type=jnp.float32)


def bf(x):
    return x.astype(jnp.bfloat16)


def call(body, outs, *args, flops=0, specs=None, out_specs=None, scratch=(), vmem=32, aliases=None):
    size = sum(a.size * a.dtype.itemsize for a in args)
    size += sum(o.size * o.dtype.itemsize for o in outs)
    return pl.pallas_call(
        body,
        out_shape=outs,
        in_specs=specs or [VMEM] * len(args),
        out_specs=out_specs or [VMEM] * len(outs),
        scratch_shapes=list(scratch),
        input_output_aliases=aliases or {},
        cost_estimate=pl.CostEstimate(flops=flops, bytes_accessed=size, transcendentals=0),
        compiler_params=pltpu.CompilerParams(vmem_limit_bytes=int(vmem * 1024 * 1024)),
    )(*args)


def struct(shape, dtype=jnp.bfloat16):
    return jax.ShapeDtypeStruct(shape, dtype)


def tiles(long, rows):
    size = 256 if long % 256 == 0 else rows
    return [(at, at + size) for at in range(0, long, size)]


def causal(scores):
    row = lax.broadcasted_iota(jnp.int32, scores.shape, 0)
    col = lax.broadcasted_iota(jnp.int32, scores.shape, 1)
    return jnp.where(col <= row, scores, 0.0)


def lower(left, right, spans):
    out = {}
    for i, (a, b) in enumerate(spans):
        for j, (c, d) in enumerate(spans[: i + 1]):
            tile = mm(left[a:b], right[c:d], NT)
            out[i, j] = bf(causal(tile) if i == j else tile)
    return out


def times(tile_at, right, spans):
    return [
        sum(mm(tile_at(i, j), right[c:d]) for j, (c, d) in enumerate(spans[: i + 1]))
        for i in range(len(spans))
    ]


def transposed_times(tile_at, right, spans):
    return [
        sum(mm(tile_at(i, j), right[a:b], TN) for i, (a, b) in enumerate(spans) if i >= j)
        for j in range(len(spans))
    ]


def swap(array, axis, bit):
    size = lax.axis_size(axis)
    return lax.ppermute(array, axis, [(i, i ^ bit) for i in range(size)])


def bits_of(size):
    return [1 << b for b in range(size.bit_length() - 1)]


def sum_kernel(*refs):
    out_ref = refs[-1]
    out_ref[...] = bf(sum(ref[...].astype(jnp.float32) for ref in refs[:-2]))


def reduce_blocks(parts, bits):
    held = {o: [part] for o, part in enumerate(parts)}
    for bit in bits:
        for o in reversed(range(bit, len(parts), 2 * bit)):
            block = held[o][0]
            if bit > 1:
                (mark,) = call(
                    mark_kernel, [struct((8, 128), jnp.float32)], block, specs=[ANY],
                    flops=28 * 10**8,
                )
                (block,) = call(
                    sum_kernel, [struct(block.shape)], *held[o], mark,
                    specs=[VMEM] * len(held[o]) + [ANY],
                )
            held[o ^ bit].append(swap(block, "head", bit))
    return held[0]


def member(n):
    return lax.rem(lax.axis_index("seq"), n)


def exchange(parts):
    return [swap(part, "seq", k) for k, part in enumerate(parts, 1)][::-1]


def swap_totals(total, n):
    size, step, got = lax.axis_size("seq"), n, []
    while step < size:
        got.append(swap(bf(total), "seq", step))
        total = total.astype(jnp.float32) + got[-1].astype(jnp.float32)
        step *= 2
    return got


def sum_of_side(refs, n, earlier):
    group = lax.div(lax.axis_index("seq"), n)
    total = jnp.zeros(refs[0].shape, jnp.float32)
    for at, ref in enumerate(refs):
        from_earlier = lax.rem(lax.shift_right_logical(group, at), 2) == 1
        keep = from_earlier if earlier else jnp.logical_not(from_earlier)
        total = total + jnp.where(keep, ref[...].astype(jnp.float32), 0.0)
    return bf(total)


def lane(index, width):
    return pl.ds(pl.multiple_of(index * width, 128), width)


def pack_kernel(n, q_ref, k_ref, v_ref, *rest):
    outs, sems = rest[:-1], rest[-1]
    r = member(n)
    dim = outs[0].shape[2]
    copies = [
        pltpu.make_async_copy(ref.at[:, lane(r ^ k, dim)], out.at[at], sems.at[k - 1, at])
        for k, out in enumerate(outs, 1)
        for at, ref in enumerate((q_ref, k_ref, v_ref)[-out.shape[0] :])
    ]
    for copy in copies:
        copy.start()
    for copy in copies:
        copy.wait()


def mark_kernel(_, out_ref):
    out_ref[...] = jnp.zeros(out_ref.shape, out_ref.dtype)


def early_blocks_kernel(offsets, *refs):
    blocks, w_ref, total_ref = refs[: len(offsets)], refs[-3], refs[-1]
    h = lax.axis_index("head")
    width = blocks[0].shape[1]
    total = None
    for offset, ref in zip(offsets, blocks):
        part = mm(ref[...], w_ref[:, lane(h ^ offset, width)], NT)
        total = part if total is None else total + part
    total_ref[...] = total


def grad_mixed_kernel(n, offset, q_ref, total_ref, block_ref, w_ref, *refs):
    outs, scr = refs[:-1], refs[-1]
    r, h = member(n), lax.axis_index("head")
    width = block_ref.shape[1]
    dim = outs[0].shape[2]
    scr[...] = bf(total_ref[...] + mm(block_ref[...], w_ref[:, lane(h ^ offset, width)], NT))
    for k in range(n):
        outs[k][0] = scr[:, lane(r ^ k, dim)]
        if k > 1:
            outs[k][1] = q_ref[:, lane(r ^ k, dim)]


def first_kernel(n, *refs):
    got, own, om_ref = refs[: n - 1][::-1], refs[n - 1 : n + 1], refs[n + 1]
    kv_ref, kf_ref, total_ref = refs[n + 3 :]
    r = member(n)
    rows, dim = own[0].shape[0], om_ref.shape[1]
    scale = dim ** (-0.25)
    for k in range(n):
        at = pl.ds(pl.multiple_of((r ^ k) * rows, 128), rows)
        if k:
            kv_ref[:, at, :] = got[k - 1][-2:]
        else:
            for i, ref in enumerate(own):
                kv_ref[i, at, :] = ref[:, lane(r, dim)]
    k_all = kv_ref[0]
    wide = k_all.astype(jnp.float32)
    half_sq = jnp.sum(wide * wide, axis=1, keepdims=True) * (scale * scale * 0.5)
    kf = bf(jnp.exp(mm(k_all, om_ref[r]) * scale - half_sq))
    kf_ref[...] = kf
    total_ref[...] = bf(mm(kv_ref[1], kf, TN))


def inner_kernel(n, *refs):
    parts, (own_ref, first_ref, kv_ref, om_ref, kf_ref) = refs[: n - 1][::-1], refs[n - 1 : n + 4]
    gm_ref, qf_ref, scores_ref, num_ref, q_scr = refs[n + 4 :]
    long, dim = num_ref.shape
    rows = long // n
    r = member(n)
    places = [pl.ds(pl.multiple_of((r ^ k) * rows, 128), rows) for k in range(n)]
    gm_ref[places[0], :] = parts[0][0]
    q_scr[places[0], :] = own_ref[:, lane(r, dim)]
    gm_ref[places[1], :] = jnp.zeros((rows, dim), gm_ref.dtype)
    q_scr[places[1], :] = first_ref[0]
    for k in range(2, n):
        gm_ref[places[k], :] = parts[k - 1][0]
        q_scr[places[k], :] = parts[k - 1][1]
    scale = dim ** (-0.25)
    spans = tiles(long, rows)
    qf = bf(jnp.exp(mm(q_scr[...], om_ref[r]) * scale))
    qf_ref[...] = qf
    scores = lower(qf, kf_ref[...], spans)
    for (i, j), tile in scores.items():
        scores_ref[slice(*spans[i]), slice(*spans[j])] = tile
    for (a, b), part in zip(spans, times(lambda i, j: scores[i, j], kv_ref[1], spans)):
        num_ref[a:b, :] = part


def turn_kernel(n, *refs):
    gm_ref, late_ref, qf_ref, num_ref, *earlier = refs[: -n - 4]
    carried_ref, gn_ref, total_ref = refs[-n - 4 : -n - 1]
    outs, scr = refs[-n - 1 : -1], refs[-1]
    r = member(n)
    rows = outs[0].shape[0]
    places = [
        pl.ds(pl.multiple_of((r ^ k) * rows, 128), rows) for k in range(n)
    ]
    scr[...] = gm_ref[...]
    scr[places[1], :] = late_ref[0]
    carried = sum_of_side(earlier, n, True)
    carried_ref[...] = carried
    num = num_ref[...] + mm(qf_ref[...], carried, NT)
    inv = lax.rsqrt(jnp.mean(num * num, axis=1, keepdims=True) + EPSILON)
    normed = num * inv
    gm = scr[...].astype(jnp.float32)
    gn = bf((gm - normed * jnp.mean(gm * normed, axis=1, keepdims=True)) * inv)
    gn_ref[...] = gn
    scr[...] = bf(normed)
    for k in range(n):
        outs[k][...] = scr[places[k], :]
    total_ref[...] = bf(mm(gn, qf_ref[...], TN))


def back_kernel(rows, kv_ref, om_ref, kf_ref, qf_ref, scores_ref, gn_ref, carried_ref,
                gq_ref, gv_ref, gkf_ref):
    long, dim = gn_ref.shape
    r = member(long // rows)
    scale = dim ** (-0.25)
    spans = tiles(long, rows)
    gn, qf = gn_ref[...], qf_ref[...]
    gs = lower(gn, kv_ref[1], spans)
    cross = mm(gn, carried_ref[...])
    for (a, b), part in zip(spans, times(lambda i, j: gs[i, j], kf_ref[...], spans)):
        terms = bf((cross[a:b] + part) * qf[a:b].astype(jnp.float32))
        gq_ref[a:b, :] = bf(mm(terms, om_ref[r], NT) * scale)
    for (a, b), part in zip(spans, transposed_times(lambda i, j: gs[i, j], qf, spans)):
        gkf_ref[a:b, :] = part

    def scores_at(i, j):
        return scores_ref[slice(*spans[i]), slice(*spans[j])]

    for (a, b), part in zip(spans, transposed_times(scores_at, gn, spans)):
        gv_ref[a:b, :] = part


def end_kernel(n, kv_ref, om_ref, kf_ref, gq_ref, gv_ref, gkf_ref, *rest):
    later, outs, (gk_scr, gv_scr) = rest[: -n - 2], rest[-n - 2 : -2], rest[-2:]
    r, dim = member(n), om_ref.shape[1]
    rows = outs[0].shape[1]
    scale = dim ** (-0.25)
    kf, after = kf_ref[...], sum_of_side(later, n, False)
    gv_scr[...] = bf(gv_ref[...] + mm(kf, after, NT))
    gkf = gkf_ref[...] + mm(kv_ref[1], after)
    terms = bf(gkf * kf.astype(jnp.float32))
    total = jnp.sum(terms.astype(jnp.float32), axis=1, keepdims=True)
    wide = kv_ref[0].astype(jnp.float32)
    gk_scr[...] = bf(mm(terms, om_ref[r], NT) * scale - total * wide * (scale * scale))
    for k in range(n):
        at = pl.ds(pl.multiple_of((r ^ k) * rows, 128), rows)
        outs[k][0] = gq_ref[at, :]
        outs[k][1] = gk_scr[at, :]
        outs[k][2] = gv_scr[at, :]


def mixed_project_kernel(n, *refs):
    mixed_in, (w_ref, _, *outs, scr) = refs[:n][::-1], refs[n:]
    r, h = member(n), lax.axis_index("head")
    width = outs[0].shape[1]
    dim = mixed_in[0].shape[1]
    for k in range(n):
        scr[:, lane(r ^ k, dim)] = mixed_in[k][...]
    mixed = scr[...]
    for offset in reversed(range(len(outs))):
        outs[offset][...] = bf(mm(mixed, w_ref[:, lane(h ^ offset, width)]))


def unpack_kernel(ks, n, *refs):
    got, (*outs, sems) = refs[: len(ks)], refs[len(ks) :]
    r = member(n)
    dim = got[0].shape[2]
    copies = [
        pltpu.make_async_copy(ref.at[at], out.at[:, lane(r ^ k, dim)], sems.at[i, at])
        for i, (k, ref) in enumerate(zip(ks, got))
        for at, out in enumerate(outs)
    ]
    for copy in copies:
        copy.start()
    for copy in copies:
        copy.wait()


def last_kernel(n, got_ref, *refs):
    parts, (out_ref, *outs), (scr, sems) = refs[:-9], refs[-6:-2], refs[-2:]
    r = member(n)
    dim = got_ref.shape[2]
    copies = [
        pltpu.make_async_copy(got_ref.at[at], out.at[:, lane(r ^ 1, dim)], sems.at[at])
        for at, out in enumerate(outs)
    ]
    for copy in copies:
        copy.start()
    scr[...] = bf(sum(ref[...].astype(jnp.float32) for ref in parts))
    copies.append(pltpu.make_async_copy(scr, out_ref, sems.at[3]))
    copies[-1].start()
    for copy in copies:
        copy.wait()


def local(queries, key_vectors, value_vectors, feature_proj, out_weight, grad_output):
    n, dim, feats = feature_proj.shape
    rows, width = grad_output.shape
    split = lax.axis_size("head")
    bits = bits_of(split)
    long = n * rows
    macs = long * dim * feats * 2
    f32 = jnp.float32

    offsets, blocks = [0], [grad_output]
    for bit in reversed(bits):
        blocks = blocks + [swap(b, "head", bit) for b in blocks]
        offsets = offsets + [o ^ bit for o in offsets]
    sends = call(
        functools.partial(pack_kernel, n),
        [struct((3 if k == 1 else 2, rows, dim)) for k in range(1, n)],
        queries, key_vectors, value_vectors,
        specs=[ANY] * 3, scratch=[pltpu.SemaphoreType.DMA((n - 1, 3))], vmem=53.68,
    )
    got = exchange(sends)
    (mark,) = call(mark_kernel, [struct((8, 128), f32)], blocks[offsets.index(1)], specs=[ANY], flops=10**10)
    (gm_early,) = call(
        functools.partial(early_blocks_kernel, offsets[:-1]),
        [struct((rows, n * dim), f32)],
        *blocks[:-1], out_weight, mark, flops=2 * rows * out_weight.size,
        specs=[VMEM] * split + [ANY],
    )
    gm_parts = call(
        functools.partial(grad_mixed_kernel, n, offsets[-1]),
        [struct((1 if k < 2 else 2, rows, dim)) for k in range(n)],
        queries, gm_early, blocks[-1], out_weight, flops=2 * rows * out_weight.size,
        scratch=[pltpu.VMEM((rows, n * dim), jnp.bfloat16)],
    )
    gm_in = exchange(gm_parts[1:]) + [gm_parts[0]]
    kv, kf, total = call(
        functools.partial(first_kernel, n),
        [
            struct((2, long, dim)),
            struct((long, feats)),
            struct((dim, feats)),
        ],
        *got, key_vectors, value_vectors, feature_proj, gm_parts[0],
        flops=2 * macs, specs=[VMEM] * (n + 2) + [ANY],
    )
    earlier = swap_totals(total, n)
    gm, qf, scores, num = call(
        functools.partial(inner_kernel, n),
        [struct((long, dim)), struct((long, feats)), struct((long, long)), struct((long, dim), f32)],
        *gm_in[:-2], gm_in[-1], queries, got[-1], kv, feature_proj, kf, flops=16 * macs,
        scratch=[pltpu.VMEM((long, dim), jnp.bfloat16)],
    )
    carried, gn, later_total, *mixed_parts = call(
        functools.partial(turn_kernel, n),
        [
            struct((dim, feats)),
            struct((long, dim)),
            struct((dim, feats)),
        ]
        + [struct((rows, dim))] * n,
        gm, gm_in[-2], qf, num, *earlier, flops=2 * macs,
        scratch=[pltpu.VMEM((long, dim), jnp.bfloat16)],
    )
    after = swap_totals(later_total, n)
    mixed_in = exchange(mixed_parts[1:]) + [mixed_parts[0]]
    gq, gv_part, gkf_part = call(
        functools.partial(back_kernel, rows),
        [struct((long, dim)), struct((long, dim), f32), struct((long, feats), f32)],
        kv, feature_proj, kf, qf, scores, gn, carried, flops=8 * macs,
    )
    grads = call(
        functools.partial(end_kernel, n),
        [struct((3, rows, dim))] * n,
        kv, feature_proj, kf, gq, gv_part, gkf_part, *after, flops=3 * macs,
        scratch=[pltpu.VMEM((long, dim), jnp.bfloat16)] * 2,
    )
    grads_in = exchange(grads[1:]) + [grads[0]]

    parts = call(
        functools.partial(mixed_project_kernel, n),
        [struct((rows, width))] * split,
        *mixed_in, out_weight, grads[0], flops=2 * rows * out_weight.size,
        specs=[VMEM] * (n + 1) + [ANY],
        scratch=[pltpu.VMEM((rows, n * dim), jnp.bfloat16)],
    )
    kept = reduce_blocks(parts, bits)
    *early, late, own_grads = grads_in
    ks = [k for k in range(n - 1, 1, -1)] + [0]
    arrays = [struct((rows, n * dim))] * 3
    partial_grads = call(
        functools.partial(unpack_kernel, ks, n), arrays,
        *early, own_grads, flops=8 * 10**8,
        out_specs=[ANY] * 3, scratch=[pltpu.SemaphoreType.DMA((n - 1, 3))],
    )
    return call(
        functools.partial(last_kernel, n),
        [struct((rows, width))] + arrays,
        late, *kept, *partial_grads,
        specs=[VMEM] * (1 + len(kept)) + [ANY] * 3, out_specs=[ANY] * 4,
        aliases={1 + len(kept) + i: 1 + i for i in range(3)},
        scratch=[pltpu.VMEM((rows, width), jnp.bfloat16), pltpu.SemaphoreType.DMA((4,))],
    )


def solution(mesh):
    placed = (
        P("seq", "head"),
        P("seq", "head"),
        P("seq", "head"),
        P("head", None, None),
        P("head", None),
        P("seq", "head"),
    )
    return jax.shard_map(
        local,
        mesh=mesh,
        in_specs=placed,
        out_specs=(P("seq", "head"),) * 4,
        check_vma=False,
    )
```

```python
import functools

import jax
import jax.numpy as jnp
from jax import lax
from jax.experimental import pallas as pl
from jax.experimental.pallas import tpu as pltpu
from jax.sharding import PartitionSpec as P

EPSILON = 1e-05
VMEM = pl.BlockSpec(memory_space=pltpu.VMEM)
ANY = pl.BlockSpec(memory_space=pl.ANY)
NN = (((1,), (0,)), ((), ()))
NT = (((1,), (1,)), ((), ()))
TN = (((0,), (0,)), ((), ()))


def mm(a, b, dims=NN):
    return lax.dot_general(a, b, dims, preferred_element_type=jnp.float32)


def bf(x):
    return x.astype(jnp.bfloat16)


def call(body, outs, *args, flops=0, specs=None, out_specs=None, scratch=(), vmem=32, aliases=None):
    size = sum(a.size * a.dtype.itemsize for a in args)
    size += sum(o.size * o.dtype.itemsize for o in outs)
    return pl.pallas_call(
        body,
        out_shape=outs,
        in_specs=specs or [VMEM] * len(args),
        out_specs=out_specs or [VMEM] * len(outs),
        scratch_shapes=list(scratch),
        input_output_aliases=aliases or {},
        cost_estimate=pl.CostEstimate(flops=flops, bytes_accessed=size, transcendentals=0),
        compiler_params=pltpu.CompilerParams(vmem_limit_bytes=int(vmem * 1024 * 1024)),
    )(*args)


def struct(shape, dtype=jnp.bfloat16):
    return jax.ShapeDtypeStruct(shape, dtype)


def tiles(long, rows):
    size = 256 if long % 256 == 0 else rows
    return [(at, at + size) for at in range(0, long, size)]


def causal(scores):
    row = lax.broadcasted_iota(jnp.int32, scores.shape, 0)
    col = lax.broadcasted_iota(jnp.int32, scores.shape, 1)
    return jnp.where(col <= row, scores, 0.0)


def lower(left, right, spans):
    out = {}
    for i, (a, b) in enumerate(spans):
        for j, (c, d) in enumerate(spans[: i + 1]):
            tile = mm(left[a:b], right[c:d], NT)
            out[i, j] = bf(causal(tile) if i == j else tile)
    return out


def times(tile_at, right, spans):
    return [
        sum(mm(tile_at(i, j), right[c:d]) for j, (c, d) in enumerate(spans[: i + 1]))
        for i in range(len(spans))
    ]


def transposed_times(tile_at, right, spans):
    return [
        sum(mm(tile_at(i, j), right[a:b], TN) for i, (a, b) in enumerate(spans) if i >= j)
        for j in range(len(spans))
    ]


def swap(array, axis, bit):
    size = lax.axis_size(axis)
    return lax.ppermute(array, axis, [(i, i ^ bit) for i in range(size)])


def bits_of(size):
    return [1 << b for b in range(size.bit_length() - 1)]


def sum_kernel(*refs):
    out_ref = refs[-1]
    out_ref[...] = bf(sum(ref[...].astype(jnp.float32) for ref in refs[:-1]))


def reduce_blocks(parts, bits):
    held = {o: [part] for o, part in enumerate(parts)}
    for bit in bits:
        for o in reversed(range(bit, len(parts), 2 * bit)):
            block = held[o][0]
            if bit > 1:
                (block,) = call(sum_kernel, [struct(block.shape)], *held[o])
            held[o ^ bit].append(swap(block, "head", bit))
    return held[0]


def member(n):
    return lax.rem(lax.axis_index("seq"), n)


def exchange(parts):
    return [swap(part, "seq", k) for k, part in enumerate(parts, 1)][::-1]


def swap_totals(total, n):
    size, step, got = lax.axis_size("seq"), n, []
    while step < size:
        got.append(swap(bf(total), "seq", step))
        total = total.astype(jnp.float32) + got[-1].astype(jnp.float32)
        step *= 2
    return got


def sum_of_side(refs, n, earlier):
    group = lax.div(lax.axis_index("seq"), n)
    total = jnp.zeros(refs[0].shape, jnp.float32)
    for at, ref in enumerate(refs):
        from_earlier = lax.rem(lax.shift_right_logical(group, at), 2) == 1
        keep = from_earlier if earlier else jnp.logical_not(from_earlier)
        total = total + jnp.where(keep, ref[...].astype(jnp.float32), 0.0)
    return bf(total)


def lane(index, width):
    return pl.ds(pl.multiple_of(index * width, 128), width)


def pack_kernel(n, q_ref, k_ref, v_ref, *rest):
    outs, sems = rest[:-1], rest[-1]
    r = member(n)
    dim = outs[0].shape[2]
    copies = [
        pltpu.make_async_copy(ref.at[:, lane(r ^ k, dim)], out.at[at], sems.at[k - 1, at])
        for k, out in enumerate(outs, 1)
        for at, ref in enumerate((q_ref, k_ref, v_ref)[-out.shape[0] :])
    ]
    for copy in copies:
        copy.start()
    for copy in copies:
        copy.wait()


def mark_kernel(_, out_ref):
    out_ref[...] = jnp.zeros(out_ref.shape, out_ref.dtype)


def early_blocks_kernel(offsets, *refs):
    blocks, w_ref, total_ref = refs[: len(offsets)], refs[-3], refs[-1]
    h = lax.axis_index("head")
    width = blocks[0].shape[1]
    total = None
    for offset, ref in zip(offsets, blocks):
        part = mm(ref[...], w_ref[:, lane(h ^ offset, width)], NT)
        total = part if total is None else total + part
    total_ref[...] = total


def grad_mixed_kernel(n, offset, q_ref, total_ref, block_ref, w_ref, *refs):
    outs, scr = refs[:-1], refs[-1]
    r, h = member(n), lax.axis_index("head")
    width = block_ref.shape[1]
    dim = outs[0].shape[2]
    scr[...] = bf(total_ref[...] + mm(block_ref[...], w_ref[:, lane(h ^ offset, width)], NT))
    for k in range(n):
        outs[k][0] = scr[:, lane(r ^ k, dim)]
        if k > 1:
            outs[k][1] = q_ref[:, lane(r ^ k, dim)]


def first_kernel(n, *refs):
    got, own, om_ref = refs[: n - 1][::-1], refs[n - 1 : n + 1], refs[n + 1]
    kv_ref, kf_ref, total_ref = refs[n + 3 :]
    r = member(n)
    rows, dim = own[0].shape[0], om_ref.shape[1]
    scale = dim ** (-0.25)
    for k in range(n):
        at = pl.ds(pl.multiple_of((r ^ k) * rows, 128), rows)
        if k:
            kv_ref[:, at, :] = got[k - 1][-2:]
        else:
            for i, ref in enumerate(own):
                kv_ref[i, at, :] = ref[:, lane(r, dim)]
    k_all = kv_ref[0]
    wide = k_all.astype(jnp.float32)
    half_sq = jnp.sum(wide * wide, axis=1, keepdims=True) * (scale * scale * 0.5)
    kf = bf(jnp.exp(mm(k_all, om_ref[r]) * scale - half_sq))
    kf_ref[...] = kf
    total_ref[...] = bf(mm(kv_ref[1], kf, TN))


def inner_kernel(n, *refs):
    parts, (own_ref, first_ref, kv_ref, om_ref, kf_ref) = refs[: n - 1][::-1], refs[n - 1 : n + 4]
    gm_ref, qf_ref, scores_ref, num_ref, q_scr = refs[n + 4 :]
    long, dim = num_ref.shape
    rows = long // n
    r = member(n)
    places = [pl.ds(pl.multiple_of((r ^ k) * rows, 128), rows) for k in range(n)]
    gm_ref[places[0], :] = parts[0][0]
    q_scr[places[0], :] = own_ref[:, lane(r, dim)]
    gm_ref[places[1], :] = jnp.zeros((rows, dim), gm_ref.dtype)
    q_scr[places[1], :] = first_ref[0]
    for k in range(2, n):
        gm_ref[places[k], :] = parts[k - 1][0]
        q_scr[places[k], :] = parts[k - 1][1]
    scale = dim ** (-0.25)
    spans = tiles(long, rows)
    qf = bf(jnp.exp(mm(q_scr[...], om_ref[r]) * scale))
    qf_ref[...] = qf
    scores = lower(qf, kf_ref[...], spans)
    for (i, j), tile in scores.items():
        scores_ref[slice(*spans[i]), slice(*spans[j])] = tile
    for (a, b), part in zip(spans, times(lambda i, j: scores[i, j], kv_ref[1], spans)):
        num_ref[a:b, :] = part


def turn_kernel(n, *refs):
    gm_ref, late_ref, qf_ref, num_ref, *earlier = refs[: -n - 4]
    carried_ref, gn_ref, total_ref = refs[-n - 4 : -n - 1]
    outs, scr = refs[-n - 1 : -1], refs[-1]
    r = member(n)
    rows = outs[0].shape[0]
    places = [
        pl.ds(pl.multiple_of((r ^ k) * rows, 128), rows) for k in range(n)
    ]
    scr[...] = gm_ref[...]
    scr[places[1], :] = late_ref[0]
    carried = sum_of_side(earlier, n, True)
    carried_ref[...] = carried
    num = num_ref[...] + mm(qf_ref[...], carried, NT)
    inv = lax.rsqrt(jnp.mean(num * num, axis=1, keepdims=True) + EPSILON)
    normed = num * inv
    gm = scr[...].astype(jnp.float32)
    gn = bf((gm - normed * jnp.mean(gm * normed, axis=1, keepdims=True)) * inv)
    gn_ref[...] = gn
    scr[...] = bf(normed)
    for k in range(n):
        outs[k][...] = scr[places[k], :]
    total_ref[...] = bf(mm(gn, qf_ref[...], TN))


def back_kernel(rows, kv_ref, om_ref, kf_ref, qf_ref, scores_ref, gn_ref, carried_ref,
                gq_ref, gv_ref, gkf_ref):
    long, dim = gn_ref.shape
    r = member(long // rows)
    scale = dim ** (-0.25)
    spans = tiles(long, rows)
    gn, qf = gn_ref[...], qf_ref[...]
    gs = lower(gn, kv_ref[1], spans)
    cross = mm(gn, carried_ref[...])
    for (a, b), part in zip(spans, times(lambda i, j: gs[i, j], kf_ref[...], spans)):
        terms = bf((cross[a:b] + part) * qf[a:b].astype(jnp.float32))
        gq_ref[a:b, :] = bf(mm(terms, om_ref[r], NT) * scale)
    for (a, b), part in zip(spans, transposed_times(lambda i, j: gs[i, j], qf, spans)):
        gkf_ref[a:b, :] = part

    def scores_at(i, j):
        return scores_ref[slice(*spans[i]), slice(*spans[j])]

    for (a, b), part in zip(spans, transposed_times(scores_at, gn, spans)):
        gv_ref[a:b, :] = part


def end_kernel(n, kv_ref, om_ref, kf_ref, gq_ref, gv_ref, gkf_ref, *rest):
    later, outs, (gk_scr, gv_scr) = rest[: -n - 2], rest[-n - 2 : -2], rest[-2:]
    r, dim = member(n), om_ref.shape[1]
    rows = outs[0].shape[1]
    scale = dim ** (-0.25)
    kf, after = kf_ref[...], sum_of_side(later, n, False)
    gv_scr[...] = bf(gv_ref[...] + mm(kf, after, NT))
    gkf = gkf_ref[...] + mm(kv_ref[1], after)
    terms = bf(gkf * kf.astype(jnp.float32))
    total = jnp.sum(terms.astype(jnp.float32), axis=1, keepdims=True)
    wide = kv_ref[0].astype(jnp.float32)
    gk_scr[...] = bf(mm(terms, om_ref[r], NT) * scale - total * wide * (scale * scale))
    for k in range(n):
        at = pl.ds(pl.multiple_of((r ^ k) * rows, 128), rows)
        outs[k][0] = gq_ref[at, :]
        outs[k][1] = gk_scr[at, :]
        outs[k][2] = gv_scr[at, :]


def far_project_kernel(n, offset, *refs):
    mixed_in, (w_ref, _, mixed_ref, out_ref) = refs[:n][::-1], refs[n:]
    r, h = member(n), lax.axis_index("head")
    width = out_ref.shape[1]
    dim = mixed_in[0].shape[1]
    for k in range(n):
        mixed_ref[:, lane(r ^ k, dim)] = mixed_in[k][...]
    out_ref[...] = bf(mm(mixed_ref[...], w_ref[:, lane(h ^ offset, width)]))


def project_kernel(mixed_ref, w_ref, *outs):
    h = lax.axis_index("head")
    width = outs[0].shape[1]
    mixed = mixed_ref[...]
    for offset, out in enumerate(outs):
        out[...] = bf(mm(mixed, w_ref[:, lane(h ^ offset, width)]))


def unpack_kernel(ks, n, *refs):
    got, (*outs, sems) = refs[: len(ks)], refs[len(ks) :]
    r = member(n)
    dim = got[0].shape[2]
    copies = [
        pltpu.make_async_copy(ref.at[at], out.at[:, lane(r ^ k, dim)], sems.at[i, at])
        for i, (k, ref) in enumerate(zip(ks, got))
        for at, out in enumerate(outs)
    ]
    for copy in copies:
        copy.start()
    for copy in copies:
        copy.wait()


def last_kernel(n, got_ref, *refs):
    parts, (out_ref, *outs), (scr, sems) = refs[:-9], refs[-6:-2], refs[-2:]
    r = member(n)
    dim = got_ref.shape[2]
    copies = [
        pltpu.make_async_copy(got_ref.at[at], out.at[:, lane(r ^ 1, dim)], sems.at[at])
        for at, out in enumerate(outs)
    ]
    for copy in copies:
        copy.start()
    scr[...] = bf(sum(ref[...].astype(jnp.float32) for ref in parts))
    copies.append(pltpu.make_async_copy(scr, out_ref, sems.at[3]))
    copies[-1].start()
    for copy in copies:
        copy.wait()


def local(queries, key_vectors, value_vectors, feature_proj, out_weight, grad_output):
    n, dim, feats = feature_proj.shape
    rows, width = grad_output.shape
    split = lax.axis_size("head")
    bits = bits_of(split)
    long = n * rows
    macs = long * dim * feats * 2
    f32 = jnp.float32

    offsets, blocks = [0], [grad_output]
    for bit in reversed(bits):
        blocks = blocks + [swap(b, "head", bit) for b in blocks]
        offsets = offsets + [o ^ bit for o in offsets]
    sends = call(
        functools.partial(pack_kernel, n),
        [struct((3 if k == 1 else 2, rows, dim)) for k in range(1, n)],
        queries, key_vectors, value_vectors,
        specs=[ANY] * 3, scratch=[pltpu.SemaphoreType.DMA((n - 1, 3))], vmem=53.68,
    )
    got = exchange(sends)
    (mark,) = call(mark_kernel, [struct((8, 128), f32)], blocks[offsets.index(1)], specs=[ANY], flops=10**10)
    (gm_early,) = call(
        functools.partial(early_blocks_kernel, offsets[:-1]),
        [struct((rows, n * dim), f32)],
        *blocks[:-1], out_weight, mark, flops=2 * rows * out_weight.size,
        specs=[VMEM] * split + [ANY],
    )
    gm_parts = call(
        functools.partial(grad_mixed_kernel, n, offsets[-1]),
        [struct((1 if k < 2 else 2, rows, dim)) for k in range(n)],
        queries, gm_early, blocks[-1], out_weight, flops=2 * rows * out_weight.size,
        scratch=[pltpu.VMEM((rows, n * dim), jnp.bfloat16)],
    )
    gm_in = exchange(gm_parts[1:]) + [gm_parts[0]]
    kv, kf, total = call(
        functools.partial(first_kernel, n),
        [
            struct((2, long, dim)),
            struct((long, feats)),
            struct((dim, feats)),
        ],
        *got, key_vectors, value_vectors, feature_proj, gm_parts[0],
        flops=2 * macs, specs=[VMEM] * (n + 2) + [ANY],
    )
    earlier = swap_totals(total, n)
    gm, qf, scores, num = call(
        functools.partial(inner_kernel, n),
        [struct((long, dim)), struct((long, feats)), struct((long, long)), struct((long, dim), f32)],
        *gm_in[:-2], gm_in[-1], queries, got[-1], kv, feature_proj, kf, flops=16 * macs,
        scratch=[pltpu.VMEM((long, dim), jnp.bfloat16)],
    )
    carried, gn, later_total, *mixed_parts = call(
        functools.partial(turn_kernel, n),
        [
            struct((dim, feats)),
            struct((long, dim)),
            struct((dim, feats)),
        ]
        + [struct((rows, dim))] * n,
        gm, gm_in[-2], qf, num, *earlier, flops=2 * macs,
        scratch=[pltpu.VMEM((long, dim), jnp.bfloat16)],
    )
    after = swap_totals(later_total, n)
    mixed_in = exchange(mixed_parts[1:]) + [mixed_parts[0]]
    gq, gv_part, gkf_part = call(
        functools.partial(back_kernel, rows),
        [struct((long, dim)), struct((long, dim), f32), struct((long, feats), f32)],
        kv, feature_proj, kf, qf, scores, gn, carried, flops=8 * macs,
    )
    grads = call(
        functools.partial(end_kernel, n),
        [struct((3, rows, dim))] * n,
        kv, feature_proj, kf, gq, gv_part, gkf_part, *after, flops=3 * macs,
        scratch=[pltpu.VMEM((long, dim), jnp.bfloat16)] * 2,
    )
    grads_in = exchange(grads[1:]) + [grads[0]]

    mixed, far = call(
        functools.partial(far_project_kernel, n, split - 1),
        [struct((rows, n * dim)), struct((rows, width))],
        *mixed_in, out_weight, grads[0], flops=2 * rows * out_weight.size // split,
        specs=[VMEM] * (n + 1) + [ANY],
    )
    parts = call(
        project_kernel, [struct((rows, width))] * (split - 1), mixed, out_weight,
        flops=28 * 10**8,
    )
    parts = list(parts) + [far]
    kept = reduce_blocks(parts, bits)
    *early, late, own_grads = grads_in
    ks = [k for k in range(n - 1, 1, -1)] + [0]
    arrays = [struct((rows, n * dim))] * 3
    partial_grads = call(
        functools.partial(unpack_kernel, ks, n), arrays,
        *early, own_grads, flops=8 * 10**8,
        out_specs=[ANY] * 3, scratch=[pltpu.SemaphoreType.DMA((n - 1, 3))],
    )
    return call(
        functools.partial(last_kernel, n),
        [struct((rows, width))] + arrays,
        late, *kept, *partial_grads,
        specs=[VMEM] * (1 + len(kept)) + [ANY] * 3, out_specs=[ANY] * 4,
        aliases={1 + len(kept) + i: 1 + i for i in range(3)},
        scratch=[pltpu.VMEM((rows, width), jnp.bfloat16), pltpu.SemaphoreType.DMA((4,))],
    )


def solution(mesh):
    placed = (
        P("seq", "head"),
        P("seq", "head"),
        P("seq", "head"),
        P("head", None, None),
        P("head", None),
        P("seq", "head"),
    )
    return jax.shard_map(
        local,
        mesh=mesh,
        in_specs=placed,
        out_specs=(P("seq", "head"),) * 4,
        check_vma=False,
    )
```

```python
import functools

import jax
import jax.numpy as jnp
from jax import lax
from jax.experimental import pallas as pl
from jax.experimental.pallas import tpu as pltpu
from jax.sharding import PartitionSpec as P

EPSILON = 1e-05
VMEM = pl.BlockSpec(memory_space=pltpu.VMEM)
ANY = pl.BlockSpec(memory_space=pl.ANY)
NN = (((1,), (0,)), ((), ()))
NT = (((1,), (1,)), ((), ()))
TN = (((0,), (0,)), ((), ()))


def mm(a, b, dims=NN):
    return lax.dot_general(a, b, dims, preferred_element_type=jnp.float32)


def bf(x):
    return x.astype(jnp.bfloat16)


def call(body, outs, *args, flops=0, specs=None, out_specs=None, scratch=(), vmem=32, aliases=None):
    size = sum(a.size * a.dtype.itemsize for a in args)
    size += sum(o.size * o.dtype.itemsize for o in outs)
    return pl.pallas_call(
        body,
        out_shape=outs,
        in_specs=specs or [VMEM] * len(args),
        out_specs=out_specs or [VMEM] * len(outs),
        scratch_shapes=list(scratch),
        input_output_aliases=aliases or {},
        cost_estimate=pl.CostEstimate(flops=flops, bytes_accessed=size, transcendentals=0),
        compiler_params=pltpu.CompilerParams(vmem_limit_bytes=int(vmem * 1024 * 1024)),
    )(*args)


def struct(shape, dtype=jnp.bfloat16):
    return jax.ShapeDtypeStruct(shape, dtype)


def tiles(long, rows):
    size = 256 if long % 256 == 0 else rows
    return [(at, at + size) for at in range(0, long, size)]


def causal(scores):
    row = lax.broadcasted_iota(jnp.int32, scores.shape, 0)
    col = lax.broadcasted_iota(jnp.int32, scores.shape, 1)
    return jnp.where(col <= row, scores, 0.0)


def lower(left, right, spans):
    out = {}
    for i, (a, b) in enumerate(spans):
        for j, (c, d) in enumerate(spans[: i + 1]):
            tile = mm(left[a:b], right[c:d], NT)
            out[i, j] = bf(causal(tile) if i == j else tile)
    return out


def times(tile_at, right, spans):
    return [
        sum(mm(tile_at(i, j), right[c:d]) for j, (c, d) in enumerate(spans[: i + 1]))
        for i in range(len(spans))
    ]


def transposed_times(tile_at, right, spans):
    return [
        sum(mm(tile_at(i, j), right[a:b], TN) for i, (a, b) in enumerate(spans) if i >= j)
        for j in range(len(spans))
    ]


def swap(array, axis, bit):
    size = lax.axis_size(axis)
    return lax.ppermute(array, axis, [(i, i ^ bit) for i in range(size)])


def bits_of(size):
    return [1 << b for b in range(size.bit_length() - 1)]


def sum_kernel(*refs):
    out_ref = refs[-1]
    out_ref[...] = bf(sum(ref[...].astype(jnp.float32) for ref in refs[:-1]))


def reduce_blocks(parts, bits):
    held = {o: [part] for o, part in enumerate(parts)}
    for bit in bits:
        for o in reversed(range(bit, len(parts), 2 * bit)):
            block = held[o][0]
            if bit > 1:
                (block,) = call(sum_kernel, [struct(block.shape)], *held[o])
            held[o ^ bit].append(swap(block, "head", bit))
    return held[0]


def member(n):
    return lax.rem(lax.axis_index("seq"), n)


def exchange(parts):
    return [swap(part, "seq", k) for k, part in enumerate(parts, 1)][::-1]


def swap_totals(total, n):
    size, step, got = lax.axis_size("seq"), n, []
    while step < size:
        got.append(swap(bf(total), "seq", step))
        total = total.astype(jnp.float32) + got[-1].astype(jnp.float32)
        step *= 2
    return got


def sum_of_side(refs, n, earlier):
    group = lax.div(lax.axis_index("seq"), n)
    total = jnp.zeros(refs[0].shape, jnp.float32)
    for at, ref in enumerate(refs):
        from_earlier = lax.rem(lax.shift_right_logical(group, at), 2) == 1
        keep = from_earlier if earlier else jnp.logical_not(from_earlier)
        total = total + jnp.where(keep, ref[...].astype(jnp.float32), 0.0)
    return bf(total)


def lane(index, width):
    return pl.ds(pl.multiple_of(index * width, 128), width)


def pack_kernel(n, q_ref, k_ref, v_ref, *rest):
    outs, sems = rest[:-1], rest[-1]
    r = member(n)
    dim = outs[0].shape[2]
    copies = [
        pltpu.make_async_copy(ref.at[:, lane(r ^ k, dim)], out.at[at], sems.at[k - 1, at])
        for k, out in enumerate(outs, 1)
        for at, ref in enumerate((q_ref, k_ref, v_ref)[-out.shape[0] :])
    ]
    for copy in copies:
        copy.start()
    for copy in copies:
        copy.wait()


def mark_kernel(_, out_ref):
    out_ref[...] = jnp.zeros(out_ref.shape, out_ref.dtype)


def early_blocks_kernel(offsets, *refs):
    blocks, w_ref, total_ref = refs[: len(offsets)], refs[-3], refs[-1]
    h = lax.axis_index("head")
    width = blocks[0].shape[1]
    total = None
    for offset, ref in zip(offsets, blocks):
        part = mm(ref[...], w_ref[:, lane(h ^ offset, width)], NT)
        total = part if total is None else total + part
    total_ref[...] = total


def grad_mixed_kernel(n, offset, q_ref, total_ref, block_ref, w_ref, *refs):
    outs, scr = refs[:-1], refs[-1]
    r, h = member(n), lax.axis_index("head")
    width = block_ref.shape[1]
    dim = outs[0].shape[2]
    scr[...] = bf(total_ref[...] + mm(block_ref[...], w_ref[:, lane(h ^ offset, width)], NT))
    for k in range(n):
        outs[k][0] = scr[:, lane(r ^ k, dim)]
        if k > 1:
            outs[k][1] = q_ref[:, lane(r ^ k, dim)]


def first_kernel(n, *refs):
    got, own, om_ref = refs[: n - 1][::-1], refs[n - 1 : n + 1], refs[n + 1]
    kv_ref, kf_ref, total_ref = refs[n + 3 :]
    r = member(n)
    rows, dim = own[0].shape[0], om_ref.shape[1]
    scale = dim ** (-0.25)
    for k in range(n):
        at = pl.ds(pl.multiple_of((r ^ k) * rows, 128), rows)
        if k:
            kv_ref[:, at, :] = got[k - 1][-2:]
        else:
            for i, ref in enumerate(own):
                kv_ref[i, at, :] = ref[:, lane(r, dim)]
    k_all = kv_ref[0]
    wide = k_all.astype(jnp.float32)
    half_sq = jnp.sum(wide * wide, axis=1, keepdims=True) * (scale * scale * 0.5)
    kf = bf(jnp.exp(mm(k_all, om_ref[r]) * scale - half_sq))
    kf_ref[...] = kf
    total_ref[...] = bf(mm(kv_ref[1], kf, TN))


def inner_kernel(n, *refs):
    parts, (own_ref, first_ref, kv_ref, om_ref, kf_ref) = refs[: n - 1][::-1], refs[n - 1 : n + 4]
    gm_ref, qf_ref, scores_ref, num_ref, q_scr = refs[n + 4 :]
    long, dim = num_ref.shape
    rows = long // n
    r = member(n)
    places = [pl.ds(pl.multiple_of((r ^ k) * rows, 128), rows) for k in range(n)]
    gm_ref[places[0], :] = parts[0][0]
    q_scr[places[0], :] = own_ref[:, lane(r, dim)]
    gm_ref[places[1], :] = jnp.zeros((rows, dim), gm_ref.dtype)
    q_scr[places[1], :] = first_ref[0]
    for k in range(2, n):
        gm_ref[places[k], :] = parts[k - 1][0]
        q_scr[places[k], :] = parts[k - 1][1]
    scale = dim ** (-0.25)
    spans = tiles(long, rows)
    qf = bf(jnp.exp(mm(q_scr[...], om_ref[r]) * scale))
    qf_ref[...] = qf
    scores = lower(qf, kf_ref[...], spans)
    for (i, j), tile in scores.items():
        scores_ref[slice(*spans[i]), slice(*spans[j])] = tile
    for (a, b), part in zip(spans, times(lambda i, j: scores[i, j], kv_ref[1], spans)):
        num_ref[a:b, :] = part


def turn_kernel(n, *refs):
    gm_ref, late_ref, qf_ref, num_ref, *earlier = refs[: -n - 4]
    carried_ref, gn_ref, total_ref = refs[-n - 4 : -n - 1]
    outs, scr = refs[-n - 1 : -1], refs[-1]
    r = member(n)
    rows = outs[0].shape[0]
    places = [
        pl.ds(pl.multiple_of((r ^ k) * rows, 128), rows) for k in range(n)
    ]
    scr[...] = gm_ref[...]
    scr[places[1], :] = late_ref[0]
    carried = sum_of_side(earlier, n, True)
    carried_ref[...] = carried
    num = num_ref[...] + mm(qf_ref[...], carried, NT)
    inv = lax.rsqrt(jnp.mean(num * num, axis=1, keepdims=True) + EPSILON)
    normed = num * inv
    gm = scr[...].astype(jnp.float32)
    gn = bf((gm - normed * jnp.mean(gm * normed, axis=1, keepdims=True)) * inv)
    gn_ref[...] = gn
    scr[...] = bf(normed)
    for k in range(n):
        outs[k][...] = scr[places[k], :]
    total_ref[...] = bf(mm(gn, qf_ref[...], TN))


def back_kernel(rows, kv_ref, om_ref, kf_ref, qf_ref, scores_ref, gn_ref, carried_ref,
                gq_ref, gv_ref, gkf_ref):
    long, dim = gn_ref.shape
    r = member(long // rows)
    scale = dim ** (-0.25)
    spans = tiles(long, rows)
    gn, qf = gn_ref[...], qf_ref[...]
    gs = lower(gn, kv_ref[1], spans)
    cross = mm(gn, carried_ref[...])
    for (a, b), part in zip(spans, times(lambda i, j: gs[i, j], kf_ref[...], spans)):
        terms = bf((cross[a:b] + part) * qf[a:b].astype(jnp.float32))
        gq_ref[a:b, :] = bf(mm(terms, om_ref[r], NT) * scale)
    for (a, b), part in zip(spans, transposed_times(lambda i, j: gs[i, j], qf, spans)):
        gkf_ref[a:b, :] = part

    def scores_at(i, j):
        return scores_ref[slice(*spans[i]), slice(*spans[j])]

    for (a, b), part in zip(spans, transposed_times(scores_at, gn, spans)):
        gv_ref[a:b, :] = part


def end_kernel(n, kv_ref, om_ref, kf_ref, gq_ref, gv_ref, gkf_ref, *rest):
    later, outs, (gk_scr, gv_scr) = rest[: -n - 2], rest[-n - 2 : -2], rest[-2:]
    r, dim = member(n), om_ref.shape[1]
    rows = outs[0].shape[1]
    scale = dim ** (-0.25)
    kf, after = kf_ref[...], sum_of_side(later, n, False)
    gv_scr[...] = bf(gv_ref[...] + mm(kf, after, NT))
    gkf = gkf_ref[...] + mm(kv_ref[1], after)
    terms = bf(gkf * kf.astype(jnp.float32))
    total = jnp.sum(terms.astype(jnp.float32), axis=1, keepdims=True)
    wide = kv_ref[0].astype(jnp.float32)
    gk_scr[...] = bf(mm(terms, om_ref[r], NT) * scale - total * wide * (scale * scale))
    for k in range(n):
        at = pl.ds(pl.multiple_of((r ^ k) * rows, 128), rows)
        outs[k][0] = gq_ref[at, :]
        outs[k][1] = gk_scr[at, :]
        outs[k][2] = gv_scr[at, :]


def far_project_kernel(n, offset, *refs):
    mixed_in, (w_ref, _, mixed_ref, out_ref) = refs[:n][::-1], refs[n:]
    r, h = member(n), lax.axis_index("head")
    width = out_ref.shape[1]
    dim = mixed_in[0].shape[1]
    for k in range(n):
        mixed_ref[:, lane(r ^ k, dim)] = mixed_in[k][...]
    out_ref[...] = bf(mm(mixed_ref[...], w_ref[:, lane(h ^ offset, width)]))


def project_kernel(mixed_ref, w_ref, *outs):
    h = lax.axis_index("head")
    width = outs[0].shape[1]
    mixed = mixed_ref[...]
    for offset, out in enumerate(outs):
        out[...] = bf(mm(mixed, w_ref[:, lane(h ^ offset, width)]))


def unpack_kernel(ks, n, *refs):
    got, (*outs, sems) = refs[: len(ks)], refs[len(ks) :]
    r = member(n)
    dim = got[0].shape[2]
    copies = [
        pltpu.make_async_copy(ref.at[at], out.at[:, lane(r ^ k, dim)], sems.at[i, at])
        for i, (k, ref) in enumerate(zip(ks, got))
        for at, out in enumerate(outs)
    ]
    for copy in copies:
        copy.start()
    for copy in copies:
        copy.wait()


def last_kernel(n, got_ref, *refs):
    parts, (out_ref, *outs), (scr, sems) = refs[:-9], refs[-6:-2], refs[-2:]
    r = member(n)
    dim = got_ref.shape[2]
    copies = [
        pltpu.make_async_copy(got_ref.at[at], out.at[:, lane(r ^ 1, dim)], sems.at[at])
        for at, out in enumerate(outs)
    ]
    for copy in copies:
        copy.start()
    scr[...] = bf(sum(ref[...].astype(jnp.float32) for ref in parts))
    copies.append(pltpu.make_async_copy(scr, out_ref, sems.at[3]))
    copies[-1].start()
    for copy in copies:
        copy.wait()


def local(queries, key_vectors, value_vectors, feature_proj, out_weight, grad_output):
    n, dim, feats = feature_proj.shape
    rows, width = grad_output.shape
    split = lax.axis_size("head")
    bits = bits_of(split)
    long = n * rows
    macs = long * dim * feats * 2
    f32 = jnp.float32

    offsets, blocks = [0], [grad_output]
    for bit in reversed(bits):
        blocks = blocks + [swap(b, "head", bit) for b in blocks]
        offsets = offsets + [o ^ bit for o in offsets]
    sends = call(
        functools.partial(pack_kernel, n),
        [struct((3 if k == 1 else 2, rows, dim)) for k in range(1, n)],
        queries, key_vectors, value_vectors,
        specs=[ANY] * 3, scratch=[pltpu.SemaphoreType.DMA((n - 1, 3))], vmem=53.68,
    )
    got = exchange(sends)
    (mark,) = call(mark_kernel, [struct((8, 128), f32)], blocks[offsets.index(1)], specs=[ANY], flops=10**10)
    (gm_early,) = call(
        functools.partial(early_blocks_kernel, offsets[:-1]),
        [struct((rows, n * dim), f32)],
        *blocks[:-1], out_weight, mark, flops=2 * rows * out_weight.size,
        specs=[VMEM] * split + [ANY],
    )
    gm_parts = call(
        functools.partial(grad_mixed_kernel, n, offsets[-1]),
        [struct((1 if k < 2 else 2, rows, dim)) for k in range(n)],
        queries, gm_early, blocks[-1], out_weight, flops=2 * rows * out_weight.size,
        scratch=[pltpu.VMEM((rows, n * dim), jnp.bfloat16)],
    )
    gm_in = exchange(gm_parts[1:]) + [gm_parts[0]]
    kv, kf, total = call(
        functools.partial(first_kernel, n),
        [
            struct((2, long, dim)),
            struct((long, feats)),
            struct((dim, feats)),
        ],
        *got, key_vectors, value_vectors, feature_proj, gm_parts[0],
        flops=2 * macs, specs=[VMEM] * (n + 2) + [ANY],
    )
    earlier = swap_totals(total, n)
    gm, qf, scores, num = call(
        functools.partial(inner_kernel, n),
        [struct((long, dim)), struct((long, feats)), struct((long, long)), struct((long, dim), f32)],
        *gm_in[:-2], gm_in[-1], queries, got[-1], kv, feature_proj, kf, flops=16 * macs,
        scratch=[pltpu.VMEM((long, dim), jnp.bfloat16)],
    )
    carried, gn, later_total, *mixed_parts = call(
        functools.partial(turn_kernel, n),
        [
            struct((dim, feats)),
            struct((long, dim)),
            struct((dim, feats)),
        ]
        + [struct((rows, dim))] * n,
        gm, gm_in[-2], qf, num, *earlier, flops=2 * macs,
        scratch=[pltpu.VMEM((long, dim), jnp.bfloat16)],
    )
    after = swap_totals(later_total, n)
    mixed_in = exchange(mixed_parts[1:]) + [mixed_parts[0]]
    gq, gv_part, gkf_part = call(
        functools.partial(back_kernel, rows),
        [struct((long, dim)), struct((long, dim), f32), struct((long, feats), f32)],
        kv, feature_proj, kf, qf, scores, gn, carried, flops=8 * macs,
    )
    grads = call(
        functools.partial(end_kernel, n),
        [struct((3, rows, dim))] * n,
        kv, feature_proj, kf, gq, gv_part, gkf_part, *after, flops=3 * macs,
        scratch=[pltpu.VMEM((long, dim), jnp.bfloat16)] * 2,
    )
    grads_in = exchange(grads[1:]) + [grads[0]]

    mixed, far = call(
        functools.partial(far_project_kernel, n, split - 1),
        [struct((rows, n * dim)), struct((rows, width))],
        *mixed_in, out_weight, grads[0], flops=2 * rows * out_weight.size // split,
        specs=[VMEM] * (n + 1) + [ANY],
    )
    parts = call(
        project_kernel, [struct((rows, width))] * (split - 1), mixed, out_weight,
        flops=10 * 10**8,
    )
    parts = list(parts) + [far]
    kept = reduce_blocks(parts, bits)
    *early, late, own_grads = grads_in
    ks = [k for k in range(n - 1, 1, -1)] + [0]
    arrays = [struct((rows, n * dim))] * 3
    partial_grads = call(
        functools.partial(unpack_kernel, ks, n), arrays,
        *early, own_grads, flops=8 * 10**8,
        out_specs=[ANY] * 3, scratch=[pltpu.SemaphoreType.DMA((n - 1, 3))],
    )
    return call(
        functools.partial(last_kernel, n),
        [struct((rows, width))] + arrays,
        late, *kept, *partial_grads,
        specs=[VMEM] * (1 + len(kept)) + [ANY] * 3, out_specs=[ANY] * 4,
        aliases={1 + len(kept) + i: 1 + i for i in range(3)},
        scratch=[pltpu.VMEM((rows, width), jnp.bfloat16), pltpu.SemaphoreType.DMA((4,))],
    )


def solution(mesh):
    placed = (
        P("seq", "head"),
        P("seq", "head"),
        P("seq", "head"),
        P("head", None, None),
        P("head", None),
        P("seq", "head"),
    )
    return jax.shard_map(
        local,
        mesh=mesh,
        in_specs=placed,
        out_specs=(P("seq", "head"),) * 4,
        check_vma=False,
    )
```
